512 devices in a mesh: band: 8 (over y_lo, core), dom: 64 (over x, y_hi, z).
Axes of the slice: x: 4, y: 8 (y_hi: 2, y_lo: 4; y = y_hi * 4 + y_lo), z: 8, core: 2. Of those that a mesh axis runs over, the one named last changes fastest.
Arguments:
- states_in: float32 [512, 65536], P('band', 'dom'), may hold values from -6 to 6
- stiffness: float32 [343, 343], replicated, may hold values from -2 to 2, as said below
- cell_scale: float32 [384], P('dom'), may hold values from 0.5 to 2
- potential: float32 [65536], P('dom'), may hold values from 0 to 2
- inv_mass_sqrt: float32 [65536], P('dom'), may hold values from 0.25 to 1.75
- cell_nodes: int32 [384, 343], P('dom'), may hold values from 0 to 1151, as said below
- shared_nodes: int32 [8192], P('dom'), may hold values from 0 to 1023, as said below
Outputs:
- filtered: float32 [512, 65536], P('band', 'dom')
- margin: float32 [512, 512], P('band')
The draws below stay inside these ranges and needn't reach their ends.
Inputs may be any that keep to these rules, and one draw needn't show every extreme that they name: `stiffness`: symmetric. `cell_nodes`: in the cells of a subdomain, an entry below 1024 is one of its own nodes and an entry l of 1024 or more stands for entry l - 1024 of the next subdomain's (cyclically) shared_nodes list; every value from 0 to 1151 occurs in the subdomain's cells. `shared_nodes`: the 128 entries of each subdomain are distinct.
All inputs are finite; a program needn't handle non-finite values.
Results may differ from the reference program's by a relative error of at most 0.0001.
Values sent between devices are 32-bit elements; how exact they have to be, the bound alone decides.
No kernel may reach another device: no remote copies, remote signals or barrier semaphores. Data moves between devices by JAX's collectives and lax.ppermute only.
A program may use at most 64 MiB of HBM per device.

```python
import math
import jax
import jax.numpy as jnp
from jax import lax

NPC = 343
BLOCK = 64
DEGREE = 3
NODES_DEV = 1024
SHARED = 128
CELLS_DEV = 6
STATES = 512
NODES = 65536
CELLS = 384
N_BAND = 8
N_DOM = 64


def draw_stiffness(key, part):
    entries = jnp.clip(jax.random.normal(key, (NPC, NPC), jnp.float32), -4.0, 4.0)
    entries = entries / jnp.sqrt(jnp.float32(NPC))
    return (entries + entries.T) / jnp.sqrt(jnp.float32(2.0))


def draw_cell_nodes(key, part):
    local_count = NODES_DEV + SHARED
    slot_count = CELLS_DEV * NPC

    def one_domain(sub_key):
        key_first, key_second, key_third = jax.random.split(sub_key, 3)
        covering = jax.random.permutation(key_first, local_count).astype(jnp.int32)
        further = jax.random.randint(key_second, (slot_count - local_count,), 0, local_count, dtype=jnp.int32)
        joined = jnp.concatenate([covering, further])
        return jax.random.permutation(key_third, joined).reshape(CELLS_DEV, NPC)
    key_list = jax.random.split(jax.random.fold_in(key, 11), N_DOM)
    return jax.vmap(one_domain)(key_list).reshape(CELLS_DEV * N_DOM, NPC).astype(jnp.int32)


def draw_shared_nodes(key, part):

    def one_domain(sub_key):
        return jax.random.permutation(sub_key, NODES_DEV)[:SHARED].astype(jnp.int32)
    key_list = jax.random.split(jax.random.fold_in(key, 23), N_DOM)
    return jax.vmap(one_domain)(key_list).reshape(SHARED * N_DOM).astype(jnp.int32)


def levels(stream_key, extent, cuts, smallest, top_value):
    factor_of = 1.0
    for axis_at, parts in cuts:
        heights = jax.random.uniform(jax.random.fold_in(jax.random.fold_in(stream_key, 6), axis_at), (parts,), jnp.float32, smallest / len(cuts), top_value / len(cuts))
        factor_of = factor_of * jnp.repeat(jnp.exp(heights), extent[axis_at] // parts).reshape((-1,) + (1,) * (len(extent) - 1 - axis_at))
    return factor_of


def gaussian(own_key, extent, width, most, shards=(), held_as=jnp.bfloat16):
    gain = levels(own_key, extent, shards, -0.22, 0.18) if shards else 1.0
    values = jax.random.normal(own_key, extent, jnp.float32) * width * gain
    return jnp.minimum(jnp.maximum(values, -most), most).astype(held_as)


def setup_inputs(seed: int = 0) -> dict:
    arg_keys = jax.random.split(jax.random.key(seed), 8)
    states_in = gaussian(arg_keys[0], (STATES, NODES), 1.0, 6.0, ((0, 8), (1, 64)), jnp.float32)
    stiffness = draw_stiffness(jax.random.fold_in(arg_keys[7], 71), 0)
    cell_scale = jnp.clip(jnp.exp(math.log(2.0) - 1.3862944 * jax.random.uniform(arg_keys[2], (CELLS,), jnp.float32) ** levels(arg_keys[2], (CELLS,), ((0, 64),), -0.2, 0.2)), 0.5, 2.0)
    potential = jnp.clip(2.0 * jax.random.uniform(arg_keys[3], (NODES,), jnp.float32) ** levels(arg_keys[3], (NODES,), ((0, 64),), -0.2, 0.2), 0.0, 2.0)
    inv_mass_sqrt = jnp.clip(1.0 + 0.15 * jax.random.normal(arg_keys[4], (NODES,), jnp.float32), 0.25, 1.75)
    cell_nodes = draw_cell_nodes(jax.random.fold_in(arg_keys[7], 71), 0)
    shared_nodes = draw_shared_nodes(jax.random.fold_in(arg_keys[7], 71), 0)
    return dict(states_in=states_in, stiffness=stiffness, cell_scale=cell_scale, potential=potential, inv_mass_sqrt=inv_mass_sqrt, cell_nodes=cell_nodes, shared_nodes=shared_nodes)


center_shift = 1.0
half_width = 4.0

def global_nodes(cell_nodes, shared_nodes):
    count = cell_nodes.shape[0]
    holder = (jnp.arange(count, dtype=jnp.int32) // CELLS_DEV)[:, None]
    follower = (holder + 1) % N_DOM
    offset = jnp.clip(cell_nodes - NODES_DEV, 0, SHARED - 1)
    remote = shared_nodes[(follower * SHARED + offset).astype(jnp.int32)]
    inside = holder * NODES_DEV + cell_nodes
    outside = follower * NODES_DEV + remote
    return jnp.where(cell_nodes < NODES_DEV, inside, outside).astype(jnp.int32)

def operate(vector, stiffness, cell_scale, potential, inv_mass_sqrt, indices):
    scaled = vector * inv_mass_sqrt[None, :]
    cellwise = scaled[:, indices]
    product = jnp.einsum('bcj,kj->bck', cellwise, stiffness, precision=lax.Precision.HIGHEST, preferred_element_type=jnp.float32)
    product = product * cell_scale[None, :, None]
    summed = jnp.zeros_like(vector).at[:, indices].add(product)
    return inv_mass_sqrt[None, :] * summed + potential[None, :] * vector

def reference(states_in, stiffness, cell_scale, potential, inv_mass_sqrt, cell_nodes, shared_nodes):
    indices = global_nodes(cell_nodes, shared_nodes)

    def apply_once(vector):
        return operate(vector, stiffness, cell_scale, potential, inv_mass_sqrt, indices)

    def filter_block(block_states):
        previous = block_states
        current = (apply_once(block_states) - center_shift * block_states) / half_width
        for degree_step in range(DEGREE - 1):
            following = 2.0 * (apply_once(current) - center_shift * current) / half_width - previous
            previous = current
            current = following
        return current
    blocks = states_in.reshape(N_BAND, BLOCK, states_in.shape[1])
    filtered = lax.map(filter_block, blocks).reshape(STATES, states_in.shape[1])
    margin = jnp.dot(filtered, filtered.T, precision=lax.Precision.HIGHEST, preferred_element_type=jnp.float32)
    margin = margin / (NODES_DEV * N_DOM)
    return (filtered, margin)
```

```python
import functools

import jax
import jax.numpy as jnp
from jax import lax
from jax.experimental import pallas as pl
from jax.experimental.pallas import tpu as pltpu
from jax.sharding import PartitionSpec as P

DEGREE = 3
CENTER = 1.0
HALF_WIDTH = 4.0
LIMIT = 48 * 1024 * 1024

f32 = jnp.float32
bf16 = jnp.bfloat16


def rounded_up(count, to):
    return -(-count // to) * to


def parts(x, count):
    out = []
    for i in range(count):
        piece = x.astype(bf16)
        out.append(piece)
        if i + 1 < count:
            x = x - piece.astype(f32)
    return out


def dot(a, b):
    return jnp.dot(a, b, preferred_element_type=f32)


def dot_t(a, b):
    return lax.dot_general(a, b, (((1,), (1,)), ((), ())), preferred_element_type=f32)


def one_hot(row, count):
    at = lax.broadcasted_iota(jnp.int32, (count, row.shape[1]), 0)
    return jnp.where(at == row, 1.0, 0.0).astype(bf16)


def picked(x, chosen):
    rows = x.shape[0]
    got = dot(jnp.concatenate(parts(x, 3), axis=0), chosen)
    return got[:rows] + got[rows : 2 * rows] + got[2 * rows :]


def placed(x, chosen):
    rows = x.shape[0]
    got = dot_t(jnp.concatenate(parts(x, 3), axis=0), chosen)
    return got[:rows] + got[rows : 2 * rows] + got[2 * rows :]


def start_kernel(states, inv_mass, shared, message):
    rows, owned = states.shape
    chosen = one_hot(shared[...], owned)
    both = jnp.concatenate(
        [states[...], jnp.broadcast_to(inv_mass[...], (8, owned))], axis=0
    )
    message[...] = picked(both, chosen)


def apply_cells(own, ghost, cells, stiff, scale, chosen_all, cells_pad, stiff_pad):
    rows = own.shape[0]
    n_cells, npc = cells.shape
    pad = stiff_pad.shape[0]
    nodes = chosen_all.shape[0]
    cells_pad[...] = jnp.full(cells_pad.shape, -1, jnp.int32)
    cells_pad[:n_cells, :npc] = cells[...]
    stiff_pad[...] = jnp.zeros(stiff_pad.shape, f32)
    stiff_pad[:npc, :npc] = stiff[...]
    for c in range(n_cells):
        chosen_all[:, c * pad : (c + 1) * pad] = one_hot(cells_pad[c : c + 1, :], nodes)
    values = jnp.concatenate([own, ghost], axis=1)
    gathered = dot(jnp.concatenate(parts(values, 2), axis=0), chosen_all[...])
    gathered = gathered.astype(bf16)
    high, low = parts(stiff_pad[...], 2)
    stacked = jnp.concatenate(
        [gathered[:rows, c * pad : (c + 1) * pad] for c in range(n_cells)]
        + [gathered[rows:, c * pad : (c + 1) * pad] for c in range(n_cells)],
        axis=0,
    )
    half = n_cells * rows
    by_high = dot(stacked, high)
    product = by_high[:half] + by_high[half:] + dot(stacked[:half], low)
    product = jnp.concatenate(
        [product[c * rows : (c + 1) * rows] * scale[c] for c in range(n_cells)], axis=1
    )
    summed = dot_t(jnp.concatenate(parts(product, 2), axis=0), chosen_all[...])
    summed = summed[:rows] + summed[rows:]
    return summed[:, : own.shape[1]], summed[:, own.shape[1] :]


def first_kernel(
    states, fetched, inv_mass, potential, cells, stiff, scale, shared,
    partial, down, up, chosen_all, cells_pad, stiff_pad,
):
    rows, owned = states.shape
    current = states[...]
    ghost_inv = fetched[rows : rows + 1, :]
    ghost = fetched[:rows, :]
    own_sum, ghost_sum = apply_cells(
        current * inv_mass[...], ghost * ghost_inv, cells, stiff, scale,
        chosen_all, cells_pad, stiff_pad,
    )
    up[...] = ghost_inv * ghost_sum * (1.0 / HALF_WIDTH)
    here = (inv_mass[...] * own_sum + (potential[...] - CENTER) * current) * (1.0 / HALF_WIDTH)
    partial[...] = here
    down[...] = picked(here, one_hot(shared[...], owned))


def next_kernel(
    last, previous, part, fetched, sent_up, got_down, got_up, inv_mass, potential,
    cells, stiff, scale, shared, *rest,
):
    if last:
        partial, up, chosen_all, cells_pad, stiff_pad = rest
    else:
        current_out, partial, down, up, chosen_all, cells_pad, stiff_pad = rest
    rows, owned = previous.shape
    chosen = one_hot(shared[...], owned)
    current = part[...] + placed(got_up[...], chosen)
    ghost_inv = fetched[rows : rows + 1, :]
    ghost = got_down[...] + sent_up[...]
    own_sum, ghost_sum = apply_cells(
        current * inv_mass[...], ghost * ghost_inv, cells, stiff, scale,
        chosen_all, cells_pad, stiff_pad,
    )
    up[...] = ghost_inv * ghost_sum * (2.0 / HALF_WIDTH)
    here = (inv_mass[...] * own_sum + (potential[...] - CENTER) * current) * (
        2.0 / HALF_WIDTH
    ) - previous[...]
    partial[...] = here
    if not last:
        current_out[...] = current
        down[...] = picked(here, chosen)


def finish_kernel(part, got_up, shared, filtered, at_shared):
    owned = part.shape[1]
    chosen = one_hot(shared[...], owned)
    here = part[...] + placed(got_up[...], chosen)
    filtered[...] = here
    at_shared[...] = picked(here, chosen)


def gram_kernel(total_nodes, filtered, at_shared, gathered, late, out):
    rows = filtered.shape[0]

    def against(a, b):
        a_high, a_low = parts(a, 2)
        b_high, b_low = parts(b, 2)
        by_high = dot_t(jnp.concatenate([a_high, a_low], axis=0), b_high)
        return by_high[:rows] + by_high[rows:] + dot_t(a_high, b_low)

    whole = against(filtered[...], gathered[...]) + against(at_shared[...], late[...])
    out[...] = whole * (1.0 / total_nodes)


def per_device(
    states_in, stiffness, cell_scale, potential, inv_mass_sqrt, cell_nodes, shared_nodes
):
    rows, owned = states_in.shape
    shared_count = shared_nodes.shape[0]
    n_cells, npc = cell_nodes.shape
    nodes = owned + shared_count
    pad = rounded_up(npc, 128)
    n_dom = lax.axis_size("dom")
    n_band = lax.axis_size("band")
    backward = [(i, (i - 1) % n_dom) for i in range(n_dom)]
    forward = [(i, (i + 1) % n_dom) for i in range(n_dom)]

    in_vmem = pl.BlockSpec(memory_space=pltpu.VMEM)
    in_smem = pl.BlockSpec(memory_space=pltpu.SMEM)
    params = pltpu.CompilerParams(vmem_limit_bytes=LIMIT)
    inv_mass = inv_mass_sqrt.reshape(1, owned)
    pot = potential.reshape(1, owned)
    shared = shared_nodes.reshape(1, shared_count)
    block = jax.ShapeDtypeStruct((rows, owned), f32)
    edge = jax.ShapeDtypeStruct((rows, shared_count), f32)
    scratch = [
        pltpu.VMEM((nodes, n_cells * pad), bf16),
        pltpu.VMEM((8, pad), jnp.int32),
        pltpu.VMEM((pad, pad), f32),
    ]

    def call(kernel, out_shape, specs, scratch_shapes=()):
        return pl.pallas_call(
            kernel,
            out_shape=out_shape,
            in_specs=specs,
            out_specs=jax.tree.map(lambda _: in_vmem, out_shape),
            scratch_shapes=scratch_shapes,
            compiler_params=params,
        )

    message = call(
        start_kernel, jax.ShapeDtypeStruct((rows + 8, shared_count), f32), [in_vmem] * 3
    )(states_in, inv_mass, shared)
    fetched = lax.ppermute(message, "dom", backward)
    fixed = (inv_mass, pot, cell_nodes, stiffness, cell_scale, shared)
    fixed_specs = [in_vmem] * 4 + [in_smem, in_vmem]
    partial, down, up = call(
        first_kernel, (block, edge, edge), [in_vmem] * 2 + fixed_specs, scratch
    )(states_in, fetched, *fixed)
    previous = states_in
    for step in range(DEGREE - 1):
        last = step == DEGREE - 2
        got_up = lax.ppermute(up, "dom", forward)
        got_down = lax.ppermute(down, "dom", backward)
        outs = (block, edge) if last else (block, block, edge, edge)
        results = call(
            functools.partial(next_kernel, last), outs, [in_vmem] * 6 + fixed_specs, scratch
        )(previous, partial, fetched, up, got_down, got_up, *fixed)
        if last:
            partial, up = results
        else:
            previous, partial, down, up = results
    gathered = lax.all_gather(partial, "band", axis=0, tiled=True)
    got_up = lax.ppermute(up, "dom", forward)
    filtered, at_shared = call(finish_kernel, (block, edge), [in_vmem] * 3)(
        partial, got_up, shared
    )
    late = lax.all_to_all(
        jnp.broadcast_to(got_up[None], (n_band, rows, shared_count)),
        "band", split_axis=0, concat_axis=0, tiled=True,
    ).reshape(n_band * rows, shared_count)
    gram = call(
        functools.partial(gram_kernel, owned * n_dom),
        jax.ShapeDtypeStruct((rows, n_band * rows), f32),
        [in_vmem] * 4,
    )(filtered, at_shared, gathered, late)
    pieces = lax.all_to_all(gram, "dom", split_axis=0, concat_axis=0, tiled=True)
    pieces = pieces.reshape(n_dom, rows // n_dom, n_band * rows)
    own_rows = jnp.broadcast_to(jnp.sum(pieces, axis=0)[None], pieces.shape)
    margin = lax.all_to_all(
        own_rows.reshape(rows, n_band * rows), "dom", split_axis=0, concat_axis=0, tiled=True
    )
    return filtered, margin


def solution(mesh):
    return jax.shard_map(
        per_device,
        mesh=mesh,
        in_specs=(P("band", "dom"), P(), P("dom"), P("dom"), P("dom"), P("dom", None), P("dom")),
        out_specs=(P("band", "dom"), P("band", None)),
        check_vma=False,
    )
```

```python
import functools

import jax
import jax.numpy as jnp
from jax import lax
from jax.experimental import pallas as pl
from jax.experimental.pallas import tpu as pltpu
from jax.sharding import Mesh, PartitionSpec as P

DEGREE = 3
CENTER = 1.0
HALF_WIDTH = 4.0
LIMIT = 28 * 1024 * 1024
BAND = ("chip", "core")
DOM = ("x", "half", "z")

f32 = jnp.float32
bf16 = jnp.bfloat16


def rounded_up(count, to):
    return -(-count // to) * to


def parts(x, count):
    out = []
    for i in range(count):
        piece = x.astype(bf16)
        out.append(piece)
        if i + 1 < count:
            x = x - piece.astype(f32)
    return out


def dot(a, b):
    return jnp.dot(a, b, preferred_element_type=f32)


def dot_t(a, b):
    return lax.dot_general(a, b, (((1,), (1,)), ((), ())), preferred_element_type=f32)


def one_hot(row, count):
    at = lax.broadcasted_iota(jnp.int32, (count, row.shape[1]), 0)
    return jnp.where(at == row, 1.0, 0.0).astype(bf16)


def picked(x, chosen):
    rows = x.shape[0]
    got = dot(jnp.concatenate(parts(x, 3), axis=0), chosen)
    return got[:rows] + got[rows : 2 * rows] + got[2 * rows :]


def placed(x, chosen):
    rows = x.shape[0]
    got = dot_t(jnp.concatenate(parts(x, 3), axis=0), chosen)
    return got[:rows] + got[rows : 2 * rows] + got[2 * rows :]


def start_kernel(states, inv_mass, shared, message):
    rows, owned = states.shape
    chosen = one_hot(shared[...], owned)
    both = jnp.concatenate(
        [states[...], jnp.broadcast_to(inv_mass[...], (8, owned))], axis=0
    )
    message[...] = picked(both, chosen)


def prepare_kernel(cells, stiff, shared, chosen_all, high, low, chosen, cells_pad, stiff_pad):
    n_cells, npc = cells.shape
    pad = stiff_pad.shape[0]
    nodes = chosen_all.shape[0]
    cells_pad[...] = jnp.full(cells_pad.shape, -1, jnp.int32)
    cells_pad[:n_cells, :npc] = cells[...]
    stiff_pad[...] = jnp.zeros(stiff_pad.shape, f32)
    stiff_pad[:npc, :npc] = stiff[...]
    for c in range(n_cells):
        chosen_all[:, c * pad : (c + 1) * pad] = one_hot(cells_pad[c : c + 1, :], nodes)
    high[...], low[...] = parts(stiff_pad[...], 2)
    chosen[...] = one_hot(shared[...], chosen.shape[0])


def apply_cells(own, ghost, scale, chosen_all, high, low):
    rows, owned = own.shape
    pad = high.shape[0]
    n_cells = chosen_all.shape[1] // pad
    values = jnp.concatenate([own, ghost], axis=1)
    gathered = dot(jnp.concatenate(parts(values, 2), axis=0), chosen_all[...])
    gathered = gathered.astype(bf16)
    stacked = jnp.concatenate(
        [gathered[:rows, c * pad : (c + 1) * pad] for c in range(n_cells)]
        + [gathered[rows:, c * pad : (c + 1) * pad] for c in range(n_cells)],
        axis=0,
    )
    half = n_cells * rows
    by_high = dot(stacked, high[...])
    product = by_high[:half] + by_high[half:] + dot(stacked[:half], low[...])
    product = jnp.concatenate(
        [product[c * rows : (c + 1) * rows] * scale[c] for c in range(n_cells)], axis=1
    )
    summed = dot_t(jnp.concatenate(parts(product, 2), axis=0), chosen_all[...])
    summed = summed[:rows] + summed[rows:]
    return summed[:, :owned], summed[:, owned:]


def is_even():
    return lax.axis_index("z") % 2 == 0


def send_both(up, down, near, far):
    even = is_even()
    near[...] = jnp.where(even, up, down)
    far[...] = jnp.zeros(far.shape, f32)
    far[: down.shape[0], :] = jnp.where(even, down, up)


def first_kernel(
    states, fetched, inv_mass, potential, scale, chosen_all, high, low, chosen,
    far, near, partial,
):
    rows, owned = states.shape
    current = states[...]
    ghost_inv = fetched[rows : rows + 1, :]
    ghost = fetched[:rows, :]
    own_sum, ghost_sum = apply_cells(
        current * inv_mass[...], ghost * ghost_inv, scale, chosen_all, high, low
    )
    up = ghost_inv * ghost_sum * (1.0 / HALF_WIDTH)
    here = (inv_mass[...] * own_sum + (potential[...] - CENTER) * current) * (1.0 / HALF_WIDTH)
    partial[...] = here
    send_both(up, picked(here, chosen[...]), near, far)


def next_kernel(
    last, previous, part, fetched, sent_near, sent_far, got_near, got_far, inv_mass,
    potential, scale, chosen_all, high, low, chosen, *outs,
):
    rows, owned = previous.shape
    even = is_even()
    got_up = jnp.where(even, got_far[:rows, :], got_near[...])
    got_down = jnp.where(even, got_near[...], got_far[:rows, :])
    sent_up = jnp.where(even, sent_near[...], sent_far[:rows, :])
    current = part[...] + placed(got_up, chosen[...])
    ghost_inv = fetched[rows : rows + 1, :]
    ghost = got_down + sent_up
    own_sum, ghost_sum = apply_cells(
        current * inv_mass[...], ghost * ghost_inv, scale, chosen_all, high, low
    )
    up_now = ghost_inv * ghost_sum * (2.0 / HALF_WIDTH)
    here = (inv_mass[...] * own_sum + (potential[...] - CENTER) * current) * (
        2.0 / HALF_WIDTH
    ) - previous[...]
    if last:
        up, partial = outs
        up[...] = up_now
    else:
        far, near, partial, current_out = outs
        current_out[...] = current
        send_both(up_now, picked(here, chosen[...]), near, far)
    partial[...] = here


def finish_kernel(part, got_up, chosen, filtered):
    filtered[...] = part[...] + placed(got_up[...], chosen[...])


def gram_kernel(total_nodes, filtered, sibling, *rest):
    chips = (len(rest) - 4) // 2 + 1
    blocks, lates = rest[: chips - 1], rest[chips - 1 : 2 * chips - 2]
    chosen, out, g_high, g_low = rest[2 * chips - 2 :]
    rows, owned = filtered.shape
    chip = lax.axis_index("chip")
    core = lax.axis_index("core")

    for s in range(chips):
        base = lax.rem(chip - s + chips, chips) * (2 * rows)
        here = pl.ds(pl.multiple_of(base + core * rows, rows), rows)
        other = pl.ds(pl.multiple_of(base + (1 - core) * rows, rows), rows)
        block = filtered if s == 0 else blocks[s - 1]
        g_high[here, :owned], g_low[here, :owned] = parts(block[...], 2)
        if s == 0:
            g_high[here, owned:] = jnp.zeros((rows, g_high.shape[1] - owned), bf16)
            g_low[here, owned:] = jnp.zeros((rows, g_high.shape[1] - owned), bf16)
        else:
            g_high[here, owned:], g_low[here, owned:] = parts(lates[s - 1][...], 2)
        g_high[other, :] = jnp.zeros((rows, g_high.shape[1]), bf16)
        g_low[other, :] = jnp.zeros((rows, g_high.shape[1]), bf16)
    both = jnp.concatenate([filtered[...], sibling[...]], axis=0)
    both = jnp.concatenate([both, picked(both, chosen[...])], axis=1)
    b_high, b_low = parts(both, 2)
    by_high = dot_t(jnp.concatenate([b_high, b_low], axis=0), g_high[...])
    whole = by_high[: 2 * rows] + by_high[2 * rows :] + dot_t(b_high, g_low[...])
    whole = whole * (1.0 / total_nodes)
    out[pl.ds(pl.multiple_of(core * rows, rows), rows), :] = whole[:rows]
    out[pl.ds(pl.multiple_of((1 - core) * rows, rows), rows), :] = whole[rows:]


def per_device(
    states_in, stiffness, cell_scale, potential, inv_mass_sqrt, cell_nodes, shared_nodes
):
    rows, owned = states_in.shape
    shared_count = shared_nodes.shape[0]
    n_cells, npc = cell_nodes.shape
    nodes = owned + shared_count
    pad = rounded_up(npc, 128)
    n_dom = lax.axis_size(DOM)
    n_band = lax.axis_size(BAND)
    chips = lax.axis_size("chip")
    backward = [(i, (i - 1) % n_dom) for i in range(n_dom)]
    forward = [(i, (i + 1) % n_dom) for i in range(n_dom)]
    near_pairs = [(i, i ^ 1) for i in range(n_dom)]
    far_pairs = [(i, (((i + 1) ^ 1) - 1) % n_dom) for i in range(n_dom)]

    in_vmem = pl.BlockSpec(memory_space=pltpu.VMEM)
    in_smem = pl.BlockSpec(memory_space=pltpu.SMEM)
    params = pltpu.CompilerParams(vmem_limit_bytes=LIMIT)
    inv_mass = inv_mass_sqrt.reshape(1, owned)
    pot = potential.reshape(1, owned)
    shared = shared_nodes.reshape(1, shared_count)
    block = jax.ShapeDtypeStruct((rows, owned), f32)
    edge = jax.ShapeDtypeStruct((rows, shared_count), f32)
    tall = jax.ShapeDtypeStruct((rows + 8, shared_count), f32)

    def call(kernel, out_shape, specs, scratch_shapes=()):
        return pl.pallas_call(
            kernel,
            out_shape=out_shape,
            in_specs=specs,
            out_specs=jax.tree.map(lambda _: in_vmem, out_shape),
            scratch_shapes=scratch_shapes,
            compiler_params=params,
        )

    message = call(
        start_kernel, jax.ShapeDtypeStruct((rows + 8, shared_count), f32), [in_vmem] * 3
    )(states_in, inv_mass, shared)
    fetched = lax.ppermute(message, DOM, backward)
    prepared = call(
        prepare_kernel,
        (
            jax.ShapeDtypeStruct((nodes, n_cells * pad), bf16),
            jax.ShapeDtypeStruct((pad, pad), bf16),
            jax.ShapeDtypeStruct((pad, pad), bf16),
            jax.ShapeDtypeStruct((owned, shared_count), bf16),
        ),
        [in_vmem] * 3,
        [pltpu.VMEM((8, pad), jnp.int32), pltpu.VMEM((pad, pad), f32)],
    )(cell_nodes, stiffness, shared)
    chosen = prepared[3]
    fixed = (inv_mass, pot, cell_scale, *prepared)
    fixed_specs = [in_vmem] * 2 + [in_smem] + [in_vmem] * 4
    far, near, partial = call(
        first_kernel, (tall, edge, block), [in_vmem] * 2 + fixed_specs
    )(states_in, fetched, *fixed)
    previous = states_in
    for step in range(DEGREE - 1):
        last = step == DEGREE - 2
        got_near = lax.ppermute(near, DOM, near_pairs)
        got_far = lax.ppermute(far, DOM, far_pairs)
        outs = (edge, block) if last else (tall, edge, block, block)
        results = call(
            functools.partial(next_kernel, last), outs, [in_vmem] * 7 + fixed_specs
        )(previous, partial, fetched, near, far, got_near, got_far, *fixed)
        if last:
            up, partial = results
        else:
            far, near, partial, previous = results

    def from_chip(x, s):
        return lax.ppermute(x, "chip", [(i, (i + s) % chips) for i in range(chips)])

    got_up = lax.ppermute(up, DOM, forward)
    blocks = [from_chip(partial, s) for s in range(1, chips)]
    filtered = call(finish_kernel, block, [in_vmem] * 3)(partial, got_up, chosen)
    lates = [from_chip(got_up, s) for s in range(1, chips)]
    sibling = lax.ppermute(filtered, "core", [(0, 1), (1, 0)])
    gram = call(
        functools.partial(gram_kernel, owned * n_dom),
        jax.ShapeDtypeStruct((2 * rows, n_band * rows), f32),
        [in_vmem] * (2 + 2 * (chips - 1) + 1),
        [pltpu.VMEM((n_band * rows, nodes), bf16)] * 2,
    )(filtered, sibling, *blocks, *lates, chosen)
    columns = n_band * rows
    flat = n_dom // 2
    pieces = lax.all_to_all(
        gram.reshape(2 * flat, rows // flat, columns), ("core", "x", "z"), 0, 0, tiled=True
    )
    mine = jnp.sum(pieces, axis=0)
    spread = lax.all_to_all(
        jnp.broadcast_to(mine[None], (n_dom, rows // flat, columns)), DOM, 0, 0, tiled=True
    )
    n_x, n_half, n_z = (lax.axis_size(name) for name in DOM)
    margin = jnp.sum(spread.reshape(n_x, n_half, n_z, rows // flat, columns), axis=1)
    return filtered, margin.reshape(rows, columns)


def solution(mesh):
    fine = Mesh(mesh.devices.reshape(4, 2, 4, 2, 8), BAND + DOM)
    return jax.shard_map(
        per_device,
        mesh=fine,
        in_specs=(P(BAND, DOM), P(), P(DOM), P(DOM), P(DOM), P(DOM, None), P(DOM)),
        out_specs=(P(BAND, DOM), P(BAND, None)),
        check_vma=False,
    )
```

```python
import functools

import jax
import jax.numpy as jnp
from jax import lax
from jax.experimental import pallas as pl
from jax.experimental.pallas import tpu as pltpu
from jax.sharding import Mesh, PartitionSpec as P

DEGREE = 3
CENTER = 1.0
HALF_WIDTH = 4.0
LIMIT = 28 * 1024 * 1024
BAND = ("chip", "core")
DOM = ("x", "half", "z")

f32 = jnp.float32
bf16 = jnp.bfloat16


def rounded_up(count, to):
    return -(-count // to) * to


def parts(x, count):
    out = []
    for i in range(count):
        piece = x.astype(bf16)
        out.append(piece)
        if i + 1 < count:
            x = x - piece.astype(f32)
    return out


def dot(a, b):
    return jnp.dot(a, b, preferred_element_type=f32)


def dot_t(a, b):
    return lax.dot_general(a, b, (((1,), (1,)), ((), ())), preferred_element_type=f32)


def one_hot(row, count):
    at = lax.broadcasted_iota(jnp.int32, (count, row.shape[1]), 0)
    return jnp.where(at == row, 1.0, 0.0).astype(bf16)


def picked(x, chosen):
    rows = x.shape[0]
    got = dot(jnp.concatenate(parts(x, 3), axis=0), chosen)
    return got[:rows] + got[rows : 2 * rows] + got[2 * rows :]


def placed(x, chosen):
    rows = x.shape[0]
    got = dot_t(jnp.concatenate(parts(x, 3), axis=0), chosen)
    return got[:rows] + got[rows : 2 * rows] + got[2 * rows :]


def start_kernel(
    states, inv_mass, shared, potential, cells, stiff,
    message, states_in, inv_in, shared_in, pot_in, cells_in, stiff_in, done,
):
    moves = [
        pltpu.make_async_copy(source, target, done.at[i])
        for i, (source, target) in enumerate(
            [
                (shared, shared_in), (inv_mass, inv_in), (states, states_in),
                (potential, pot_in), (cells, cells_in), (stiff, stiff_in),
            ]
        )
    ]
    for move in moves:
        move.start()
    for move in moves[:3]:
        move.wait()
    owned = states_in.shape[1]
    both = jnp.concatenate(
        [states_in[...], jnp.broadcast_to(inv_in[...], (8, owned))], axis=0
    )
    message[...] = picked(both, one_hot(shared_in[...], owned))
    for move in moves[3:]:
        move.wait()


def prepare_kernel(
    cells, stiff, shared, scale, chosen_all, high, low, chosen, scale_row, cells_pad, stiff_pad
):
    n_cells, npc = cells.shape
    pad = stiff_pad.shape[0]
    nodes = chosen_all.shape[0]
    cells_pad[...] = jnp.full(cells_pad.shape, -1, jnp.int32)
    cells_pad[:n_cells, :npc] = cells[...]
    stiff_pad[...] = jnp.zeros(stiff_pad.shape, f32)
    stiff_pad[:npc, :npc] = stiff[...]
    for c in range(n_cells):
        at = slice(c * pad, (c + 1) * pad)
        chosen_all[:, at] = one_hot(cells_pad[c : c + 1, :], nodes)
        scale_row[:, at] = jnp.full((1, pad), scale[c], f32)
    high[...], low[...] = parts(stiff_pad[...], 2)
    chosen[...] = one_hot(shared[...], chosen.shape[0])


def apply_cells(own, ghost, scale, chosen_all, high, low):
    rows, owned = own.shape
    pad = high.shape[0]
    n_cells = chosen_all.shape[1] // pad
    values = jnp.concatenate([own, ghost], axis=1)
    gathered = dot(jnp.concatenate(parts(values, 2), axis=0), chosen_all[...])
    gathered = gathered.astype(bf16)
    stacked = jnp.concatenate(
        [gathered[:rows, c * pad : (c + 1) * pad] for c in range(n_cells)]
        + [gathered[rows:, c * pad : (c + 1) * pad] for c in range(n_cells)],
        axis=0,
    )
    half = n_cells * rows
    by_high = dot(stacked, high[...])
    product = by_high[:half] + by_high[half:] + dot(stacked[:half], low[...])
    product = jnp.concatenate(
        [product[c * rows : (c + 1) * rows] for c in range(n_cells)], axis=1
    ) * scale[...]
    summed = dot_t(jnp.concatenate(parts(product, 2), axis=0), chosen_all[...])
    summed = summed[:rows] + summed[rows:]
    return summed[:, :owned], summed[:, owned:]


def is_even():
    return lax.axis_index("z") % 2 == 0


def send_both(up, down, near, far):
    even = is_even()
    near[...] = jnp.where(even, up, down)
    far[...] = jnp.zeros(far.shape, f32)
    far[: down.shape[0], :] = jnp.where(even, down, up)


def got_both(near, far):
    rows = near.shape[0]
    even = is_even()
    up = jnp.where(even, far[:rows, :], near[...])
    down = jnp.where(even, near[...], far[:rows, :])
    return up, down


def first_kernel(
    states, fetched, inv_mass, potential, scale, chosen_all, high, low, chosen,
    far, near, partial,
):
    rows, owned = states.shape
    current = states[...]
    ghost_inv = fetched[rows : rows + 1, :]
    ghost = fetched[:rows, :]
    own_sum, ghost_sum = apply_cells(
        current * inv_mass[...], ghost * ghost_inv, scale, chosen_all, high, low
    )
    up = ghost_inv * ghost_sum * (1.0 / HALF_WIDTH)
    here = (inv_mass[...] * own_sum + (potential[...] - CENTER) * current) * (1.0 / HALF_WIDTH)
    partial[:, :owned] = here
    partial[:, owned:] = up
    send_both(up, picked(here, chosen[...]), near, far)


def complete(part, got_near, got_far, chosen):
    owned = chosen.shape[0]
    got_up, got_down = got_both(got_near, got_far)
    return part[:, :owned] + placed(got_up, chosen[...]), part[:, owned:] + got_down


def next_kernel(
    previous, part, fetched, got_near, got_far, inv_mass, potential, scale, chosen_all,
    high, low, chosen, far, near, partial, current_out,
):
    rows, owned = current_out.shape
    current, ghost = complete(part, got_near, got_far, chosen)
    ghost_inv = fetched[rows : rows + 1, :]
    own_sum, ghost_sum = apply_cells(
        current * inv_mass[...], ghost * ghost_inv, scale, chosen_all, high, low
    )
    up = ghost_inv * ghost_sum * (2.0 / HALF_WIDTH)
    here = (inv_mass[...] * own_sum + (potential[...] - CENTER) * current) * (
        2.0 / HALF_WIDTH
    ) - previous[...]
    current_out[...] = current
    partial[:, :owned] = here
    partial[:, owned:] = up
    send_both(up, picked(here, chosen[...]), near, far)


def finish_kernel(part, got_near, got_far, chosen, filtered, left):
    owned = filtered.shape[1]
    current, ghost = complete(part, got_near, got_far, chosen)
    filtered[...] = current
    left[:, :owned] = current
    left[:, owned:] = ghost


def gram_kernel(total_nodes, left, sibling, *rest):
    blocks, (out, g_high, g_low) = rest[:-3], rest[-3:]
    chips = len(blocks)
    rows = left.shape[0]
    chip = lax.axis_index("chip")
    core = lax.axis_index("core")
    for s in range(chips):
        at = pl.ds(pl.multiple_of(lax.rem(chip - s + chips, chips) * rows, rows), rows)
        g_high[at, :], g_low[at, :] = parts(blocks[s][...], 2)
    high, low = parts(jnp.concatenate([left[...], sibling[...]], axis=0), 2)
    by_high = dot_t(jnp.concatenate([high, low], axis=0), g_high[...])
    whole = by_high[: 2 * rows] + by_high[2 * rows :] + dot_t(high, g_low[...])
    whole = whole * (1.0 / total_nodes)
    out[pl.ds(pl.multiple_of(core * rows, rows), rows), :] = whole[:rows]
    out[pl.ds(pl.multiple_of((1 - core) * rows, rows), rows), :] = whole[rows:]


def fold_kernel(rows, pieces, out):
    count = pieces.shape[0] // 2
    copies = out.shape[0]
    sums = []
    for core in range(2):
        total = pieces[core * count]
        for i in range(1, count):
            total = total + pieces[core * count + i]
        sums.append(total)
    chips = pieces.shape[2] // rows
    ordered = jnp.concatenate(
        [sums[core][:, i * rows : (i + 1) * rows] for i in range(chips) for core in range(2)],
        axis=1,
    )
    for i in range(copies):
        out[i] = ordered


def per_device(
    states_in, stiffness, cell_scale, potential, inv_mass_sqrt, cell_nodes, shared_nodes
):
    rows, owned = states_in.shape
    shared_count = shared_nodes.shape[0]
    n_cells, npc = cell_nodes.shape
    nodes = owned + shared_count
    pad = rounded_up(npc, 128)
    n_dom = lax.axis_size(DOM)
    n_band = lax.axis_size(BAND)
    chips = lax.axis_size("chip")
    backward = [(i, (i - 1) % n_dom) for i in range(n_dom)]
    near_pairs = [(i, i ^ 1) for i in range(n_dom)]
    far_pairs = [(i, (((i + 1) ^ 1) - 1) % n_dom) for i in range(n_dom)]

    in_vmem = pl.BlockSpec(memory_space=pltpu.VMEM)
    in_smem = pl.BlockSpec(memory_space=pltpu.SMEM)
    in_hbm = pl.BlockSpec(memory_space=pltpu.HBM)
    params = pltpu.CompilerParams(vmem_limit_bytes=LIMIT)

    def shape_of(*sizes, dtype=f32):
        return jax.ShapeDtypeStruct(sizes, dtype)

    block = shape_of(rows, owned)
    wide = shape_of(rows, nodes)
    edge = shape_of(rows, shared_count)
    tall = shape_of(rows + 8, shared_count)

    def call(kernel, out_shape, specs, scratch_shapes=()):
        return pl.pallas_call(
            kernel,
            out_shape=out_shape,
            in_specs=specs,
            out_specs=jax.tree.map(lambda _: in_vmem, out_shape),
            scratch_shapes=scratch_shapes,
            compiler_params=params,
        )

    message, states, inv_mass, shared, pot, cells, stiff = call(
        start_kernel,
        (
            tall, block, shape_of(1, owned), shape_of(1, shared_count, dtype=jnp.int32),
            shape_of(1, owned), shape_of(n_cells, npc, dtype=jnp.int32), shape_of(npc, npc),
        ),
        [in_hbm] * 6,
        [pltpu.SemaphoreType.DMA((6,))],
    )(
        *(
            pltpu.with_memory_space_constraint(x, pltpu.HBM)
            for x in (
                states_in, inv_mass_sqrt.reshape(1, owned),
                shared_nodes.reshape(1, shared_count), potential.reshape(1, owned),
                cell_nodes, stiffness,
            )
        )
    )
    fetched = lax.ppermute(message, DOM, backward)
    prepared = call(
        prepare_kernel,
        (
            shape_of(nodes, n_cells * pad, dtype=bf16),
            shape_of(pad, pad, dtype=bf16),
            shape_of(pad, pad, dtype=bf16),
            shape_of(owned, shared_count, dtype=bf16),
            shape_of(1, n_cells * pad),
        ),
        [in_vmem] * 3 + [in_smem],
        [pltpu.VMEM((8, pad), jnp.int32), pltpu.VMEM((pad, pad), f32)],
    )(cells, stiff, shared, cell_scale)
    *matrices, chosen, scale_row = prepared
    fixed = (inv_mass, pot, scale_row, *matrices, chosen)

    def swapped(near, far):
        return lax.ppermute(near, DOM, near_pairs), lax.ppermute(far, DOM, far_pairs)

    far, near, partial = call(first_kernel, (tall, edge, wide), [in_vmem] * 9)(
        states, fetched, *fixed
    )
    previous = states
    for _ in range(DEGREE - 1):
        far, near, partial, previous = call(
            next_kernel, (tall, edge, wide, block), [in_vmem] * 12
        )(previous, partial, fetched, *swapped(near, far), *fixed)

    blocks = [partial] + [
        lax.ppermute(partial, "chip", [(i, (i + s) % chips) for i in range(chips)])
        for s in range(1, chips)
    ]
    filtered, left = call(finish_kernel, (block, wide), [in_vmem] * 4)(
        partial, *swapped(near, far), chosen
    )
    sibling = lax.ppermute(left, "core", [(0, 1), (1, 0)])
    gram = call(
        functools.partial(gram_kernel, owned * n_dom),
        shape_of(2 * rows, chips * rows),
        [in_vmem] * (2 + chips),
        [pltpu.VMEM((chips * rows, nodes), bf16)] * 2,
    )(left, sibling, *blocks)

    n_z = lax.axis_size("z")
    n_across = lax.axis_size(("x", "half"))
    each = rows // n_z
    pieces = lax.all_to_all(
        gram.reshape(2 * n_z, each, chips * rows), ("core", "z"), 0, 0, tiled=True
    )
    mine = call(functools.partial(fold_kernel, rows), shape_of(n_across, each, n_band * rows), [in_vmem])(pieces)
    spread = lax.all_to_all(mine, ("x", "half"), 0, 0, tiled=True)
    mine = jnp.sum(spread, axis=0)
    margin = lax.all_to_all(
        jnp.broadcast_to(mine[None], (n_z, *mine.shape)), "z", 0, 0, tiled=True
    )
    return filtered, margin.reshape(rows, n_band * rows)


def solution(mesh):
    fine = Mesh(mesh.devices.reshape(4, 2, 4, 2, 8), BAND + DOM)
    return jax.shard_map(
        per_device,
        mesh=fine,
        in_specs=(P(BAND, DOM), P(), P(DOM), P(DOM), P(DOM), P(DOM, None), P(DOM)),
        out_specs=(P(BAND, DOM), P(BAND, None)),
        check_vma=False,
    )
```

```python
import functools

import jax
import jax.numpy as jnp
from jax import lax
from jax.experimental import pallas as pl
from jax.experimental.pallas import tpu as pltpu
from jax.sharding import Mesh, PartitionSpec as P

DEGREE = 3
CENTER = 1.0
HALF_WIDTH = 4.0
LIMIT = 28 * 1024 * 1024
BAND = ("chip", "core")
DOM = ("x", "half", "z")

f32 = jnp.float32
bf16 = jnp.bfloat16


def rounded_up(count, to):
    return -(-count // to) * to


def parts(x, count):
    out = []
    for i in range(count):
        piece = x.astype(bf16)
        out.append(piece)
        if i + 1 < count:
            x = x - piece.astype(f32)
    return out


def dot(a, b):
    return jnp.dot(a, b, preferred_element_type=f32)


def dot_t(a, b):
    return lax.dot_general(a, b, (((1,), (1,)), ((), ())), preferred_element_type=f32)


def one_hot(row, count):
    at = lax.broadcasted_iota(jnp.int16, (count, row.shape[1]), 0)
    return jnp.where(at == row.astype(jnp.int16), jnp.array(1, bf16), jnp.array(0, bf16))


def picked(x, chosen):
    rows = x.shape[0]
    got = dot(jnp.concatenate(parts(x, 3), axis=0), chosen)
    return got[:rows] + got[rows : 2 * rows] + got[2 * rows :]


def placed(x, chosen):
    rows = x.shape[0]
    got = dot_t(jnp.concatenate(parts(x, 3), axis=0), chosen)
    return got[:rows] + got[rows : 2 * rows] + got[2 * rows :]


def start_kernel(
    states, inv_mass, shared, potential, cells, stiff,
    message, states_in, inv_in, shared_in, pot_in, cells_in, stiff_in, done,
):
    moves = [
        pltpu.make_async_copy(source, target, done.at[i])
        for i, (source, target) in enumerate(
            [
                (shared, shared_in), (inv_mass, inv_in), (states, states_in),
                (potential, pot_in), (cells, cells_in), (stiff, stiff_in),
            ]
        )
    ]
    for move in moves:
        move.start()
    for move in moves[:3]:
        move.wait()
    owned = states_in.shape[1]
    both = jnp.concatenate(
        [states_in[...], jnp.broadcast_to(inv_in[...], (8, owned))], axis=0
    )
    message[...] = picked(both, one_hot(shared_in[...], owned))
    for move in moves[3:]:
        move.wait()


def prepare_kernel(
    cells, stiff, shared, scale, chosen_all, high, low, chosen, scale_row, cells_pad, stiff_pad
):
    n_cells, npc = cells.shape
    pad = stiff_pad.shape[0]
    nodes = chosen_all.shape[0]
    cells_pad[...] = jnp.full(cells_pad.shape, -1, jnp.int32)
    cells_pad[:n_cells, :npc] = cells[...]
    stiff_pad[...] = jnp.zeros(stiff_pad.shape, f32)
    stiff_pad[:npc, :npc] = stiff[...]
    for c in range(n_cells):
        at = slice(c * pad, (c + 1) * pad)
        chosen_all[:, at] = one_hot(cells_pad[c : c + 1, :], nodes)
        scale_row[:, at] = jnp.full((1, pad), scale[c], f32)
    high[...], low[...] = parts(stiff_pad[...], 2)
    chosen[...] = one_hot(shared[...], chosen.shape[0])


def apply_cells(own, ghost, scale, chosen_all, high, low):
    rows, owned = own.shape
    pad = high.shape[0]
    n_cells = chosen_all.shape[1] // pad
    values = jnp.concatenate([own, ghost], axis=1)
    gathered = dot(jnp.concatenate(parts(values, 2), axis=0), chosen_all[...])
    gathered = gathered.astype(bf16)
    stacked = jnp.concatenate(
        [gathered[:rows, c * pad : (c + 1) * pad] for c in range(n_cells)]
        + [gathered[rows:, c * pad : (c + 1) * pad] for c in range(n_cells)],
        axis=0,
    )
    half = n_cells * rows
    by_high = dot(stacked, high[...])
    product = by_high[:half] + by_high[half:] + dot(stacked[:half], low[...])
    product = jnp.concatenate(
        [product[c * rows : (c + 1) * rows] for c in range(n_cells)], axis=1
    ) * scale[...]
    summed = dot_t(jnp.concatenate(parts(product, 2), axis=0), chosen_all[...])
    summed = summed[:rows] + summed[rows:]
    return summed[:, :owned], summed[:, owned:]


def is_even():
    return lax.axis_index("z") % 2 == 0


def send_both(up, down, near, far):
    even = is_even()
    near[...] = jnp.where(even, up, down)
    far[...] = jnp.zeros(far.shape, f32)
    far[: down.shape[0], :] = jnp.where(even, down, up)


def got_both(near, far):
    rows = near.shape[0]
    even = is_even()
    up = jnp.where(even, far[:rows, :], near[...])
    down = jnp.where(even, near[...], far[:rows, :])
    return up, down


def first_kernel(
    states, fetched, inv_mass, potential, scale, chosen_all, high, low, chosen,
    far, near, partial,
):
    rows, owned = states.shape
    current = states[...]
    ghost_inv = fetched[rows : rows + 1, :]
    ghost = fetched[:rows, :]
    own_sum, ghost_sum = apply_cells(
        current * inv_mass[...], ghost * ghost_inv, scale, chosen_all, high, low
    )
    up = ghost_inv * ghost_sum * (1.0 / HALF_WIDTH)
    here = (inv_mass[...] * own_sum + (potential[...] - CENTER) * current) * (1.0 / HALF_WIDTH)
    partial[:, :owned] = here
    partial[:, owned:] = up
    send_both(up, picked(here, chosen[...]), near, far)


def complete(part, got_up, got_down, chosen):
    owned = chosen.shape[0]
    return part[:, :owned] + placed(got_up, chosen[...]), part[:, owned:] + got_down


def next_kernel(
    previous, part, fetched, got_near, got_far, inv_mass, potential, scale, chosen_all,
    high, low, chosen, far, near, partial, current_out,
):
    rows, owned = current_out.shape
    current, ghost = complete(part, *got_both(got_near, got_far), chosen)
    ghost_inv = fetched[rows : rows + 1, :]
    own_sum, ghost_sum = apply_cells(
        current * inv_mass[...], ghost * ghost_inv, scale, chosen_all, high, low
    )
    up = ghost_inv * ghost_sum * (2.0 / HALF_WIDTH)
    here = (inv_mass[...] * own_sum + (potential[...] - CENTER) * current) * (
        2.0 / HALF_WIDTH
    ) - previous[...]
    current_out[...] = current
    partial[:, :owned] = here
    partial[:, owned:] = up
    send_both(up, picked(here, chosen[...]), near, far)


def finish_kernel(part, got_near, got_far, chosen, filtered, left):
    owned = filtered.shape[1]
    current, ghost = complete(part, *got_both(got_near, got_far), chosen)
    filtered[...] = current
    left[:, :owned] = current
    left[:, owned:] = ghost


def gram_kernel(total_nodes, left, sibling, *rest):
    blocks, (out, g_high, g_low) = rest[:-3], rest[-3:]
    rows = left.shape[0]
    chip = lax.axis_index("chip")
    core = lax.axis_index("core")
    for s, block in enumerate(blocks):
        at = pl.ds(pl.multiple_of((chip ^ s) * rows, rows), rows)
        g_high[at, :], g_low[at, :] = parts(block[...], 2)
    high, low = parts(jnp.concatenate([left[...], sibling[...]], axis=0), 2)
    by_high = dot_t(jnp.concatenate([high, low], axis=0), g_high[...])
    whole = by_high[: 2 * rows] + by_high[2 * rows :] + dot_t(high, g_low[...])
    whole = whole * (1.0 / total_nodes)
    out[pl.ds(pl.multiple_of(core * rows, rows), rows), :] = whole[:rows]
    out[pl.ds(pl.multiple_of((1 - core) * rows, rows), rows), :] = whole[rows:]


def fold_kernel(rows, pieces, out):
    count = pieces.shape[0] // 2
    copies = out.shape[0]
    sums = []
    for core in range(2):
        total = pieces[core * count]
        for i in range(1, count):
            total = total + pieces[core * count + i]
        sums.append(total)
    chips = pieces.shape[2] // rows
    ordered = jnp.concatenate(
        [sums[core][:, i * rows : (i + 1) * rows] for i in range(chips) for core in range(2)],
        axis=1,
    )
    for i in range(copies):
        out[i] = ordered


def per_device(
    states_in, stiffness, cell_scale, potential, inv_mass_sqrt, cell_nodes, shared_nodes
):
    rows, owned = states_in.shape
    shared_count = shared_nodes.shape[0]
    n_cells, npc = cell_nodes.shape
    nodes = owned + shared_count
    pad = rounded_up(npc, 128)
    n_dom = lax.axis_size(DOM)
    n_band = lax.axis_size(BAND)
    chips = lax.axis_size("chip")
    backward = [(i, (i - 1) % n_dom) for i in range(n_dom)]
    near_pairs = [(i, i ^ 1) for i in range(n_dom)]
    far_pairs = [(i, (((i + 1) ^ 1) - 1) % n_dom) for i in range(n_dom)]

    in_vmem = pl.BlockSpec(memory_space=pltpu.VMEM)
    in_smem = pl.BlockSpec(memory_space=pltpu.SMEM)
    in_hbm = pl.BlockSpec(memory_space=pltpu.HBM)
    params = pltpu.CompilerParams(vmem_limit_bytes=LIMIT)

    def shape_of(*sizes, dtype=f32):
        return jax.ShapeDtypeStruct(sizes, dtype)

    block = shape_of(rows, owned)
    wide = shape_of(rows, nodes)
    edge = shape_of(rows, shared_count)
    tall = shape_of(rows + 8, shared_count)

    def call(kernel, out_shape, specs, scratch_shapes=()):
        return pl.pallas_call(
            kernel,
            out_shape=out_shape,
            in_specs=specs,
            out_specs=jax.tree.map(lambda _: in_vmem, out_shape),
            scratch_shapes=scratch_shapes,
            compiler_params=params,
        )

    message, states, inv_mass, shared, pot, cells, stiff = call(
        start_kernel,
        (
            tall, block, shape_of(1, owned), shape_of(1, shared_count, dtype=jnp.int32),
            shape_of(1, owned), shape_of(n_cells, npc, dtype=jnp.int32), shape_of(npc, npc),
        ),
        [in_hbm] * 6,
        [pltpu.SemaphoreType.DMA((6,))],
    )(
        *(
            pltpu.with_memory_space_constraint(x, pltpu.HBM)
            for x in (
                states_in, inv_mass_sqrt.reshape(1, owned),
                shared_nodes.reshape(1, shared_count), potential.reshape(1, owned),
                cell_nodes, stiffness,
            )
        )
    )
    fetched = lax.ppermute(message, DOM, backward)
    prepared = call(
        prepare_kernel,
        (
            shape_of(nodes, n_cells * pad, dtype=bf16),
            shape_of(pad, pad, dtype=bf16),
            shape_of(pad, pad, dtype=bf16),
            shape_of(owned, shared_count, dtype=bf16),
            shape_of(1, n_cells * pad),
        ),
        [in_vmem] * 3 + [in_smem],
        [pltpu.VMEM((8, pad), jnp.int32), pltpu.VMEM((pad, pad), f32)],
    )(cells, stiff, shared, cell_scale)
    *matrices, chosen, scale_row = prepared
    fixed = (inv_mass, pot, scale_row, *matrices, chosen)

    def swapped(near, far):
        return lax.ppermute(near, DOM, near_pairs), lax.ppermute(far, DOM, far_pairs)

    far, near, partial = call(first_kernel, (tall, edge, wide), [in_vmem] * 9)(
        states, fetched, *fixed
    )
    previous = states
    for _ in range(DEGREE - 1):
        far, near, partial, previous = call(
            next_kernel, (tall, edge, wide, block), [in_vmem] * 12
        )(previous, partial, fetched, *swapped(near, far), *fixed)

    def from_chip(x, s):
        return lax.ppermute(x, "chip", [(i, i ^ s) for i in range(chips)])

    second = from_chip(partial, 2)
    blocks = [partial, from_chip(partial, 1), second, from_chip(second, 1)]

    filtered, left = call(finish_kernel, (block, wide), [in_vmem] * 4)(
        partial, *swapped(near, far), chosen
    )
    sibling = lax.ppermute(left, "core", [(0, 1), (1, 0)])
    gram = call(
        functools.partial(gram_kernel, owned * n_dom),
        shape_of(2 * rows, chips * rows),
        [in_vmem] * (2 + chips),
        [pltpu.VMEM((chips * rows, nodes), bf16)] * 2,
    )(left, sibling, *blocks)

    n_z = lax.axis_size("z")
    n_across = lax.axis_size(("x", "half"))
    each = rows // n_z
    pieces = lax.all_to_all(
        gram.reshape(2 * n_z, each, chips * rows), ("core", "z"), 0, 0, tiled=True
    )
    mine = call(functools.partial(fold_kernel, rows), shape_of(n_across, each, n_band * rows), [in_vmem])(pieces)
    spread = lax.all_to_all(mine, ("x", "half"), 0, 0, tiled=True)
    mine = jnp.sum(spread, axis=0)
    margin = lax.all_to_all(
        jnp.broadcast_to(mine[None], (n_z, *mine.shape)), "z", 0, 0, tiled=True
    )
    return filtered, margin.reshape(rows, n_band * rows)


def solution(mesh):
    fine = Mesh(mesh.devices.reshape(4, 2, 4, 2, 8), BAND + DOM)
    return jax.shard_map(
        per_device,
        mesh=fine,
        in_specs=(P(BAND, DOM), P(), P(DOM), P(DOM), P(DOM), P(DOM, None), P(DOM)),
        out_specs=(P(BAND, DOM), P(BAND, None)),
        check_vma=False,
    )
```

```python
import functools

import jax
import jax.numpy as jnp
from jax import lax
from jax.experimental import pallas as pl
from jax.experimental.pallas import tpu as pltpu
from jax.sharding import Mesh, PartitionSpec as P

DEGREE = 3
CENTER = 1.0
HALF_WIDTH = 4.0
LIMIT = 28 * 1024 * 1024
BAND = ("chip", "core")
DOM = ("x", "half", "z")

f32 = jnp.float32
bf16 = jnp.bfloat16


def rounded_up(count, to):
    return -(-count // to) * to


def parts(x, count):
    out = []
    for i in range(count):
        piece = x.astype(bf16)
        out.append(piece)
        if i + 1 < count:
            x = x - piece.astype(f32)
    return out


def dot(a, b):
    return jnp.dot(a, b, preferred_element_type=f32)


def dot_t(a, b):
    return lax.dot_general(a, b, (((1,), (1,)), ((), ())), preferred_element_type=f32)


def one_hot(row, count):
    at = lax.broadcasted_iota(jnp.int16, (count, row.shape[1]), 0)
    return jnp.where(at == row.astype(jnp.int16), jnp.array(1, bf16), jnp.array(0, bf16))


def picked(x, chosen):
    rows = x.shape[0]
    got = dot(jnp.concatenate(parts(x, 3), axis=0), chosen)
    return got[:rows] + got[rows : 2 * rows] + got[2 * rows :]


def placed(x, chosen):
    rows = x.shape[0]
    got = dot_t(jnp.concatenate(parts(x, 3), axis=0), chosen)
    return got[:rows] + got[rows : 2 * rows] + got[2 * rows :]


def start_kernel(
    states, inv_mass, shared, potential, cells, stiff,
    message, states_in, inv_in, shared_in, pot_in, cells_in, stiff_in, done,
):
    moves = [
        pltpu.make_async_copy(source, target, done.at[i])
        for i, (source, target) in enumerate(
            [
                (shared, shared_in), (inv_mass, inv_in), (states, states_in),
                (potential, pot_in), (cells, cells_in), (stiff, stiff_in),
            ]
        )
    ]
    for move in moves:
        move.start()
    for move in moves[:3]:
        move.wait()
    owned = states_in.shape[1]
    both = jnp.concatenate(
        [states_in[...], jnp.broadcast_to(inv_in[...], (8, owned))], axis=0
    )
    message[...] = picked(both, one_hot(shared_in[...], owned))
    for move in moves[3:]:
        move.wait()


def prepare_kernel(
    cells, stiff, shared, scale, chosen_all, high, low, chosen, scale_row, cells_pad, stiff_pad
):
    n_cells, npc = cells.shape
    pad = stiff_pad.shape[0]
    nodes = chosen_all.shape[0]
    cells_pad[...] = jnp.full(cells_pad.shape, -1, jnp.int32)
    cells_pad[:n_cells, :npc] = cells[...]
    stiff_pad[...] = jnp.zeros(stiff_pad.shape, f32)
    stiff_pad[:npc, :npc] = stiff[...]
    for c in range(n_cells):
        at = slice(c * pad, (c + 1) * pad)
        chosen_all[:, at] = one_hot(cells_pad[c : c + 1, :], nodes)
        scale_row[:, at] = jnp.full((1, pad), scale[c], f32)
    high[...], low[...] = parts(stiff_pad[...], 2)
    chosen[...] = one_hot(shared[...], chosen.shape[0])


def apply_cells(own, ghost, scale, chosen_all, high, low):
    rows, owned = own.shape
    pad = high.shape[0]
    n_cells = chosen_all.shape[1] // pad
    values = jnp.concatenate([own, ghost], axis=1)
    gathered = dot(jnp.concatenate(parts(values, 2), axis=0), chosen_all[...])
    gathered = gathered.astype(bf16)
    stacked = jnp.concatenate(
        [gathered[:rows, c * pad : (c + 1) * pad] for c in range(n_cells)]
        + [gathered[rows:, c * pad : (c + 1) * pad] for c in range(n_cells)],
        axis=0,
    )
    half = n_cells * rows
    by_high = dot(stacked, high[...])
    product = by_high[:half] + by_high[half:] + dot(stacked[:half], low[...])
    product = jnp.concatenate(
        [product[c * rows : (c + 1) * rows] for c in range(n_cells)], axis=1
    ) * scale[...]
    summed = dot_t(jnp.concatenate(parts(product, 2), axis=0), chosen_all[...])
    summed = summed[:rows] + summed[rows:]
    return summed[:, :owned], summed[:, owned:]


def is_even():
    return lax.axis_index("z") % 2 == 0


def send_both(up, down, near, far):
    even = is_even()
    near[...] = jnp.where(even, up, down)
    far[...] = jnp.zeros(far.shape, f32)
    far[: down.shape[0], :] = jnp.where(even, down, up)


def got_both(near, far):
    rows = near.shape[0]
    even = is_even()
    up = jnp.where(even, far[:rows, :], near[...])
    down = jnp.where(even, near[...], far[:rows, :])
    return up, down


def first_kernel(
    states, fetched, inv_mass, potential, scale, chosen_all, high, low, chosen,
    far, near, partial,
):
    rows, owned = states.shape
    current = states[...]
    ghost_inv = fetched[rows : rows + 1, :]
    ghost = fetched[:rows, :]
    own_sum, ghost_sum = apply_cells(
        current * inv_mass[...], ghost * ghost_inv, scale, chosen_all, high, low
    )
    up = ghost_inv * ghost_sum * (1.0 / HALF_WIDTH)
    here = (inv_mass[...] * own_sum + (potential[...] - CENTER) * current) * (1.0 / HALF_WIDTH)
    partial[:, :owned] = here
    partial[:, owned:] = up
    send_both(up, picked(here, chosen[...]), near, far)


def complete(part, got_up, got_down, chosen):
    owned = chosen.shape[0]
    return part[:, :owned] + placed(got_up, chosen[...]), part[:, owned:] + got_down


def next_kernel(
    previous, part, fetched, got_near, got_far, inv_mass, potential, scale, chosen_all,
    high, low, chosen, far, near, partial, current_out,
):
    rows, owned = current_out.shape
    current, ghost = complete(part, *got_both(got_near, got_far), chosen)
    ghost_inv = fetched[rows : rows + 1, :]
    own_sum, ghost_sum = apply_cells(
        current * inv_mass[...], ghost * ghost_inv, scale, chosen_all, high, low
    )
    up = ghost_inv * ghost_sum * (2.0 / HALF_WIDTH)
    here = (inv_mass[...] * own_sum + (potential[...] - CENTER) * current) * (
        2.0 / HALF_WIDTH
    ) - previous[...]
    current_out[...] = current
    partial[:, :owned] = here
    partial[:, owned:] = up
    send_both(up, picked(here, chosen[...]), near, far)


def relay_kernel(block, near, far, out):
    del near, far
    out[:8, :128] = block[:8, :128]


def late_kernel(got_near, got_far, late):
    late[...] = jnp.concatenate(got_both(got_near, got_far), axis=1)


def halves(late):
    count = late.shape[1] // 2
    return late[:, :count], late[:, count:]


def finish_kernel(part, late, chosen, filtered, left):
    owned = filtered.shape[1]
    current, ghost = complete(part, *halves(late), chosen)
    filtered[...] = current
    left[:, :owned] = current
    left[:, owned:] = ghost


def gram_kernel(total_nodes, left, sibling, late, chosen, *rest):
    blocks, (out, g_high, g_low) = rest[:-3], rest[-3:]
    chips = len(blocks)
    rows, owned = left.shape[0], chosen.shape[0]
    chip = lax.axis_index("chip")
    core = lax.axis_index("core")
    for s in range(chips):
        at = pl.ds(pl.multiple_of((chip ^ s) * rows, rows), rows)
        g_high[at, :], g_low[at, :] = parts(blocks[s][...], 2)
    theirs = jnp.concatenate(complete(sibling, *halves(late), chosen), axis=1)
    high, low = parts(jnp.concatenate([left[...], theirs], axis=0), 2)
    by_high = dot_t(jnp.concatenate([high, low], axis=0), g_high[...])
    whole = by_high[: 2 * rows] + by_high[2 * rows :] + dot_t(high, g_low[...])
    whole = whole * (1.0 / total_nodes)
    out[pl.ds(pl.multiple_of(core * rows, rows), rows), :] = whole[:rows]
    out[pl.ds(pl.multiple_of((1 - core) * rows, rows), rows), :] = whole[rows:]


def fold_kernel(rows, pieces, out):
    count = pieces.shape[0] // 2
    copies = out.shape[0]
    sums = []
    for core in range(2):
        total = pieces[core * count]
        for i in range(1, count):
            total = total + pieces[core * count + i]
        sums.append(total)
    chips = pieces.shape[2] // rows
    ordered = jnp.concatenate(
        [sums[core][:, i * rows : (i + 1) * rows] for i in range(chips) for core in range(2)],
        axis=1,
    )
    for i in range(copies):
        out[i] = ordered


def per_device(
    states_in, stiffness, cell_scale, potential, inv_mass_sqrt, cell_nodes, shared_nodes
):
    rows, owned = states_in.shape
    shared_count = shared_nodes.shape[0]
    n_cells, npc = cell_nodes.shape
    nodes = owned + shared_count
    pad = rounded_up(npc, 128)
    n_dom = lax.axis_size(DOM)
    n_band = lax.axis_size(BAND)
    chips = lax.axis_size("chip")
    backward = [(i, (i - 1) % n_dom) for i in range(n_dom)]
    near_pairs = [(i, i ^ 1) for i in range(n_dom)]
    far_pairs = [(i, (((i + 1) ^ 1) - 1) % n_dom) for i in range(n_dom)]

    in_vmem = pl.BlockSpec(memory_space=pltpu.VMEM)
    in_smem = pl.BlockSpec(memory_space=pltpu.SMEM)
    in_hbm = pl.BlockSpec(memory_space=pltpu.HBM)
    params = pltpu.CompilerParams(vmem_limit_bytes=LIMIT)

    def shape_of(*sizes, dtype=f32):
        return jax.ShapeDtypeStruct(sizes, dtype)

    block = shape_of(rows, owned)
    wide = shape_of(rows, nodes)
    edge = shape_of(rows, shared_count)
    tall = shape_of(rows + 8, shared_count)

    def call(kernel, out_shape, specs, scratch_shapes=(), aliases={}):
        return pl.pallas_call(
            kernel,
            out_shape=out_shape,
            in_specs=specs,
            out_specs=jax.tree.map(lambda _: in_vmem, out_shape),
            scratch_shapes=scratch_shapes,
            input_output_aliases=aliases,
            compiler_params=params,
        )

    message, states, inv_mass, shared, pot, cells, stiff = call(
        start_kernel,
        (
            tall, block, shape_of(1, owned), shape_of(1, shared_count, dtype=jnp.int32),
            shape_of(1, owned), shape_of(n_cells, npc, dtype=jnp.int32), shape_of(npc, npc),
        ),
        [in_hbm] * 6,
        [pltpu.SemaphoreType.DMA((6,))],
    )(
        *(
            pltpu.with_memory_space_constraint(x, pltpu.HBM)
            for x in (
                states_in, inv_mass_sqrt.reshape(1, owned),
                shared_nodes.reshape(1, shared_count), potential.reshape(1, owned),
                cell_nodes, stiffness,
            )
        )
    )
    fetched = lax.ppermute(message, DOM, backward)
    prepared = call(
        prepare_kernel,
        (
            shape_of(nodes, n_cells * pad, dtype=bf16),
            shape_of(pad, pad, dtype=bf16),
            shape_of(pad, pad, dtype=bf16),
            shape_of(owned, shared_count, dtype=bf16),
            shape_of(1, n_cells * pad),
        ),
        [in_vmem] * 3 + [in_smem],
        [pltpu.VMEM((8, pad), jnp.int32), pltpu.VMEM((pad, pad), f32)],
    )(cells, stiff, shared, cell_scale)
    *matrices, chosen, scale_row = prepared
    fixed = (inv_mass, pot, scale_row, *matrices, chosen)

    def swapped(near, far):
        return lax.ppermute(near, DOM, near_pairs), lax.ppermute(far, DOM, far_pairs)

    far, near, partial = call(first_kernel, (tall, edge, wide), [in_vmem] * 9)(
        states, fetched, *fixed
    )
    previous = states
    for _ in range(DEGREE - 1):
        far, near, partial, previous = call(
            next_kernel, (tall, edge, wide, block), [in_vmem] * 12
        )(previous, partial, fetched, *swapped(near, far), *fixed)

    def from_chip(x, s):
        return lax.ppermute(x, "chip", [(i, i ^ s) for i in range(chips)])

    got_near, got_far = swapped(near, far)
    second = from_chip(partial, 2)
    relayed = call(relay_kernel, wide, [in_vmem] * 3, aliases={0: 0})(
        second, got_near, got_far
    )
    blocks = [partial, from_chip(partial, 1), relayed, from_chip(relayed, 1)]

    def from_sibling(x):
        return lax.ppermute(x, "core", [(0, 1), (1, 0)])

    late = call(late_kernel, shape_of(rows, 2 * shared_count), [in_vmem] * 2)(
        got_near, got_far
    )
    filtered, left = call(finish_kernel, (block, wide), [in_vmem] * 3)(partial, late, chosen)
    gram = call(
        functools.partial(gram_kernel, owned * n_dom),
        shape_of(2 * rows, chips * rows),
        [in_vmem] * (4 + chips),
        [pltpu.VMEM((chips * rows, nodes), bf16)] * 2,
    )(left, from_sibling(partial), from_sibling(late), chosen, *blocks)

    n_z = lax.axis_size("z")
    n_across = lax.axis_size(("x", "half"))
    each = rows // n_z
    pieces = lax.all_to_all(
        gram.reshape(2 * n_z, each, chips * rows), ("core", "z"), 0, 0, tiled=True
    )
    mine = call(functools.partial(fold_kernel, rows), shape_of(n_across, each, n_band * rows), [in_vmem])(pieces)
    spread = lax.all_to_all(mine, ("x", "half"), 0, 0, tiled=True)
    mine = jnp.sum(spread, axis=0)
    margin = lax.all_to_all(
        jnp.broadcast_to(mine[None], (n_z, *mine.shape)), "z", 0, 0, tiled=True
    )
    return filtered, margin.reshape(rows, n_band * rows)


def solution(mesh):
    fine = Mesh(mesh.devices.reshape(4, 2, 4, 2, 8), BAND + DOM)
    return jax.shard_map(
        per_device,
        mesh=fine,
        in_specs=(P(BAND, DOM), P(), P(DOM), P(DOM), P(DOM), P(DOM, None), P(DOM)),
        out_specs=(P(BAND, DOM), P(BAND, None)),
        check_vma=False,
    )
```

```python
import functools

import jax
import jax.numpy as jnp
from jax import lax
from jax.experimental import pallas as pl
from jax.experimental.pallas import tpu as pltpu
from jax.sharding import Mesh, PartitionSpec as P

DEGREE = 3
CENTER = 1.0
HALF_WIDTH = 4.0
LIMIT = 28 * 1024 * 1024
BAND = ("chip", "core")
DOM = ("x", "half", "z")

f32 = jnp.float32
bf16 = jnp.bfloat16


def rounded_up(count, to):
    return -(-count // to) * to


def parts(x, count):
    out = []
    for i in range(count):
        piece = x.astype(bf16)
        out.append(piece)
        if i + 1 < count:
            x = x - piece.astype(f32)
    return out


def dot(a, b):
    return jnp.dot(a, b, preferred_element_type=f32)


def dot_t(a, b):
    return lax.dot_general(a, b, (((1,), (1,)), ((), ())), preferred_element_type=f32)


def one_hot(row, count):
    at = lax.broadcasted_iota(jnp.int16, (count, row.shape[1]), 0)
    return jnp.where(at == row.astype(jnp.int16), jnp.array(1, bf16), jnp.array(0, bf16))


def one_hot_rows(column, count):
    at = lax.broadcasted_iota(jnp.int16, (column.shape[0], count), 1)
    return jnp.where(at == column.astype(jnp.int16), jnp.array(1, bf16), jnp.array(0, bf16))


def picked(x, chosen):
    rows = x.shape[0]
    got = dot(jnp.concatenate(parts(x, 3), axis=0), chosen)
    return got[:rows] + got[rows : 2 * rows] + got[2 * rows :]


def placed(x, chosen_t):
    return picked(x, chosen_t)


def start_kernel(
    states, inv_mass, shared, potential, cells, stiff,
    message, states_in, inv_in, shared_in, pot_in, cells_in, stiff_in, done,
):
    moves = [
        pltpu.make_async_copy(source, target, done.at[i])
        for i, (source, target) in enumerate(
            [
                (shared, shared_in), (inv_mass, inv_in), (states, states_in),
                (potential, pot_in), (cells, cells_in), (stiff, stiff_in),
            ]
        )
    ]
    for move in moves:
        move.start()
    for move in moves[:3]:
        move.wait()
    owned = states_in.shape[1]
    both = jnp.concatenate(
        [states_in[...], jnp.broadcast_to(inv_in[...], (8, owned))], axis=0
    )
    message[...] = picked(both, one_hot(shared_in[...], owned))
    for move in moves[3:]:
        move.wait()


def prepare_kernel(
    cells, stiff, shared, scale,
    slots, late_slots, high, low, chosen, chosen_t, scale_row, cells_pad, stiff_pad,
):
    n_cells, npc = cells.shape
    pad = stiff_pad.shape[0]
    nodes = slots.shape[1]
    owned, shared_count = chosen.shape
    cells_pad[...] = jnp.full(cells_pad.shape, -1, jnp.int32)
    cells_pad[:n_cells, :npc] = cells[...]
    cells_pad[8:9, :shared_count] = shared[...]
    columns = jnp.transpose(cells_pad[...])
    shared_column = columns[:shared_count, 8:9]
    ghosts = lax.broadcasted_iota(jnp.int16, (shared_count, pad), 0) + jnp.int16(owned)
    shareds = jnp.broadcast_to(shared_column.astype(jnp.int16), (shared_count, pad))
    for c in range(n_cells):
        at = slice(c * pad, (c + 1) * pad)
        slots[at, :] = one_hot_rows(columns[:, c : c + 1], nodes)
        row = cells_pad[c : c + 1, :].astype(jnp.int16)
        for i, names in enumerate((shareds, ghosts)):
            late_slots[i * shared_count : (i + 1) * shared_count, at] = jnp.where(
                names == row, jnp.array(1, bf16), jnp.array(0, bf16)
            )
        scale_row[:, at] = jnp.full((1, pad), scale[c], f32)
    stiff_pad[...] = jnp.zeros(stiff_pad.shape, f32)
    stiff_pad[:npc, :npc] = stiff[...]
    high[...], low[...] = parts(stiff_pad[...], 2)
    chosen[...] = one_hot(shared[...], owned)
    chosen_t[...] = one_hot_rows(shared_column, owned)


def twice(x, apply):
    rows = x.shape[0]
    got = apply(jnp.concatenate(parts(x, 2), axis=0))
    return got[:rows] + got[rows:]


def first_gather_kernel(states, inv_mass, slots, gathered):
    owned = states.shape[1]
    values = states[...] * inv_mass[...]
    gathered[...] = twice(values, lambda x: dot_t(x, slots[:, :owned]))


def gather_kernel(part, fetched, inv_mass, slots, gathered):
    rows = part.shape[0]
    owned = inv_mass.shape[1]
    values = jnp.concatenate(
        [part[:, :owned] * inv_mass[...], part[:, owned:] * fetched[rows : rows + 1, :]],
        axis=1,
    )
    gathered[...] = twice(values, lambda x: dot_t(x, slots[...]))


def apply_cells(gathered, late, late_slots, scale, slots, high, low):
    rows = gathered.shape[0]
    pad = high.shape[0]
    n_cells = slots.shape[0] // pad
    values = gathered[...] + twice(late, lambda x: dot(x, late_slots))
    v_high, v_low = parts(values, 2)
    stacked = jnp.concatenate(
        [v_high[:, c * pad : (c + 1) * pad] for c in range(n_cells)]
        + [v_low[:, c * pad : (c + 1) * pad] for c in range(n_cells)],
        axis=0,
    )
    half = n_cells * rows
    by_high = dot(stacked, high[...])
    product = by_high[:half] + by_high[half:] + dot(stacked[:half], low[...])
    product = jnp.concatenate(
        [product[c * rows : (c + 1) * rows] for c in range(n_cells)], axis=1
    ) * scale[...]
    return twice(product, lambda x: dot(x, slots[...]))


def is_even():
    return lax.axis_index("z") % 2 == 0


def send_both(up, down, near, far):
    even = is_even()
    near[...] = jnp.where(even, up, down)
    far[...] = jnp.zeros(far.shape, f32)
    far[: down.shape[0], :] = jnp.where(even, down, up)


def got_both(near, far):
    rows = near.shape[0]
    even = is_even()
    up = jnp.where(even, far[:rows, :], near[...])
    down = jnp.where(even, near[...], far[:rows, :])
    return up, down


def first_kernel(
    states, gathered, fetched, inv_mass, potential, scale, slots, late_slots, high, low,
    chosen, far, near, partial,
):
    rows, owned = states.shape
    ghost_inv = fetched[rows : rows + 1, :]
    shared_count = chosen.shape[1]
    summed = apply_cells(
        gathered, fetched[:rows, :] * ghost_inv, late_slots[shared_count:, :], scale, slots,
        high, low,
    )
    up = ghost_inv * summed[:, owned:] * (1.0 / HALF_WIDTH)
    here = (
        inv_mass[...] * summed[:, :owned] + (potential[...] - CENTER) * states[...]
    ) * (1.0 / HALF_WIDTH)
    partial[:, :owned] = here
    partial[:, owned:] = up
    send_both(up, picked(here, chosen[...]), near, far)


def complete(part, got_up, got_down, chosen_t):
    owned = chosen_t.shape[1]
    return part[:, :owned] + placed(got_up, chosen_t[...]), part[:, owned:] + got_down


def next_kernel(
    previous, part, gathered, message, fetched, got_near, got_far, inv_mass, potential, scale,
    slots, late_slots, high, low, chosen, chosen_t, far, near, partial, current_out,
):
    rows, owned = current_out.shape
    got_up, got_down = got_both(got_near, got_far)
    ghost_inv = fetched[rows : rows + 1, :]
    shared_inv = message[rows : rows + 1, :]
    late = jnp.concatenate([got_up * shared_inv, got_down * ghost_inv], axis=1)
    summed = apply_cells(gathered, late, late_slots[...], scale, slots, high, low)
    current = part[:, :owned] + placed(got_up, chosen_t[...])
    up = ghost_inv * summed[:, owned:] * (2.0 / HALF_WIDTH)
    here = (inv_mass[...] * summed[:, :owned] + (potential[...] - CENTER) * current) * (
        2.0 / HALF_WIDTH
    ) - previous[...]
    current_out[...] = current
    partial[:, :owned] = here
    partial[:, owned:] = up
    send_both(up, picked(here, chosen[...]), near, far)


def relay_kernel(block, near, far, out):
    del near, far
    out[:8, :128] = block[:8, :128]


def late_kernel(got_near, got_far, late):
    late[...] = jnp.concatenate(got_both(got_near, got_far), axis=1)


def halves(late):
    count = late.shape[1] // 2
    return late[:, :count], late[:, count:]


def finish_kernel(part, late, chosen_t, filtered, left):
    owned = filtered.shape[1]
    current, ghost = complete(part, *halves(late), chosen_t)
    filtered[...] = current
    left[:, :owned] = current
    left[:, owned:] = ghost


def gram_kernel(total_nodes, left, sibling, late, chosen_t, *rest):
    blocks, (out, g_high, g_low) = rest[:-3], rest[-3:]
    chips = len(blocks)
    rows = left.shape[0]
    chip = lax.axis_index("chip")
    core = lax.axis_index("core")
    for s in range(chips):
        at = pl.ds(pl.multiple_of((chip ^ s) * rows, rows), rows)
        g_high[at, :], g_low[at, :] = parts(blocks[s][...], 2)
    theirs = jnp.concatenate(complete(sibling, *halves(late), chosen_t), axis=1)
    high, low = parts(jnp.concatenate([left[...], theirs], axis=0), 2)
    by_high = dot_t(jnp.concatenate([high, low], axis=0), g_high[...])
    whole = by_high[: 2 * rows] + by_high[2 * rows :] + dot_t(high, g_low[...])
    whole = whole * (1.0 / total_nodes)
    out[pl.ds(pl.multiple_of(core * rows, rows), rows), :] = whole[:rows]
    out[pl.ds(pl.multiple_of((1 - core) * rows, rows), rows), :] = whole[rows:]


def fold_kernel(rows, pieces, out):
    count = pieces.shape[0] // 2
    copies = out.shape[0]
    sums = []
    for core in range(2):
        total = pieces[core * count]
        for i in range(1, count):
            total = total + pieces[core * count + i]
        sums.append(total)
    chips = pieces.shape[2] // rows
    ordered = jnp.concatenate(
        [sums[core][:, i * rows : (i + 1) * rows] for i in range(chips) for core in range(2)],
        axis=1,
    )
    for i in range(copies):
        out[i] = ordered


def per_device(
    states_in, stiffness, cell_scale, potential, inv_mass_sqrt, cell_nodes, shared_nodes
):
    rows, owned = states_in.shape
    shared_count = shared_nodes.shape[0]
    n_cells, npc = cell_nodes.shape
    nodes = owned + shared_count
    pad = rounded_up(npc, 128)
    n_dom = lax.axis_size(DOM)
    n_band = lax.axis_size(BAND)
    chips = lax.axis_size("chip")
    backward = [(i, (i - 1) % n_dom) for i in range(n_dom)]
    near_pairs = [(i, i ^ 1) for i in range(n_dom)]
    far_pairs = [(i, (((i + 1) ^ 1) - 1) % n_dom) for i in range(n_dom)]

    in_vmem = pl.BlockSpec(memory_space=pltpu.VMEM)
    in_smem = pl.BlockSpec(memory_space=pltpu.SMEM)
    in_hbm = pl.BlockSpec(memory_space=pltpu.HBM)
    params = pltpu.CompilerParams(vmem_limit_bytes=LIMIT)

    def shape_of(*sizes, dtype=f32):
        return jax.ShapeDtypeStruct(sizes, dtype)

    block = shape_of(rows, owned)
    wide = shape_of(rows, nodes)
    edge = shape_of(rows, shared_count)
    tall = shape_of(rows + 8, shared_count)

    def call(kernel, out_shape, specs, scratch_shapes=(), aliases={}):
        return pl.pallas_call(
            kernel,
            out_shape=out_shape,
            in_specs=specs,
            out_specs=jax.tree.map(lambda _: in_vmem, out_shape),
            scratch_shapes=scratch_shapes,
            input_output_aliases=aliases,
            compiler_params=params,
        )

    message, states, inv_mass, shared, pot, cells, stiff = call(
        start_kernel,
        (
            tall, block, shape_of(1, owned), shape_of(1, shared_count, dtype=jnp.int32),
            shape_of(1, owned), shape_of(n_cells, npc, dtype=jnp.int32), shape_of(npc, npc),
        ),
        [in_hbm] * 6,
        [pltpu.SemaphoreType.DMA((6,))],
    )(
        *(
            pltpu.with_memory_space_constraint(x, pltpu.HBM)
            for x in (
                states_in, inv_mass_sqrt.reshape(1, owned),
                shared_nodes.reshape(1, shared_count), potential.reshape(1, owned),
                cell_nodes, stiffness,
            )
        )
    )
    fetched = lax.ppermute(message, DOM, backward)
    slot_count = n_cells * pad
    slots, late_slots, high, low, chosen, chosen_t, scale = call(
        prepare_kernel,
        (
            shape_of(slot_count, nodes, dtype=bf16),
            shape_of(2 * shared_count, slot_count, dtype=bf16),
            shape_of(pad, pad, dtype=bf16),
            shape_of(pad, pad, dtype=bf16),
            shape_of(owned, shared_count, dtype=bf16),
            shape_of(shared_count, owned, dtype=bf16),
            shape_of(1, slot_count),
        ),
        [in_vmem] * 3 + [in_smem],
        [pltpu.VMEM((16, pad), jnp.int32), pltpu.VMEM((pad, pad), f32)],
    )(cells, stiff, shared, cell_scale)
    fixed = (inv_mass, pot, scale, slots, late_slots, high, low, chosen)
    by_slot = shape_of(rows, slot_count)

    def swapped(near, far):
        return lax.ppermute(near, DOM, near_pairs), lax.ppermute(far, DOM, far_pairs)

    gathered = call(first_gather_kernel, by_slot, [in_vmem] * 3)(states, inv_mass, slots)
    far, near, partial = call(first_kernel, (tall, edge, wide), [in_vmem] * 11)(
        states, gathered, fetched, *fixed
    )
    previous = states
    for _ in range(DEGREE - 1):
        gathered = call(gather_kernel, by_slot, [in_vmem] * 4)(
            partial, fetched, inv_mass, slots
        )
        far, near, partial, previous = call(
            next_kernel, (tall, edge, wide, block), [in_vmem] * 16
        )(previous, partial, gathered, message, fetched, *swapped(near, far), *fixed, chosen_t)

    def from_chip(x, s):
        return lax.ppermute(x, "chip", [(i, i ^ s) for i in range(chips)])

    got_near, got_far = swapped(near, far)
    second = from_chip(partial, 2)
    relayed = call(relay_kernel, wide, [in_vmem] * 3, aliases={0: 0})(
        second, got_near, got_far
    )
    blocks = [partial, from_chip(partial, 1), relayed, from_chip(relayed, 1)]

    def from_sibling(x):
        return lax.ppermute(x, "core", [(0, 1), (1, 0)])

    late = call(late_kernel, shape_of(rows, 2 * shared_count), [in_vmem] * 2)(
        got_near, got_far
    )
    filtered, left = call(finish_kernel, (block, wide), [in_vmem] * 3)(partial, late, chosen_t)
    gram = call(
        functools.partial(gram_kernel, owned * n_dom),
        shape_of(2 * rows, chips * rows),
        [in_vmem] * (4 + chips),
        [pltpu.VMEM((chips * rows, nodes), bf16)] * 2,
    )(left, from_sibling(partial), from_sibling(late), chosen_t, *blocks)

    n_z = lax.axis_size("z")
    n_across = lax.axis_size(("x", "half"))
    each = rows // n_z
    pieces = lax.all_to_all(
        gram.reshape(2 * n_z, each, chips * rows), ("core", "z"), 0, 0, tiled=True
    )
    mine = call(functools.partial(fold_kernel, rows), shape_of(n_across, each, n_band * rows), [in_vmem])(pieces)
    spread = lax.all_to_all(mine, ("x", "half"), 0, 0, tiled=True)
    mine = jnp.sum(spread, axis=0)
    margin = lax.all_to_all(
        jnp.broadcast_to(mine[None], (n_z, *mine.shape)), "z", 0, 0, tiled=True
    )
    return filtered, margin.reshape(rows, n_band * rows)


def solution(mesh):
    fine = Mesh(mesh.devices.reshape(4, 2, 4, 2, 8), BAND + DOM)
    return jax.shard_map(
        per_device,
        mesh=fine,
        in_specs=(P(BAND, DOM), P(), P(DOM), P(DOM), P(DOM), P(DOM, None), P(DOM)),
        out_specs=(P(BAND, DOM), P(BAND, None)),
        check_vma=False,
    )
```

```python
import functools

import jax
import jax.numpy as jnp
from jax import lax
from jax.experimental import pallas as pl
from jax.experimental.pallas import tpu as pltpu
from jax.sharding import Mesh, PartitionSpec as P

DEGREE = 3
CENTER = 1.0
HALF_WIDTH = 4.0
LIMIT = 28 * 1024 * 1024
LATE = 8
BAND = ("chip", "core")
DOM = ("x", "half", "z")

f32 = jnp.float32
bf16 = jnp.bfloat16


def rounded_up(count, to):
    return -(-count // to) * to


def parts(x, count):
    out = []
    for i in range(count):
        piece = x.astype(bf16)
        out.append(piece)
        if i + 1 < count:
            x = x - piece.astype(f32)
    return out


def dot(a, b):
    return jnp.dot(a, b, preferred_element_type=f32)


def dot_t(a, b):
    return lax.dot_general(a, b, (((1,), (1,)), ((), ())), preferred_element_type=f32)


def one_hot(row, count):
    at = lax.broadcasted_iota(jnp.int16, (count, row.shape[1]), 0)
    return jnp.where(at == row.astype(jnp.int16), jnp.array(1, bf16), jnp.array(0, bf16))


def one_hot_rows(column, count):
    at = lax.broadcasted_iota(jnp.int16, (column.shape[0], count), 1)
    return jnp.where(at == column.astype(jnp.int16), jnp.array(1, bf16), jnp.array(0, bf16))


def picked(x, chosen):
    rows = x.shape[0]
    got = dot(jnp.concatenate(parts(x, 3), axis=0), chosen)
    return got[:rows] + got[rows : 2 * rows] + got[2 * rows :]


def placed(x, chosen_t):
    return picked(x, chosen_t)


def start_kernel(
    states, inv_mass, shared, potential, cells, stiff,
    message, states_in, inv_in, shared_in, pot_in, cells_in, stiff_in, done,
):
    moves = [
        pltpu.make_async_copy(source, target, done.at[i])
        for i, (source, target) in enumerate(
            [
                (shared, shared_in), (inv_mass, inv_in), (states, states_in),
                (potential, pot_in), (cells, cells_in), (stiff, stiff_in),
            ]
        )
    ]
    for move in moves:
        move.start()
    for move in moves[:3]:
        move.wait()
    owned = states_in.shape[1]
    both = jnp.concatenate(
        [states_in[...], jnp.broadcast_to(inv_in[...], (8, owned))], axis=0
    )
    message[...] = picked(both, one_hot(shared_in[...], owned))
    for move in moves[3:]:
        move.wait()


def prepare_kernel(
    cells, stiff, shared, scale,
    slots, late_slots, high, low, chosen, chosen_t, scale_row, cells_pad, stiff_pad,
):
    n_cells, npc = cells.shape
    pad = stiff_pad.shape[0]
    nodes = slots.shape[1]
    owned, shared_count = chosen.shape
    cells_pad[...] = jnp.full(cells_pad.shape, -1, jnp.int32)
    cells_pad[:n_cells, :npc] = cells[...]
    cells_pad[8:9, :shared_count] = shared[...]
    columns = jnp.transpose(cells_pad[...])
    shared_column = columns[:shared_count, 8:9]
    ghosts = lax.broadcasted_iota(jnp.int16, (shared_count, pad), 0) + jnp.int16(owned)
    shareds = jnp.broadcast_to(shared_column.astype(jnp.int16), (shared_count, pad))
    for c in range(n_cells):
        at = slice(c * pad, (c + 1) * pad)
        slots[at, :] = one_hot_rows(columns[:, c : c + 1], nodes)
        row = cells_pad[c : c + 1, :].astype(jnp.int16)
        for i, names in enumerate((shareds, ghosts)):
            late_slots[i * shared_count : (i + 1) * shared_count, at] = jnp.where(
                names == row, jnp.array(1, bf16), jnp.array(0, bf16)
            )
        scale_row[:, at] = jnp.full((1, pad), scale[c], f32)
    stiff_pad[...] = jnp.zeros(stiff_pad.shape, f32)
    stiff_pad[:npc, :npc] = stiff[...]
    high[...], low[...] = parts(stiff_pad[...], 2)
    chosen[...] = one_hot(shared[...], owned)
    chosen_t[...] = one_hot_rows(shared_column, owned)


def twice(x, apply):
    rows = x.shape[0]
    got = apply(jnp.concatenate(parts(x, 2), axis=0))
    return got[:rows] + got[rows:]


def first_gather_kernel(states, inv_mass, slots, gathered):
    owned = states.shape[1]
    values = states[...] * inv_mass[...]
    gathered[...] = twice(values, lambda x: dot_t(x, slots[:, :owned]))


def gather_kernel(part, fetched, inv_mass, slots, gathered):
    rows = part.shape[0]
    owned = inv_mass.shape[1]
    values = jnp.concatenate(
        [part[:, :owned] * inv_mass[...], part[:, owned:] * fetched[rows : rows + 1, :]],
        axis=1,
    )
    gathered[...] = twice(values, lambda x: dot_t(x, slots[...]))


def apply_cells(gathered, late, late_slots, scale, slots, high, low):
    rows = gathered.shape[0]
    pad = high.shape[0]
    n_cells = slots.shape[0] // pad
    values = gathered[...] + twice(late, lambda x: dot(x, late_slots))
    v_high, v_low = parts(values, 2)
    stacked = jnp.concatenate(
        [v_high[:, c * pad : (c + 1) * pad] for c in range(n_cells)]
        + [v_low[:, c * pad : (c + 1) * pad] for c in range(n_cells)],
        axis=0,
    )
    half = n_cells * rows
    by_high = dot(stacked, high[...])
    product = by_high[:half] + by_high[half:] + dot(stacked[:half], low[...])
    product = jnp.concatenate(
        [product[c * rows : (c + 1) * rows] for c in range(n_cells)], axis=1
    ) * scale[...]
    return twice(product, lambda x: dot(x, slots[...]))


def is_even():
    return lax.axis_index("z") % 2 == 0


def send_both(up, down, near, far):
    even = is_even()
    near[...] = jnp.where(even, up, down)
    far[...] = jnp.zeros(far.shape, f32)
    far[: down.shape[0], :] = jnp.where(even, down, up)


def got_both(near, far):
    rows = near.shape[0]
    even = is_even()
    up = jnp.where(even, far[:rows, :], near[...])
    down = jnp.where(even, near[...], far[:rows, :])
    return up, down


def first_kernel(
    states, gathered, fetched, inv_mass, potential, scale, slots, late_slots, high, low,
    chosen, far, near, partial,
):
    rows, owned = states.shape
    ghost_inv = fetched[rows : rows + 1, :]
    shared_count = chosen.shape[1]
    summed = apply_cells(
        gathered, fetched[:rows, :] * ghost_inv, late_slots[shared_count:, :], scale, slots,
        high, low,
    )
    up = ghost_inv * summed[:, owned:] * (1.0 / HALF_WIDTH)
    here = (
        inv_mass[...] * summed[:, :owned] + (potential[...] - CENTER) * states[...]
    ) * (1.0 / HALF_WIDTH)
    partial[:, :owned] = here
    partial[:, owned:] = up
    send_both(up, picked(here, chosen[...]), near, far)


def complete(part, got_up, got_down, chosen_t):
    owned = chosen_t.shape[1]
    return part[:, :owned] + placed(got_up, chosen_t[...]), part[:, owned:] + got_down


def next_kernel(
    previous, part, gathered, message, fetched, got_near, got_far, inv_mass, potential, scale,
    slots, late_slots, high, low, chosen, chosen_t, far, near, partial, *current_out,
):
    rows, owned = previous.shape
    got_up, got_down = got_both(got_near, got_far)
    ghost_inv = fetched[rows : rows + 1, :]
    shared_inv = message[rows : rows + 1, :]
    late = jnp.concatenate([got_up * shared_inv, got_down * ghost_inv], axis=1)
    summed = apply_cells(gathered, late, late_slots[...], scale, slots, high, low)
    current = part[:, :owned] + placed(got_up, chosen_t[...])
    up = ghost_inv * summed[:, owned:] * (2.0 / HALF_WIDTH)
    here = (inv_mass[...] * summed[:, :owned] + (potential[...] - CENTER) * current) * (
        2.0 / HALF_WIDTH
    ) - previous[...]
    for out in current_out:
        out[...] = current
    partial[:, :owned] = here
    partial[:, owned:] = up
    send_both(up, picked(here, chosen[...]), near, far)


def relay_kernel(block, near, out):
    del near
    out[:8, :128] = block[:8, :128]


def late_kernel(got_near, got_far, late):
    up, down = got_both(got_near, got_far)
    count = up.shape[1]
    late[:, :count] = up
    late[:, count : 2 * count] = down
    late[:, 2 * count :] = jnp.zeros((up.shape[0], late.shape[1] - 2 * count), f32)


def halves(late, count):
    return late[:, :count], late[:, count : 2 * count]


def finish_kernel(part, late, chosen_t, filtered, left):
    owned = filtered.shape[1]
    current, ghost = complete(part, *halves(late, chosen_t.shape[0]), chosen_t)
    filtered[...] = current
    left[:, :owned] = current
    left[:, owned:] = ghost


def gram_kernel(total_nodes, left, sibling, late, chosen_t, *rest):
    blocks, (out, g_high, g_low) = rest[:-3], rest[-3:]
    chips = len(blocks)
    rows = left.shape[0]
    chip = lax.axis_index("chip")
    core = lax.axis_index("core")
    for s in range(chips):
        at = pl.ds(pl.multiple_of((chip ^ s) * rows, rows), rows)
        g_high[at, :], g_low[at, :] = parts(blocks[s][...], 2)
    theirs = jnp.concatenate(complete(sibling, *halves(late, chosen_t.shape[0]), chosen_t), axis=1)
    high, low = parts(jnp.concatenate([left[...], theirs], axis=0), 2)
    by_high = dot_t(jnp.concatenate([high, low], axis=0), g_high[...])
    whole = by_high[: 2 * rows] + by_high[2 * rows :] + dot_t(high, g_low[...])
    whole = whole * (1.0 / total_nodes)
    out[pl.ds(pl.multiple_of(core * rows, rows), rows), :] = whole[:rows]
    out[pl.ds(pl.multiple_of((1 - core) * rows, rows), rows), :] = whole[rows:]


def fold_kernel(rows, pieces, out):
    count = pieces.shape[0] // 2
    copies = out.shape[0]
    sums = []
    for core in range(2):
        total = pieces[core * count]
        for i in range(1, count):
            total = total + pieces[core * count + i]
        sums.append(total)
    chips = pieces.shape[2] // rows
    ordered = jnp.concatenate(
        [sums[core][:, i * rows : (i + 1) * rows] for i in range(chips) for core in range(2)],
        axis=1,
    )
    for i in range(copies):
        out[i] = ordered


def per_device(
    states_in, stiffness, cell_scale, potential, inv_mass_sqrt, cell_nodes, shared_nodes
):
    rows, owned = states_in.shape
    shared_count = shared_nodes.shape[0]
    n_cells, npc = cell_nodes.shape
    nodes = owned + shared_count
    pad = rounded_up(npc, 128)
    n_dom = lax.axis_size(DOM)
    n_band = lax.axis_size(BAND)
    chips = lax.axis_size("chip")
    backward = [(i, (i - 1) % n_dom) for i in range(n_dom)]
    near_pairs = [(i, i ^ 1) for i in range(n_dom)]
    far_pairs = [(i, (((i + 1) ^ 1) - 1) % n_dom) for i in range(n_dom)]

    in_vmem = pl.BlockSpec(memory_space=pltpu.VMEM)
    in_smem = pl.BlockSpec(memory_space=pltpu.SMEM)
    in_hbm = pl.BlockSpec(memory_space=pltpu.HBM)
    params = pltpu.CompilerParams(vmem_limit_bytes=LIMIT)

    def shape_of(*sizes, dtype=f32):
        return jax.ShapeDtypeStruct(sizes, dtype)

    block = shape_of(rows, owned)
    wide = shape_of(rows, nodes)
    edge = shape_of(rows, shared_count)
    tall = shape_of(rows + 8, shared_count)

    def call(kernel, out_shape, specs, scratch_shapes=(), aliases={}):
        return pl.pallas_call(
            kernel,
            out_shape=out_shape,
            in_specs=specs,
            out_specs=jax.tree.map(lambda _: in_vmem, out_shape),
            scratch_shapes=scratch_shapes,
            input_output_aliases=aliases,
            compiler_params=params,
        )

    message, states, inv_mass, shared, pot, cells, stiff = call(
        start_kernel,
        (
            tall, block, shape_of(1, owned), shape_of(1, shared_count, dtype=jnp.int32),
            shape_of(1, owned), shape_of(n_cells, npc, dtype=jnp.int32), shape_of(npc, npc),
        ),
        [in_hbm] * 6,
        [pltpu.SemaphoreType.DMA((6,))],
    )(
        *(
            pltpu.with_memory_space_constraint(x, pltpu.HBM)
            for x in (
                states_in, inv_mass_sqrt.reshape(1, owned),
                shared_nodes.reshape(1, shared_count), potential.reshape(1, owned),
                cell_nodes, stiffness,
            )
        )
    )
    fetched = lax.ppermute(message, DOM, backward)
    slot_count = n_cells * pad
    slots, late_slots, high, low, chosen, chosen_t, scale = call(
        prepare_kernel,
        (
            shape_of(slot_count, nodes, dtype=bf16),
            shape_of(2 * shared_count, slot_count, dtype=bf16),
            shape_of(pad, pad, dtype=bf16),
            shape_of(pad, pad, dtype=bf16),
            shape_of(owned, shared_count, dtype=bf16),
            shape_of(shared_count, owned, dtype=bf16),
            shape_of(1, slot_count),
        ),
        [in_vmem] * 3 + [in_smem],
        [pltpu.VMEM((16, pad), jnp.int32), pltpu.VMEM((pad, pad), f32)],
    )(cells, stiff, shared, cell_scale)
    fixed = (inv_mass, pot, scale, slots, late_slots, high, low, chosen)
    by_slot = shape_of(rows, slot_count)

    def swapped(near, far):
        return lax.ppermute(near, DOM, near_pairs), lax.ppermute(far, DOM, far_pairs)

    gathered = call(first_gather_kernel, by_slot, [in_vmem] * 3)(states, inv_mass, slots)
    far, near, partial = call(first_kernel, (tall, edge, wide), [in_vmem] * 11)(
        states, gathered, fetched, *fixed
    )
    previous = [states]
    for step in range(DEGREE - 1):
        gathered = call(gather_kernel, by_slot, [in_vmem] * 4)(
            partial, fetched, inv_mass, slots
        )
        currents = [block] * (step < DEGREE - 2)
        far, near, partial, *previous = call(
            next_kernel, (tall, edge, wide, *currents), [in_vmem] * 16
        )(*previous, partial, gathered, message, fetched, *swapped(near, far), *fixed, chosen_t)

    def from_chip(x, s):
        return lax.ppermute(x, "chip", [(i, i ^ s) for i in range(chips)])

    got_near, got_far = swapped(near, far)
    second = from_chip(partial, 2)
    relayed = call(relay_kernel, wide, [in_vmem] * 2, aliases={0: 0})(second, got_near)
    blocks = [partial, from_chip(partial, 1), relayed, from_chip(relayed, 1)]

    def from_sibling(x):
        return lax.ppermute(x, "core", [(0, 1), (1, 0)])

    late = call(late_kernel, shape_of(rows, LATE * shared_count), [in_vmem] * 2)(
        got_near, got_far
    )
    filtered, left = call(finish_kernel, (block, wide), [in_vmem] * 3)(partial, late, chosen_t)
    gram = call(
        functools.partial(gram_kernel, owned * n_dom),
        shape_of(2 * rows, chips * rows),
        [in_vmem] * (4 + chips),
        [pltpu.VMEM((chips * rows, nodes), bf16)] * 2,
    )(left, from_sibling(partial), from_sibling(late), chosen_t, *blocks)

    n_z = lax.axis_size("z")
    n_across = lax.axis_size(("x", "half"))
    each = rows // n_z
    pieces = lax.all_to_all(
        gram.reshape(2 * n_z, each, chips * rows), ("core", "z"), 0, 0, tiled=True
    )
    mine = call(functools.partial(fold_kernel, rows), shape_of(n_across, each, n_band * rows), [in_vmem])(pieces)
    spread = lax.all_to_all(mine, ("x", "half"), 0, 0, tiled=True)
    mine = jnp.sum(spread, axis=0)
    margin = lax.all_to_all(
        jnp.broadcast_to(mine[None], (n_z, *mine.shape)), "z", 0, 0, tiled=True
    )
    return filtered, margin.reshape(rows, n_band * rows)


def solution(mesh):
    fine = Mesh(mesh.devices.reshape(4, 2, 4, 2, 8), BAND + DOM)
    return jax.shard_map(
        per_device,
        mesh=fine,
        in_specs=(P(BAND, DOM), P(), P(DOM), P(DOM), P(DOM), P(DOM, None), P(DOM)),
        out_specs=(P(BAND, DOM), P(BAND, None)),
        check_vma=False,
    )
```

```python
import functools

import jax
import jax.numpy as jnp
from jax import lax
from jax.experimental import pallas as pl
from jax.experimental.pallas import tpu as pltpu
from jax.sharding import Mesh, PartitionSpec as P

DEGREE = 3
CENTER = 1.0
HALF_WIDTH = 4.0
LIMIT = 28 * 1024 * 1024
LATE = 8
BAND = ("chip", "core")
DOM = ("x", "half", "z")

f32 = jnp.float32
bf16 = jnp.bfloat16


def rounded_up(count, to):
    return -(-count // to) * to


def parts(x, count):
    out = []
    for i in range(count):
        piece = x.astype(bf16)
        out.append(piece)
        if i + 1 < count:
            x = x - piece.astype(f32)
    return out


def dot(a, b):
    return jnp.dot(a, b, preferred_element_type=f32)


def dot_t(a, b):
    return lax.dot_general(a, b, (((1,), (1,)), ((), ())), preferred_element_type=f32)


def one_hot(row, count):
    at = lax.broadcasted_iota(jnp.int16, (count, row.shape[1]), 0)
    return jnp.where(at == row.astype(jnp.int16), jnp.array(1, bf16), jnp.array(0, bf16))


def one_hot_rows(column, count):
    at = lax.broadcasted_iota(jnp.int16, (column.shape[0], count), 1)
    return jnp.where(at == column.astype(jnp.int16), jnp.array(1, bf16), jnp.array(0, bf16))


def picked(x, chosen):
    rows = x.shape[0]
    got = dot(jnp.concatenate(parts(x, 3), axis=0), chosen)
    return got[:rows] + got[rows : 2 * rows] + got[2 * rows :]


def placed(x, chosen_t):
    return picked(x, chosen_t)


def start_kernel(
    states, inv_mass, shared, potential, cells, stiff,
    message, states_in, inv_in, shared_in, pot_in, cells_in, stiff_in, done,
):
    moves = [
        pltpu.make_async_copy(source, target, done.at[i])
        for i, (source, target) in enumerate(
            [
                (shared, shared_in), (inv_mass, inv_in), (states, states_in),
                (potential, pot_in), (cells, cells_in), (stiff, stiff_in),
            ]
        )
    ]
    for move in moves:
        move.start()
    for move in moves[:3]:
        move.wait()
    owned = states_in.shape[1]
    both = jnp.concatenate(
        [states_in[...], jnp.broadcast_to(inv_in[...], (8, owned))], axis=0
    )
    message[...] = picked(both, one_hot(shared_in[...], owned))
    for move in moves[3:]:
        move.wait()


def prepare_kernel(
    cells, stiff, shared, scale,
    slots, late_slots, high, low, chosen, chosen_t, scale_row, cells_pad, stiff_pad,
):
    n_cells, npc = cells.shape
    pad = stiff_pad.shape[0]
    nodes = slots.shape[1]
    owned, shared_count = chosen.shape
    cells_pad[...] = jnp.full(cells_pad.shape, -1, jnp.int32)
    cells_pad[:n_cells, :npc] = cells[...]
    cells_pad[8:9, :shared_count] = shared[...]
    columns = jnp.transpose(cells_pad[...])
    shared_column = columns[:shared_count, 8:9]
    ghosts = lax.broadcasted_iota(jnp.int16, (shared_count, pad), 0) + jnp.int16(owned)
    shareds = jnp.broadcast_to(shared_column.astype(jnp.int16), (shared_count, pad))
    for c in range(n_cells):
        at = slice(c * pad, (c + 1) * pad)
        slots[at, :] = one_hot_rows(columns[:, c : c + 1], nodes)
        row = cells_pad[c : c + 1, :].astype(jnp.int16)
        for i, names in enumerate((shareds, ghosts)):
            late_slots[i * shared_count : (i + 1) * shared_count, at] = jnp.where(
                names == row, jnp.array(1, bf16), jnp.array(0, bf16)
            )
        scale_row[:, at] = jnp.full((1, pad), scale[c], f32)
    stiff_pad[...] = jnp.zeros(stiff_pad.shape, f32)
    stiff_pad[:npc, :npc] = stiff[...]
    high[...], low[...] = parts(stiff_pad[...], 2)
    chosen[...] = one_hot(shared[...], owned)
    chosen_t[...] = one_hot_rows(shared_column, owned)


def twice(x, apply):
    rows = x.shape[0]
    got = apply(jnp.concatenate(parts(x, 2), axis=0))
    return got[:rows] + got[rows:]


def first_gather_kernel(states, inv_mass, slots, gathered):
    owned = states.shape[1]
    values = states[...] * inv_mass[...]
    gathered[...] = twice(values, lambda x: dot_t(x, slots[:, :owned]))


def gather_kernel(part, fetched, inv_mass, slots, gathered):
    rows = part.shape[0]
    owned = inv_mass.shape[1]
    values = jnp.concatenate(
        [part[:, :owned] * inv_mass[...], part[:, owned:] * fetched[rows : rows + 1, :]],
        axis=1,
    )
    gathered[...] = twice(values, lambda x: dot_t(x, slots[...]))


def apply_cells(gathered, late, late_slots, scale, slots, high, low):
    rows = gathered.shape[0]
    pad = high.shape[0]
    n_cells = slots.shape[0] // pad
    values = gathered[...] + twice(late, lambda x: dot(x, late_slots))
    v_high, v_low = parts(values, 2)
    stacked = jnp.concatenate(
        [v_high[:, c * pad : (c + 1) * pad] for c in range(n_cells)]
        + [v_low[:, c * pad : (c + 1) * pad] for c in range(n_cells)],
        axis=0,
    )
    half = n_cells * rows
    by_high = dot(stacked, high[...])
    product = by_high[:half] + by_high[half:] + dot(stacked[:half], low[...])
    product = jnp.concatenate(
        [product[c * rows : (c + 1) * rows] for c in range(n_cells)], axis=1
    ) * scale[...]
    return twice(product, lambda x: dot(x, slots[...]))


def is_even():
    return lax.axis_index("z") % 2 == 0


def send_both(up, down, near, far):
    even = is_even()
    near[...] = jnp.where(even, up, down)
    far[...] = jnp.zeros(far.shape, f32)
    far[: down.shape[0], :] = jnp.where(even, down, up)


def got_both(near, far):
    rows = near.shape[0]
    even = is_even()
    up = jnp.where(even, far[:rows, :], near[...])
    down = jnp.where(even, near[...], far[:rows, :])
    return up, down


def first_kernel(
    states, gathered, fetched, inv_mass, potential, scale, slots, late_slots, high, low,
    chosen, far, near, partial,
):
    rows, owned = states.shape
    ghost_inv = fetched[rows : rows + 1, :]
    shared_count = chosen.shape[1]
    summed = apply_cells(
        gathered, fetched[:rows, :] * ghost_inv, late_slots[shared_count:, :], scale, slots,
        high, low,
    )
    up = ghost_inv * summed[:, owned:] * (1.0 / HALF_WIDTH)
    here = (
        inv_mass[...] * summed[:, :owned] + (potential[...] - CENTER) * states[...]
    ) * (1.0 / HALF_WIDTH)
    partial[:, :owned] = here
    partial[:, owned:] = up
    send_both(up, picked(here, chosen[...]), near, far)


def complete(part, got_up, got_down, chosen_t):
    owned = chosen_t.shape[1]
    return part[:, :owned] + placed(got_up, chosen_t[...]), part[:, owned:] + got_down


def next_kernel(
    previous, part, gathered, message, fetched, got_near, got_far, inv_mass, potential, scale,
    slots, late_slots, high, low, chosen, chosen_t, far, near, partial, *current_out,
):
    rows, owned = previous.shape
    got_up, got_down = got_both(got_near, got_far)
    ghost_inv = fetched[rows : rows + 1, :]
    shared_inv = message[rows : rows + 1, :]
    late = jnp.concatenate([got_up * shared_inv, got_down * ghost_inv], axis=1)
    summed = apply_cells(gathered, late, late_slots[...], scale, slots, high, low)
    current = part[:, :owned] + placed(got_up, chosen_t[...])
    up = ghost_inv * summed[:, owned:] * (2.0 / HALF_WIDTH)
    here = (inv_mass[...] * summed[:, :owned] + (potential[...] - CENTER) * current) * (
        2.0 / HALF_WIDTH
    ) - previous[...]
    for out in current_out:
        out[...] = current
    partial[:, :owned] = here
    partial[:, owned:] = up
    send_both(up, picked(here, chosen[...]), near, far)


def relay_kernel(block, beside, near, out):
    del beside, near
    out[:8, :128] = block[:8, :128]


def late_kernel(got_near, got_far, late):
    up, down = got_both(got_near, got_far)
    count = up.shape[1]
    late[:, :count] = up
    late[:, count : 2 * count] = down
    late[:, 2 * count :] = jnp.zeros((up.shape[0], late.shape[1] - 2 * count), f32)


def halves(late, count):
    return late[:, :count], late[:, count : 2 * count]


def finish_kernel(part, late, chosen_t, filtered, left):
    owned = filtered.shape[1]
    current, ghost = complete(part, *halves(late, chosen_t.shape[0]), chosen_t)
    filtered[...] = current
    left[:, :owned] = current
    left[:, owned:] = ghost


def gram_kernel(total_nodes, left, sibling, late, chosen_t, *rest):
    blocks, (out, g_high, g_low) = rest[:-3], rest[-3:]
    chips = len(blocks)
    rows = left.shape[0]
    chip = lax.axis_index("chip")
    core = lax.axis_index("core")
    for s in range(chips):
        at = pl.ds(pl.multiple_of((chip ^ s) * rows, rows), rows)
        g_high[at, :], g_low[at, :] = parts(blocks[s][...], 2)
    theirs = jnp.concatenate(complete(sibling, *halves(late, chosen_t.shape[0]), chosen_t), axis=1)
    high, low = parts(jnp.concatenate([left[...], theirs], axis=0), 2)
    by_high = dot_t(jnp.concatenate([high, low], axis=0), g_high[...])
    whole = by_high[: 2 * rows] + by_high[2 * rows :] + dot_t(high, g_low[...])
    whole = whole * (1.0 / total_nodes)
    out[pl.ds(pl.multiple_of(core * rows, rows), rows), :] = whole[:rows]
    out[pl.ds(pl.multiple_of((1 - core) * rows, rows), rows), :] = whole[rows:]


def fold_kernel(rows, pieces, out):
    count = pieces.shape[0] // 2
    copies = out.shape[0]
    sums = []
    for core in range(2):
        total = pieces[core * count]
        for i in range(1, count):
            total = total + pieces[core * count + i]
        sums.append(total)
    chips = pieces.shape[2] // rows
    ordered = jnp.concatenate(
        [sums[core][:, i * rows : (i + 1) * rows] for i in range(chips) for core in range(2)],
        axis=1,
    )
    for i in range(copies):
        out[i] = ordered


def per_device(
    states_in, stiffness, cell_scale, potential, inv_mass_sqrt, cell_nodes, shared_nodes
):
    rows, owned = states_in.shape
    shared_count = shared_nodes.shape[0]
    n_cells, npc = cell_nodes.shape
    nodes = owned + shared_count
    pad = rounded_up(npc, 128)
    n_dom = lax.axis_size(DOM)
    n_band = lax.axis_size(BAND)
    chips = lax.axis_size("chip")
    backward = [(i, (i - 1) % n_dom) for i in range(n_dom)]
    near_pairs = [(i, i ^ 1) for i in range(n_dom)]
    far_pairs = [(i, (((i + 1) ^ 1) - 1) % n_dom) for i in range(n_dom)]

    in_vmem = pl.BlockSpec(memory_space=pltpu.VMEM)
    in_smem = pl.BlockSpec(memory_space=pltpu.SMEM)
    in_hbm = pl.BlockSpec(memory_space=pltpu.HBM)
    params = pltpu.CompilerParams(vmem_limit_bytes=LIMIT)

    def shape_of(*sizes, dtype=f32):
        return jax.ShapeDtypeStruct(sizes, dtype)

    block = shape_of(rows, owned)
    wide = shape_of(rows, nodes)
    edge = shape_of(rows, shared_count)
    tall = shape_of(rows + 8, shared_count)

    def call(kernel, out_shape, specs, scratch_shapes=(), aliases={}):
        return pl.pallas_call(
            kernel,
            out_shape=out_shape,
            in_specs=specs,
            out_specs=jax.tree.map(lambda _: in_vmem, out_shape),
            scratch_shapes=scratch_shapes,
            input_output_aliases=aliases,
            compiler_params=params,
        )

    message, states, inv_mass, shared, pot, cells, stiff = call(
        start_kernel,
        (
            tall, block, shape_of(1, owned), shape_of(1, shared_count, dtype=jnp.int32),
            shape_of(1, owned), shape_of(n_cells, npc, dtype=jnp.int32), shape_of(npc, npc),
        ),
        [in_hbm] * 6,
        [pltpu.SemaphoreType.DMA((6,))],
    )(
        *(
            pltpu.with_memory_space_constraint(x, pltpu.HBM)
            for x in (
                states_in, inv_mass_sqrt.reshape(1, owned),
                shared_nodes.reshape(1, shared_count), potential.reshape(1, owned),
                cell_nodes, stiffness,
            )
        )
    )
    fetched = lax.ppermute(message, DOM, backward)
    slot_count = n_cells * pad
    slots, late_slots, high, low, chosen, chosen_t, scale = call(
        prepare_kernel,
        (
            shape_of(slot_count, nodes, dtype=bf16),
            shape_of(2 * shared_count, slot_count, dtype=bf16),
            shape_of(pad, pad, dtype=bf16),
            shape_of(pad, pad, dtype=bf16),
            shape_of(owned, shared_count, dtype=bf16),
            shape_of(shared_count, owned, dtype=bf16),
            shape_of(1, slot_count),
        ),
        [in_vmem] * 3 + [in_smem],
        [pltpu.VMEM((16, pad), jnp.int32), pltpu.VMEM((pad, pad), f32)],
    )(cells, stiff, shared, cell_scale)
    fixed = (inv_mass, pot, scale, slots, late_slots, high, low, chosen)
    by_slot = shape_of(rows, slot_count)

    def swapped(near, far):
        return lax.ppermute(near, DOM, near_pairs), lax.ppermute(far, DOM, far_pairs)

    gathered = call(first_gather_kernel, by_slot, [in_vmem] * 3)(states, inv_mass, slots)
    far, near, partial = call(first_kernel, (tall, edge, wide), [in_vmem] * 11)(
        states, gathered, fetched, *fixed
    )
    previous = [states]
    for step in range(DEGREE - 1):
        gathered = call(gather_kernel, by_slot, [in_vmem] * 4)(
            partial, fetched, inv_mass, slots
        )
        currents = [block] * (step < DEGREE - 2)
        far, near, partial, *previous = call(
            next_kernel, (tall, edge, wide, *currents), [in_vmem] * 16
        )(*previous, partial, gathered, message, fetched, *swapped(near, far), *fixed, chosen_t)

    def from_chip(x, s):
        return lax.ppermute(x, "chip", [(i, i ^ s) for i in range(chips)])

    got_near, got_far = swapped(near, far)
    second = from_chip(partial, 2)
    beside = from_chip(partial, 1)
    relayed = call(relay_kernel, wide, [in_vmem] * 3, aliases={0: 0})(
        second, beside, got_near
    )
    blocks = [partial, beside, relayed, from_chip(relayed, 1)]

    def from_sibling(x):
        return lax.ppermute(x, "core", [(0, 1), (1, 0)])

    late = call(late_kernel, shape_of(rows, LATE * shared_count), [in_vmem] * 2)(
        got_near, got_far
    )
    filtered, left = call(finish_kernel, (block, wide), [in_vmem] * 3)(partial, late, chosen_t)
    gram = call(
        functools.partial(gram_kernel, owned * n_dom),
        shape_of(2 * rows, chips * rows),
        [in_vmem] * (4 + chips),
        [pltpu.VMEM((chips * rows, nodes), bf16)] * 2,
    )(left, from_sibling(partial), from_sibling(late), chosen_t, *blocks)

    n_z = lax.axis_size("z")
    n_across = lax.axis_size(("x", "half"))
    each = rows // n_z
    pieces = lax.all_to_all(
        gram.reshape(2 * n_z, each, chips * rows), ("core", "z"), 0, 0, tiled=True
    )
    mine = call(functools.partial(fold_kernel, rows), shape_of(n_across, each, n_band * rows), [in_vmem])(pieces)
    spread = lax.all_to_all(mine, ("x", "half"), 0, 0, tiled=True)
    mine = jnp.sum(spread, axis=0)
    margin = lax.all_to_all(
        jnp.broadcast_to(mine[None], (n_z, *mine.shape)), "z", 0, 0, tiled=True
    )
    return filtered, margin.reshape(rows, n_band * rows)


def solution(mesh):
    fine = Mesh(mesh.devices.reshape(4, 2, 4, 2, 8), BAND + DOM)
    return jax.shard_map(
        per_device,
        mesh=fine,
        in_specs=(P(BAND, DOM), P(), P(DOM), P(DOM), P(DOM), P(DOM, None), P(DOM)),
        out_specs=(P(BAND, DOM), P(BAND, None)),
        check_vma=False,
    )
```

```python
import functools

import jax
import jax.numpy as jnp
from jax import lax
from jax.experimental import pallas as pl
from jax.experimental.pallas import tpu as pltpu
from jax.sharding import Mesh, PartitionSpec as P

DEGREE = 3
CENTER = 1.0
HALF_WIDTH = 4.0
LIMIT = 28 * 1024 * 1024
LATE = 8
BAND = ("chip", "core")
DOM = ("x", "half", "z")

f32 = jnp.float32
bf16 = jnp.bfloat16


def rounded_up(count, to):
    return -(-count // to) * to


def parts(x, count):
    out = []
    for i in range(count):
        piece = x.astype(bf16)
        out.append(piece)
        if i + 1 < count:
            x = x - piece.astype(f32)
    return out


def dot(a, b):
    return jnp.dot(a, b, preferred_element_type=f32)


def dot_t(a, b):
    return lax.dot_general(a, b, (((1,), (1,)), ((), ())), preferred_element_type=f32)


def one_hot(row, count):
    at = lax.broadcasted_iota(jnp.int16, (count, row.shape[1]), 0)
    return jnp.where(at == row.astype(jnp.int16), jnp.array(1, bf16), jnp.array(0, bf16))


def one_hot_rows(column, count):
    at = lax.broadcasted_iota(jnp.int16, (column.shape[0], count), 1)
    return jnp.where(at == column.astype(jnp.int16), jnp.array(1, bf16), jnp.array(0, bf16))


def picked(x, chosen):
    rows = x.shape[0]
    got = dot(jnp.concatenate(parts(x, 3), axis=0), chosen)
    return got[:rows] + got[rows : 2 * rows] + got[2 * rows :]


def placed(x, chosen_t):
    return picked(x, chosen_t)


def start_kernel(
    states, inv_mass, shared, potential, cells, stiff,
    message, states_in, inv_in, shared_in, pot_in, cells_in, stiff_in, done,
):
    moves = [
        pltpu.make_async_copy(source, target, done.at[i])
        for i, (source, target) in enumerate(
            [
                (shared, shared_in), (inv_mass, inv_in), (states, states_in),
                (potential, pot_in), (cells, cells_in), (stiff, stiff_in),
            ]
        )
    ]
    for move in moves:
        move.start()
    for move in moves[:3]:
        move.wait()
    owned = states_in.shape[1]
    both = jnp.concatenate(
        [states_in[...], jnp.broadcast_to(inv_in[...], (8, owned))], axis=0
    )
    message[...] = picked(both, one_hot(shared_in[...], owned))
    for move in moves[3:]:
        move.wait()


def prepare_kernel(
    cells, stiff, shared, scale,
    slots, late_slots, high, low, chosen, chosen_t, scale_row, cells_pad, stiff_pad,
):
    n_cells, npc = cells.shape
    pad = stiff_pad.shape[0]
    nodes = slots.shape[1]
    owned, shared_count = chosen.shape
    cells_pad[...] = jnp.full(cells_pad.shape, -1, jnp.int32)
    cells_pad[:n_cells, :npc] = cells[...]
    cells_pad[8:9, :shared_count] = shared[...]
    columns = jnp.transpose(cells_pad[...])
    shared_column = columns[:shared_count, 8:9]
    ghosts = lax.broadcasted_iota(jnp.int16, (shared_count, pad), 0) + jnp.int16(owned)
    shareds = jnp.broadcast_to(shared_column.astype(jnp.int16), (shared_count, pad))
    for c in range(n_cells):
        at = slice(c * pad, (c + 1) * pad)
        slots[at, :] = one_hot_rows(columns[:, c : c + 1], nodes)
        row = cells_pad[c : c + 1, :].astype(jnp.int16)
        for i, names in enumerate((shareds, ghosts)):
            late_slots[i * shared_count : (i + 1) * shared_count, at] = jnp.where(
                names == row, jnp.array(1, bf16), jnp.array(0, bf16)
            )
        scale_row[:, at] = jnp.full((1, pad), scale[c], f32)
    stiff_pad[...] = jnp.zeros(stiff_pad.shape, f32)
    stiff_pad[:npc, :npc] = stiff[...]
    high[...], low[...] = parts(stiff_pad[...], 2)
    chosen[...] = one_hot(shared[...], owned)
    chosen_t[...] = one_hot_rows(shared_column, owned)


def twice(x, apply):
    rows = x.shape[0]
    got = apply(jnp.concatenate(parts(x, 2), axis=0))
    return got[:rows] + got[rows:]


def first_gather_kernel(states, inv_mass, slots, gathered):
    owned = states.shape[1]
    values = states[...] * inv_mass[...]
    gathered[...] = twice(values, lambda x: dot_t(x, slots[:, :owned]))


def gather_kernel(part, fetched, inv_mass, slots, gathered):
    rows = part.shape[0]
    owned = inv_mass.shape[1]
    values = jnp.concatenate(
        [part[:, :owned] * inv_mass[...], part[:, owned:] * fetched[rows : rows + 1, :]],
        axis=1,
    )
    gathered[...] = twice(values, lambda x: dot_t(x, slots[...]))


def apply_cells(gathered, late, late_slots, scale, slots, high, low):
    rows = gathered.shape[0]
    pad = high.shape[0]
    n_cells = slots.shape[0] // pad
    values = gathered[...] + twice(late, lambda x: dot(x, late_slots))
    v_high, v_low = parts(values, 2)
    stacked = jnp.concatenate(
        [v_high[:, c * pad : (c + 1) * pad] for c in range(n_cells)]
        + [v_low[:, c * pad : (c + 1) * pad] for c in range(n_cells)],
        axis=0,
    )
    half = n_cells * rows
    by_high = dot(stacked, high[...])
    product = by_high[:half] + by_high[half:] + dot(stacked[:half], low[...])
    product = jnp.concatenate(
        [product[c * rows : (c + 1) * rows] for c in range(n_cells)], axis=1
    ) * scale[...]
    return twice(product, lambda x: dot(x, slots[...]))


def is_even():
    return lax.axis_index("z") % 2 == 0


def send_both(up, down, near, far):
    even = is_even()
    near[...] = jnp.where(even, up, down)
    far[...] = jnp.zeros(far.shape, f32)
    far[: down.shape[0], :] = jnp.where(even, down, up)


def got_both(near, far):
    rows = near.shape[0]
    even = is_even()
    up = jnp.where(even, far[:rows, :], near[...])
    down = jnp.where(even, near[...], far[:rows, :])
    return up, down


def first_kernel(
    states, gathered, fetched, inv_mass, potential, scale, slots, late_slots, high, low,
    chosen, far, near, partial,
):
    rows, owned = states.shape
    ghost_inv = fetched[rows : rows + 1, :]
    shared_count = chosen.shape[1]
    summed = apply_cells(
        gathered, fetched[:rows, :] * ghost_inv, late_slots[shared_count:, :], scale, slots,
        high, low,
    )
    up = ghost_inv * summed[:, owned:] * (1.0 / HALF_WIDTH)
    here = (
        inv_mass[...] * summed[:, :owned] + (potential[...] - CENTER) * states[...]
    ) * (1.0 / HALF_WIDTH)
    partial[:, :owned] = here
    partial[:, owned:] = up
    send_both(up, picked(here, chosen[...]), near, far)


def complete(part, late, chosen_t):
    count, owned = chosen_t.shape
    own = part[:, :owned] + placed(late[:, :count], chosen_t[...])
    return own, late[:, count : 2 * count]


def next_kernel(
    last, previous, part, gathered, message, fetched, got_near, got_far, inv_mass, potential, scale,
    slots, late_slots, high, low, chosen, chosen_t, far, near, partial, again,
):
    rows, owned = previous.shape
    got_up, got_down = got_both(got_near, got_far)
    ghost_inv = fetched[rows : rows + 1, :]
    shared_inv = message[rows : rows + 1, :]
    late = jnp.concatenate([got_up * shared_inv, got_down * ghost_inv], axis=1)
    summed = apply_cells(gathered, late, late_slots[...], scale, slots, high, low)
    current = part[:, :owned] + placed(got_up, chosen_t[...])
    up = ghost_inv * summed[:, owned:] * (2.0 / HALF_WIDTH)
    here = (inv_mass[...] * summed[:, :owned] + (potential[...] - CENTER) * current) * (
        2.0 / HALF_WIDTH
    ) - previous[...]
    partial[:, :owned] = here
    partial[:, owned:] = up
    again[...] = here if last else current
    send_both(up, picked(here, chosen[...]), near, far)


def relay_kernel(beside, block, own, near, block_out, own_out):
    del beside, near
    block_out[:8, :128] = block[:8, :128]
    own_out[:8, :128] = own[:8, :128]


def late_kernel(part, got_near, got_far, late):
    up, down = got_both(got_near, got_far)
    count = up.shape[1]
    late[:, :count] = up
    late[:, count : 2 * count] = part[:, part.shape[1] - count :] + down
    late[:, 2 * count :] = jnp.zeros((up.shape[0], late.shape[1] - 2 * count), f32)


def finish_kernel(part, late, chosen_t, filtered, left):
    owned = filtered.shape[1]
    current, ghost = complete(part, late, chosen_t)
    filtered[...] = current
    left[:, :owned] = current
    left[:, owned:] = ghost


def gram_kernel(total_nodes, left, sibling, late, chosen_t, *rest):
    blocks, (out, g_high, g_low) = rest[:-3], rest[-3:]
    chips = len(blocks)
    rows = left.shape[0]
    chip = lax.axis_index("chip")
    core = lax.axis_index("core")
    for s in range(chips):
        at = pl.ds(pl.multiple_of((chip ^ s) * rows, rows), rows)
        g_high[at, :], g_low[at, :] = parts(blocks[s][...], 2)
    theirs = jnp.concatenate(complete(sibling, late, chosen_t), axis=1)
    high, low = parts(jnp.concatenate([left[...], theirs], axis=0), 2)
    by_high = dot_t(jnp.concatenate([high, low], axis=0), g_high[...])
    whole = by_high[: 2 * rows] + by_high[2 * rows :] + dot_t(high, g_low[...])
    whole = whole * (1.0 / total_nodes)
    out[pl.ds(pl.multiple_of(core * rows, rows), rows), :] = whole[:rows]
    out[pl.ds(pl.multiple_of((1 - core) * rows, rows), rows), :] = whole[rows:]


def fold_kernel(rows, pieces, out):
    count = pieces.shape[0] // 2
    copies = out.shape[0]
    sums = []
    for core in range(2):
        total = pieces[core * count]
        for i in range(1, count):
            total = total + pieces[core * count + i]
        sums.append(total)
    chips = pieces.shape[2] // rows
    ordered = jnp.concatenate(
        [sums[core][:, i * rows : (i + 1) * rows] for i in range(chips) for core in range(2)],
        axis=1,
    )
    for i in range(copies):
        out[i] = ordered


def per_device(
    states_in, stiffness, cell_scale, potential, inv_mass_sqrt, cell_nodes, shared_nodes
):
    rows, owned = states_in.shape
    shared_count = shared_nodes.shape[0]
    n_cells, npc = cell_nodes.shape
    nodes = owned + shared_count
    pad = rounded_up(npc, 128)
    n_dom = lax.axis_size(DOM)
    n_band = lax.axis_size(BAND)
    chips = lax.axis_size("chip")
    backward = [(i, (i - 1) % n_dom) for i in range(n_dom)]
    near_pairs = [(i, i ^ 1) for i in range(n_dom)]
    far_pairs = [(i, (((i + 1) ^ 1) - 1) % n_dom) for i in range(n_dom)]

    in_vmem = pl.BlockSpec(memory_space=pltpu.VMEM)
    in_smem = pl.BlockSpec(memory_space=pltpu.SMEM)
    in_hbm = pl.BlockSpec(memory_space=pltpu.HBM)
    params = pltpu.CompilerParams(vmem_limit_bytes=LIMIT)

    def shape_of(*sizes, dtype=f32):
        return jax.ShapeDtypeStruct(sizes, dtype)

    block = shape_of(rows, owned)
    wide = shape_of(rows, nodes)
    edge = shape_of(rows, shared_count)
    tall = shape_of(rows + 8, shared_count)

    def call(kernel, out_shape, specs, scratch_shapes=(), aliases={}):
        return pl.pallas_call(
            kernel,
            out_shape=out_shape,
            in_specs=specs,
            out_specs=jax.tree.map(lambda _: in_vmem, out_shape),
            scratch_shapes=scratch_shapes,
            input_output_aliases=aliases,
            compiler_params=params,
        )

    message, states, inv_mass, shared, pot, cells, stiff = call(
        start_kernel,
        (
            tall, block, shape_of(1, owned), shape_of(1, shared_count, dtype=jnp.int32),
            shape_of(1, owned), shape_of(n_cells, npc, dtype=jnp.int32), shape_of(npc, npc),
        ),
        [in_hbm] * 6,
        [pltpu.SemaphoreType.DMA((6,))],
    )(
        *(
            pltpu.with_memory_space_constraint(x, pltpu.HBM)
            for x in (
                states_in, inv_mass_sqrt.reshape(1, owned),
                shared_nodes.reshape(1, shared_count), potential.reshape(1, owned),
                cell_nodes, stiffness,
            )
        )
    )
    fetched = lax.ppermute(message, DOM, backward)
    slot_count = n_cells * pad
    slots, late_slots, high, low, chosen, chosen_t, scale = call(
        prepare_kernel,
        (
            shape_of(slot_count, nodes, dtype=bf16),
            shape_of(2 * shared_count, slot_count, dtype=bf16),
            shape_of(pad, pad, dtype=bf16),
            shape_of(pad, pad, dtype=bf16),
            shape_of(owned, shared_count, dtype=bf16),
            shape_of(shared_count, owned, dtype=bf16),
            shape_of(1, slot_count),
        ),
        [in_vmem] * 3 + [in_smem],
        [pltpu.VMEM((16, pad), jnp.int32), pltpu.VMEM((pad, pad), f32)],
    )(cells, stiff, shared, cell_scale)
    fixed = (inv_mass, pot, scale, slots, late_slots, high, low, chosen)
    by_slot = shape_of(rows, slot_count)

    def swapped(near, far):
        return lax.ppermute(near, DOM, near_pairs), lax.ppermute(far, DOM, far_pairs)

    gathered = call(first_gather_kernel, by_slot, [in_vmem] * 3)(states, inv_mass, slots)
    far, near, partial = call(first_kernel, (tall, edge, wide), [in_vmem] * 11)(
        states, gathered, fetched, *fixed
    )
    previous = states
    for step in range(DEGREE - 1):
        gathered = call(gather_kernel, by_slot, [in_vmem] * 4)(
            partial, fetched, inv_mass, slots
        )
        far, near, partial, previous = call(
            functools.partial(next_kernel, step == DEGREE - 2),
            (tall, edge, wide, block),
            [in_vmem] * 16,
        )(previous, partial, gathered, message, fetched, *swapped(near, far), *fixed, chosen_t)

    def from_chip(x, s):
        return lax.ppermute(x, "chip", [(i, i ^ s) for i in range(chips)])

    got_near, got_far = swapped(near, far)
    second = from_chip(partial, 2)
    beside = from_chip(partial, 1)
    relayed, own = call(relay_kernel, (wide, block), [in_vmem] * 4, aliases={1: 0, 2: 1})(
        beside, second, previous, got_near
    )
    blocks = [partial, beside, relayed, from_chip(relayed, 1)]

    def from_sibling(x):
        return lax.ppermute(x, "core", [(0, 1), (1, 0)])

    late = call(late_kernel, shape_of(rows, LATE * shared_count), [in_vmem] * 3)(
        partial, got_near, got_far
    )
    filtered, left = call(finish_kernel, (block, wide), [in_vmem] * 3)(partial, late, chosen_t)
    gram = call(
        functools.partial(gram_kernel, owned * n_dom),
        shape_of(2 * rows, chips * rows),
        [in_vmem] * (4 + chips),
        [pltpu.VMEM((chips * rows, nodes), bf16)] * 2,
    )(left, from_sibling(own), from_sibling(late), chosen_t, *blocks)

    n_z = lax.axis_size("z")
    n_across = lax.axis_size(("x", "half"))
    each = rows // n_z
    pieces = lax.all_to_all(
        gram.reshape(2 * n_z, each, chips * rows), ("core", "z"), 0, 0, tiled=True
    )
    mine = call(functools.partial(fold_kernel, rows), shape_of(n_across, each, n_band * rows), [in_vmem])(pieces)
    spread = lax.all_to_all(mine, ("x", "half"), 0, 0, tiled=True)
    mine = jnp.sum(spread, axis=0)
    margin = lax.all_to_all(
        jnp.broadcast_to(mine[None], (n_z, *mine.shape)), "z", 0, 0, tiled=True
    )
    return filtered, margin.reshape(rows, n_band * rows)


def solution(mesh):
    fine = Mesh(mesh.devices.reshape(4, 2, 4, 2, 8), BAND + DOM)
    return jax.shard_map(
        per_device,
        mesh=fine,
        in_specs=(P(BAND, DOM), P(), P(DOM), P(DOM), P(DOM), P(DOM, None), P(DOM)),
        out_specs=(P(BAND, DOM), P(BAND, None)),
        check_vma=False,
    )
```

```python
import functools

import jax
import jax.numpy as jnp
from jax import lax
from jax.experimental import pallas as pl
from jax.experimental.pallas import tpu as pltpu
from jax.sharding import Mesh, PartitionSpec as P

DEGREE = 3
CENTER = 1.0
HALF_WIDTH = 4.0
LIMIT = 28 * 1024 * 1024
LATE = 8
BAND = ("chip", "core")
DOM = ("x", "half", "z")

f32 = jnp.float32
bf16 = jnp.bfloat16


def rounded_up(count, to):
    return -(-count // to) * to


def parts(x, count):
    out = []
    for i in range(count):
        piece = x.astype(bf16)
        out.append(piece)
        if i + 1 < count:
            x = x - piece.astype(f32)
    return out


def dot(a, b):
    return jnp.dot(a, b, preferred_element_type=f32)


def dot_t(a, b):
    return lax.dot_general(a, b, (((1,), (1,)), ((), ())), preferred_element_type=f32)


def one_hot(row, count):
    at = lax.broadcasted_iota(jnp.int16, (count, row.shape[1]), 0)
    return jnp.where(at == row.astype(jnp.int16), jnp.array(1, bf16), jnp.array(0, bf16))


def one_hot_rows(column, count):
    at = lax.broadcasted_iota(jnp.int16, (column.shape[0], count), 1)
    return jnp.where(at == column.astype(jnp.int16), jnp.array(1, bf16), jnp.array(0, bf16))


def picked(x, chosen):
    rows = x.shape[0]
    got = dot(jnp.concatenate(parts(x, 3), axis=0), chosen)
    return got[:rows] + got[rows : 2 * rows] + got[2 * rows :]


def placed(x, chosen_t):
    return picked(x, chosen_t)


def start_kernel(
    states, inv_mass, shared, potential, cells, stiff,
    message, states_in, inv_in, shared_in, pot_in, cells_in, stiff_in, done,
):
    moves = [
        pltpu.make_async_copy(source, target, done.at[i])
        for i, (source, target) in enumerate(
            [
                (shared, shared_in), (inv_mass, inv_in), (states, states_in),
                (potential, pot_in), (cells, cells_in), (stiff, stiff_in),
            ]
        )
    ]
    for move in moves:
        move.start()
    for move in moves[:4]:
        move.wait()
    owned = states_in.shape[1]
    both = jnp.concatenate(
        [
            states_in[...],
            jnp.broadcast_to(inv_in[...], (4, owned)),
            jnp.broadcast_to(pot_in[...], (4, owned)),
        ],
        axis=0,
    )
    message[...] = picked(both, one_hot(shared_in[...], owned))
    for move in moves[4:]:
        move.wait()


def prepare_kernel(
    cells, stiff, shared, scale,
    slots, late_slots, high, low, chosen_t, scale_row, cells_pad, stiff_pad,
):
    n_cells, npc = cells.shape
    pad = stiff_pad.shape[0]
    nodes = slots.shape[1]
    shared_count, owned = chosen_t.shape
    cells_pad[...] = jnp.full(cells_pad.shape, -1, jnp.int32)
    cells_pad[:n_cells, :npc] = cells[...]
    cells_pad[8:9, :shared_count] = shared[...]
    columns = jnp.transpose(cells_pad[...])
    shared_column = columns[:shared_count, 8:9]
    ghosts = lax.broadcasted_iota(jnp.int16, (shared_count, pad), 0) + jnp.int16(owned)
    shareds = jnp.broadcast_to(shared_column.astype(jnp.int16), (shared_count, pad))
    for c in range(n_cells):
        at = slice(c * pad, (c + 1) * pad)
        slots[at, :] = one_hot_rows(columns[:, c : c + 1], nodes)
        row = cells_pad[c : c + 1, :].astype(jnp.int16)
        for i, names in enumerate((shareds, ghosts)):
            late_slots[i * shared_count : (i + 1) * shared_count, at] = jnp.where(
                names == row, jnp.array(1, bf16), jnp.array(0, bf16)
            )
        scale_row[:, at] = jnp.full((1, pad), scale[c], f32)
    stiff_pad[...] = jnp.zeros(stiff_pad.shape, f32)
    stiff_pad[:npc, :npc] = stiff[...]
    high[...], low[...] = parts(stiff_pad[...], 2)
    chosen_t[...] = one_hot_rows(shared_column, owned)


def twice(x, apply):
    rows = x.shape[0]
    got = apply(jnp.concatenate(parts(x, 2), axis=0))
    return got[:rows] + got[rows:]


def first_gather_kernel(states, inv_mass, slots, gathered):
    owned = states.shape[1]
    values = states[...] * inv_mass[...]
    gathered[...] = twice(values, lambda x: dot_t(x, slots[:, :owned]))


def gather_kernel(part, fetched, inv_mass, slots, gathered):
    rows = part.shape[0]
    owned = inv_mass.shape[1]
    values = jnp.concatenate(
        [part[:, :owned] * inv_mass[...], part[:, owned:] * fetched[rows : rows + 1, :]],
        axis=1,
    )
    gathered[...] = twice(values, lambda x: dot_t(x, slots[...]))


def cell_products(gathered, late, late_slots, scale, high, low):
    rows = gathered.shape[0]
    pad = high.shape[0]
    n_cells = gathered.shape[1] // pad
    values = gathered[...] + twice(late, lambda x: dot(x, late_slots))
    v_high, v_low = parts(values, 2)
    stacked = jnp.concatenate(
        [v_high[:, c * pad : (c + 1) * pad] for c in range(n_cells)]
        + [v_low[:, c * pad : (c + 1) * pad] for c in range(n_cells)],
        axis=0,
    )
    half = n_cells * rows
    by_high = dot(stacked, high[...])
    product = by_high[:half] + by_high[half:] + dot(stacked[:half], low[...])
    product = jnp.concatenate(
        [product[c * rows : (c + 1) * rows] for c in range(n_cells)], axis=1
    ) * scale[...]
    return jnp.concatenate(parts(product, 2), axis=0)


def folded(got):
    rows = got.shape[0] // 2
    return got[:rows] + got[rows:]


def is_even():
    return lax.axis_index("z") % 2 == 0


def send_both(up, down, near, far):
    even = is_even()
    near[...] = jnp.where(even, up, down)
    far[...] = jnp.zeros(far.shape, f32)
    far[: down.shape[0], :] = jnp.where(even, down, up)


def got_both(near, far):
    rows = near.shape[0]
    even = is_even()
    up = jnp.where(even, far[:rows, :], near[...])
    down = jnp.where(even, near[...], far[:rows, :])
    return up, down


def first_edge_kernel(
    gathered, message, fetched, scale, late_slots, high, low, far, near, products, down_out
):
    rows, count = down_out.shape
    ghost_inv = fetched[rows : rows + 1, :]
    shared_inv = message[rows : rows + 1, :]
    shared_pot = message[rows + 4 : rows + 5, :]
    late = fetched[:rows, :] * ghost_inv
    product = cell_products(gathered, late, late_slots[count:, :], scale, high, low)
    products[...] = product
    summed = folded(dot_t(product, late_slots[...]))
    up = ghost_inv * summed[:, count:] * (1.0 / HALF_WIDTH)
    down = (
        shared_inv * summed[:, :count] + (shared_pot - CENTER) * message[:rows, :]
    ) * (1.0 / HALF_WIDTH)
    down_out[...] = down
    send_both(up, down, near, far)


def first_body_kernel(products, states, fetched, inv_mass, potential, slots, partial):
    rows, owned = states.shape
    summed = folded(dot(products[...], slots[...]))
    partial[:, :owned] = (
        inv_mass[...] * summed[:, :owned] + (potential[...] - CENTER) * states[...]
    ) * (1.0 / HALF_WIDTH)
    partial[:, owned:] = fetched[rows : rows + 1, :] * summed[:, owned:] * (1.0 / HALF_WIDTH)


def next_edges(
    gathered, message, fetched, got_near, got_far, down_before, shared_before, scale,
    late_slots, high, low, far, near,
):
    rows, count = near.shape
    got_up, got_down = got_both(got_near, got_far)
    ghost_inv = fetched[rows : rows + 1, :]
    shared_inv = message[rows : rows + 1, :]
    shared_pot = message[rows + 4 : rows + 5, :]
    late = jnp.concatenate([got_up * shared_inv, got_down * ghost_inv], axis=1)
    product = cell_products(gathered, late, late_slots[...], scale, high, low)
    summed = folded(dot_t(product, late_slots[...]))
    shared_now = down_before[...] + got_up
    up = ghost_inv * summed[:, count:] * (2.0 / HALF_WIDTH)
    down = (shared_inv * summed[:, :count] + (shared_pot - CENTER) * shared_now) * (
        2.0 / HALF_WIDTH
    ) - shared_before[:rows, :]
    send_both(up, down, near, far)
    return product, down, shared_now


def next_edge_kernel(*refs):
    products, down_out, shared_out = refs[-3:]
    products[...], down_out[...], shared_out[...] = next_edges(*refs[:-3])


def next_body(
    products, previous, part, fetched, got_near, got_far, inv_mass, potential, slots,
    chosen_t, partial,
):
    rows, owned = previous.shape
    got_up, _ = got_both(got_near, got_far)
    summed = folded(dot(products, slots[...]))
    current = part[:, :owned] + placed(got_up, chosen_t[...])
    here = (inv_mass[...] * summed[:, :owned] + (potential[...] - CENTER) * current) * (
        2.0 / HALF_WIDTH
    ) - previous[...]
    partial[:, :owned] = here
    partial[:, owned:] = fetched[rows : rows + 1, :] * summed[:, owned:] * (2.0 / HALF_WIDTH)
    return here, current


def next_body_kernel(products, *refs):
    _, refs[-1][...] = next_body(products[...], *refs[:-1])


def last_kernel(
    gathered, message, fetched, got_near, got_far, down_before, shared_before, scale,
    late_slots, high, low, previous, part, inv_mass, potential, slots, chosen_t,
    far, near, partial, again,
):
    products, _, _ = next_edges(
        gathered, message, fetched, got_near, got_far, down_before, shared_before, scale,
        late_slots, high, low, far, near,
    )
    again[...], _ = next_body(
        products, previous, part, fetched, got_near, got_far, inv_mass, potential, slots,
        chosen_t, partial,
    )


def complete(part, late, chosen_t):
    count, owned = chosen_t.shape
    own = part[:, :owned] + placed(late[:, :count], chosen_t[...])
    return own, late[:, count : 2 * count]


def next_kernel(
    last, previous, part, gathered, message, fetched, got_near, got_far, inv_mass, potential, scale,
    slots, late_slots, high, low, chosen, chosen_t, far, near, partial, again,
):
    rows, owned = previous.shape
    got_up, got_down = got_both(got_near, got_far)
    ghost_inv = fetched[rows : rows + 1, :]
    shared_inv = message[rows : rows + 1, :]
    late = jnp.concatenate([got_up * shared_inv, got_down * ghost_inv], axis=1)
    summed = apply_cells(gathered, late, late_slots[...], scale, slots, high, low)
    current = part[:, :owned] + placed(got_up, chosen_t[...])
    up = ghost_inv * summed[:, owned:] * (2.0 / HALF_WIDTH)
    here = (inv_mass[...] * summed[:, :owned] + (potential[...] - CENTER) * current) * (
        2.0 / HALF_WIDTH
    ) - previous[...]
    partial[:, :owned] = here
    partial[:, owned:] = up
    again[...] = here if last else current
    send_both(up, picked(here, chosen[...]), near, far)


def relay_kernel(beside, block, own, near, block_out, own_out):
    del beside, near
    block_out[:8, :128] = block[:8, :128]
    own_out[:8, :128] = own[:8, :128]


def late_kernel(part, got_near, got_far, late):
    up, down = got_both(got_near, got_far)
    count = up.shape[1]
    late[:, :count] = up
    late[:, count : 2 * count] = part[:, part.shape[1] - count :] + down
    late[:, 2 * count :] = jnp.zeros((up.shape[0], late.shape[1] - 2 * count), f32)


def finish_kernel(part, late, chosen_t, filtered, left):
    owned = filtered.shape[1]
    current, ghost = complete(part, late, chosen_t)
    filtered[...] = current
    left[:, :owned] = current
    left[:, owned:] = ghost


def gram_kernel(total_nodes, left, sibling, late, chosen_t, *rest):
    blocks, (out, g_high, g_low) = rest[:-3], rest[-3:]
    chips = len(blocks)
    rows = left.shape[0]
    chip = lax.axis_index("chip")
    core = lax.axis_index("core")
    for s in range(chips):
        at = pl.ds(pl.multiple_of((chip ^ s) * rows, rows), rows)
        g_high[at, :], g_low[at, :] = parts(blocks[s][...], 2)
    theirs = jnp.concatenate(complete(sibling, late, chosen_t), axis=1)
    high, low = parts(jnp.concatenate([left[...], theirs], axis=0), 2)
    by_high = dot_t(jnp.concatenate([high, low], axis=0), g_high[...])
    whole = by_high[: 2 * rows] + by_high[2 * rows :] + dot_t(high, g_low[...])
    whole = whole * (1.0 / total_nodes)
    out[pl.ds(pl.multiple_of(core * rows, rows), rows), :] = whole[:rows]
    out[pl.ds(pl.multiple_of((1 - core) * rows, rows), rows), :] = whole[rows:]


def fold_kernel(rows, pieces, out):
    count = pieces.shape[0] // 2
    copies = out.shape[0]
    sums = []
    for core in range(2):
        total = pieces[core * count]
        for i in range(1, count):
            total = total + pieces[core * count + i]
        sums.append(total)
    chips = pieces.shape[2] // rows
    ordered = jnp.concatenate(
        [sums[core][:, i * rows : (i + 1) * rows] for i in range(chips) for core in range(2)],
        axis=1,
    )
    for i in range(copies):
        out[i] = ordered


def per_device(
    states_in, stiffness, cell_scale, potential, inv_mass_sqrt, cell_nodes, shared_nodes
):
    rows, owned = states_in.shape
    shared_count = shared_nodes.shape[0]
    n_cells, npc = cell_nodes.shape
    nodes = owned + shared_count
    pad = rounded_up(npc, 128)
    n_dom = lax.axis_size(DOM)
    n_band = lax.axis_size(BAND)
    chips = lax.axis_size("chip")
    backward = [(i, (i - 1) % n_dom) for i in range(n_dom)]
    near_pairs = [(i, i ^ 1) for i in range(n_dom)]
    far_pairs = [(i, (((i + 1) ^ 1) - 1) % n_dom) for i in range(n_dom)]

    in_vmem = pl.BlockSpec(memory_space=pltpu.VMEM)
    in_smem = pl.BlockSpec(memory_space=pltpu.SMEM)
    in_hbm = pl.BlockSpec(memory_space=pltpu.HBM)
    params = pltpu.CompilerParams(vmem_limit_bytes=LIMIT)

    def shape_of(*sizes, dtype=f32):
        return jax.ShapeDtypeStruct(sizes, dtype)

    block = shape_of(rows, owned)
    wide = shape_of(rows, nodes)
    edge = shape_of(rows, shared_count)
    tall = shape_of(rows + 8, shared_count)

    def call(kernel, out_shape, specs, scratch_shapes=(), aliases={}):
        return pl.pallas_call(
            kernel,
            out_shape=out_shape,
            in_specs=specs,
            out_specs=jax.tree.map(lambda _: in_vmem, out_shape),
            scratch_shapes=scratch_shapes,
            input_output_aliases=aliases,
            compiler_params=params,
        )

    message, states, inv_mass, shared, pot, cells, stiff = call(
        start_kernel,
        (
            tall, block, shape_of(1, owned), shape_of(1, shared_count, dtype=jnp.int32),
            shape_of(1, owned), shape_of(n_cells, npc, dtype=jnp.int32), shape_of(npc, npc),
        ),
        [in_hbm] * 6,
        [pltpu.SemaphoreType.DMA((6,))],
    )(
        *(
            pltpu.with_memory_space_constraint(x, pltpu.HBM)
            for x in (
                states_in, inv_mass_sqrt.reshape(1, owned),
                shared_nodes.reshape(1, shared_count), potential.reshape(1, owned),
                cell_nodes, stiffness,
            )
        )
    )
    fetched = lax.ppermute(message, DOM, backward)
    slot_count = n_cells * pad
    slots, late_slots, high, low, chosen_t, scale = call(
        prepare_kernel,
        (
            shape_of(slot_count, nodes, dtype=bf16),
            shape_of(2 * shared_count, slot_count, dtype=bf16),
            shape_of(pad, pad, dtype=bf16),
            shape_of(pad, pad, dtype=bf16),
            shape_of(shared_count, owned, dtype=bf16),
            shape_of(1, slot_count),
        ),
        [in_vmem] * 3 + [in_smem],
        [pltpu.VMEM((16, pad), jnp.int32), pltpu.VMEM((pad, pad), f32)],
    )(cells, stiff, shared, cell_scale)
    fixed = (scale, late_slots, high, low)
    by_slot = shape_of(rows, slot_count)

    def swapped(near, far):
        return lax.ppermute(near, DOM, near_pairs), lax.ppermute(far, DOM, far_pairs)

    gathered = call(first_gather_kernel, by_slot, [in_vmem] * 3)(states, inv_mass, slots)
    stacked = shape_of(2 * rows, slot_count, dtype=bf16)
    far, near, products, down = call(
        first_edge_kernel, (tall, edge, stacked, edge), [in_vmem] * 7
    )(gathered, message, fetched, *fixed)
    partial = call(first_body_kernel, wide, [in_vmem] * 6)(
        products, states, fetched, inv_mass, pot, slots
    )
    previous, shared_now = states, message
    for step in range(DEGREE - 1):
        gathered = call(gather_kernel, by_slot, [in_vmem] * 4)(
            partial, fetched, inv_mass, slots
        )
        got = swapped(near, far)
        edges = (gathered, message, fetched, *got, down, shared_now, *fixed)
        body = (inv_mass, pot, slots, chosen_t)
        if step == DEGREE - 2:
            far, near, partial, own = call(
                last_kernel, (tall, edge, wide, block), [in_vmem] * 17
            )(*edges, previous, partial, *body)
        else:
            far, near, products, down, shared_now = call(
                next_edge_kernel, (tall, edge, stacked, edge, edge), [in_vmem] * 11
            )(*edges)
            partial, previous = call(next_body_kernel, (wide, block), [in_vmem] * 10)(
                products, previous, partial, fetched, *got, *body
            )

    def from_chip(x, s):
        return lax.ppermute(x, "chip", [(i, i ^ s) for i in range(chips)])

    got_near, got_far = swapped(near, far)
    second = from_chip(partial, 2)
    beside = from_chip(partial, 1)
    relayed, own = call(relay_kernel, (wide, block), [in_vmem] * 4, aliases={1: 0, 2: 1})(
        beside, second, own, got_near
    )
    blocks = [partial, beside, relayed, from_chip(relayed, 1)]

    def from_sibling(x):
        return lax.ppermute(x, "core", [(0, 1), (1, 0)])

    late = call(late_kernel, shape_of(rows, LATE * shared_count), [in_vmem] * 3)(
        partial, got_near, got_far
    )
    filtered, left = call(finish_kernel, (block, wide), [in_vmem] * 3)(partial, late, chosen_t)
    gram = call(
        functools.partial(gram_kernel, owned * n_dom),
        shape_of(2 * rows, chips * rows),
        [in_vmem] * (4 + chips),
        [pltpu.VMEM((chips * rows, nodes), bf16)] * 2,
    )(left, from_sibling(own), from_sibling(late), chosen_t, *blocks)

    n_z = lax.axis_size("z")
    n_across = lax.axis_size(("x", "half"))
    each = rows // n_z
    pieces = lax.all_to_all(
        gram.reshape(2 * n_z, each, chips * rows), ("core", "z"), 0, 0, tiled=True
    )
    mine = call(functools.partial(fold_kernel, rows), shape_of(n_across, each, n_band * rows), [in_vmem])(pieces)
    spread = lax.all_to_all(mine, ("x", "half"), 0, 0, tiled=True)
    mine = jnp.sum(spread, axis=0)
    margin = lax.all_to_all(
        jnp.broadcast_to(mine[None], (n_z, *mine.shape)), "z", 0, 0, tiled=True
    )
    return filtered, margin.reshape(rows, n_band * rows)


def solution(mesh):
    fine = Mesh(mesh.devices.reshape(4, 2, 4, 2, 8), BAND + DOM)
    return jax.shard_map(
        per_device,
        mesh=fine,
        in_specs=(P(BAND, DOM), P(), P(DOM), P(DOM), P(DOM), P(DOM, None), P(DOM)),
        out_specs=(P(BAND, DOM), P(BAND, None)),
        check_vma=False,
    )
```

```python
import functools

import jax
import jax.numpy as jnp
from jax import lax
from jax.experimental import pallas as pl
from jax.experimental.pallas import tpu as pltpu
from jax.sharding import Mesh, PartitionSpec as P

DEGREE = 3
CENTER = 1.0
HALF_WIDTH = 4.0
LIMIT = 28 * 1024 * 1024
LATE = 8
EXTRA = 4
BAND = ("chip", "core")
DOM = ("x", "half", "z")

f32 = jnp.float32
bf16 = jnp.bfloat16


def rounded_up(count, to):
    return -(-count // to) * to


def parts(x, count):
    out = []
    for i in range(count):
        piece = x.astype(bf16)
        out.append(piece)
        if i + 1 < count:
            x = x - piece.astype(f32)
    return out


def dot(a, b):
    return jnp.dot(a, b, preferred_element_type=f32)


def dot_t(a, b):
    return lax.dot_general(a, b, (((1,), (1,)), ((), ())), preferred_element_type=f32)


def one_hot(row, count):
    at = lax.broadcasted_iota(jnp.int16, (count, row.shape[1]), 0)
    return jnp.where(at == row.astype(jnp.int16), jnp.array(1, bf16), jnp.array(0, bf16))


def one_hot_rows(column, count):
    at = lax.broadcasted_iota(jnp.int16, (column.shape[0], count), 1)
    return jnp.where(at == column.astype(jnp.int16), jnp.array(1, bf16), jnp.array(0, bf16))


def picked(x, chosen):
    rows = x.shape[0]
    got = dot(jnp.concatenate(parts(x, 3), axis=0), chosen)
    return got[:rows] + got[rows : 2 * rows] + got[2 * rows :]


def placed(x, chosen_t):
    return picked(x, chosen_t)


def start_kernel(
    states, inv_mass, shared, potential, cells, stiff,
    message, states_in, inv_in, shared_in, pot_in, cells_in, stiff_in, done,
):
    moves = [
        pltpu.make_async_copy(source, target, done.at[i])
        for i, (source, target) in enumerate(
            [
                (shared, shared_in), (inv_mass, inv_in), (states, states_in),
                (potential, pot_in), (cells, cells_in), (stiff, stiff_in),
            ]
        )
    ]
    for move in moves:
        move.start()
    for move in moves[:4]:
        move.wait()
    owned = states_in.shape[1]
    both = jnp.concatenate(
        [
            states_in[...],
            jnp.broadcast_to(inv_in[...], (4, owned)),
            jnp.broadcast_to(pot_in[...], (4, owned)),
        ],
        axis=0,
    )
    message[...] = picked(both, one_hot(shared_in[...], owned))
    for move in moves[4:]:
        move.wait()


def prepare_kernel(
    cells, stiff, shared, scale,
    slots, late_slots, high, low, chosen_t, scale_row, cells_pad, stiff_pad,
):
    n_cells, npc = cells.shape
    pad = stiff_pad.shape[0]
    nodes = slots.shape[1]
    shared_count, owned = chosen_t.shape
    cells_pad[...] = jnp.full(cells_pad.shape, -1, jnp.int32)
    cells_pad[:n_cells, :npc] = cells[...]
    cells_pad[8:9, :shared_count] = shared[...]
    columns = jnp.transpose(cells_pad[...])
    shared_column = columns[:shared_count, 8:9]
    ghosts = lax.broadcasted_iota(jnp.int16, (shared_count, pad), 0) + jnp.int16(owned)
    shareds = jnp.broadcast_to(shared_column.astype(jnp.int16), (shared_count, pad))
    for c in range(n_cells):
        at = slice(c * pad, (c + 1) * pad)
        slots[at, :] = one_hot_rows(columns[:, c : c + 1], nodes)
        row = cells_pad[c : c + 1, :].astype(jnp.int16)
        for i, names in enumerate((shareds, ghosts)):
            late_slots[i * shared_count : (i + 1) * shared_count, at] = jnp.where(
                names == row, jnp.array(1, bf16), jnp.array(0, bf16)
            )
        scale_row[:, at] = jnp.full((1, pad), scale[c], f32)
    stiff_pad[...] = jnp.zeros(stiff_pad.shape, f32)
    stiff_pad[:npc, :npc] = stiff[...]
    high[...], low[...] = parts(stiff_pad[...], 2)
    chosen_t[...] = one_hot_rows(shared_column, owned)


def twice(x, apply):
    rows = x.shape[0]
    got = apply(jnp.concatenate(parts(x, 2), axis=0))
    return got[:rows] + got[rows:]


def first_gather_kernel(states, inv_mass, slots, gathered):
    owned = states.shape[1]
    values = states[...] * inv_mass[...]
    gathered[...] = twice(values, lambda x: dot_t(x, slots[:, :owned]))


def gather_kernel(part, fetched, inv_mass, slots, gathered):
    rows = part.shape[0]
    owned = inv_mass.shape[1]
    values = jnp.concatenate(
        [part[:, :owned] * inv_mass[...], part[:, owned:] * fetched[rows : rows + 1, :]],
        axis=1,
    )
    gathered[...] = twice(values, lambda x: dot_t(x, slots[...]))


def cell_products(gathered, late, late_slots, scale, high, low):
    rows = gathered.shape[0]
    pad = high.shape[0]
    n_cells = gathered.shape[1] // pad
    values = gathered[...] + twice(late, lambda x: dot(x, late_slots))
    v_high, v_low = parts(values, 2)
    stacked = jnp.concatenate(
        [v_high[:, c * pad : (c + 1) * pad] for c in range(n_cells)]
        + [v_low[:, c * pad : (c + 1) * pad] for c in range(n_cells)],
        axis=0,
    )
    half = n_cells * rows
    by_high = dot(stacked, high[...])
    product = by_high[:half] + by_high[half:] + dot(stacked[:half], low[...])
    product = jnp.concatenate(
        [product[c * rows : (c + 1) * rows] for c in range(n_cells)], axis=1
    ) * scale[...]
    return jnp.concatenate(parts(product, 2), axis=0)


def folded(got):
    rows = got.shape[0] // 2
    return got[:rows] + got[rows:]


def is_even():
    return lax.axis_index("z") % 2 == 0


def send_both(up, down, near, far):
    even = is_even()
    near[...] = jnp.where(even, up, down)
    far[...] = jnp.zeros(far.shape, f32)
    far[: down.shape[0], :] = jnp.where(even, down, up)


def got_both(near, far):
    rows = near.shape[0]
    even = is_even()
    up = jnp.where(even, far[:rows, :], near[...])
    down = jnp.where(even, near[...], far[:rows, :])
    return up, down


def first_edge_kernel(
    gathered, message, fetched, scale, late_slots, high, low, far, near, products, down_out
):
    rows, count = down_out.shape
    ghost_inv = fetched[rows : rows + 1, :]
    shared_inv = message[rows : rows + 1, :]
    shared_pot = message[rows + 4 : rows + 5, :]
    late = fetched[:rows, :] * ghost_inv
    product = cell_products(gathered, late, late_slots[count:, :], scale, high, low)
    products[...] = product
    summed = folded(dot_t(product, late_slots[...]))
    up = ghost_inv * summed[:, count:] * (1.0 / HALF_WIDTH)
    down = (
        shared_inv * summed[:, :count] + (shared_pot - CENTER) * message[:rows, :]
    ) * (1.0 / HALF_WIDTH)
    down_out[...] = down
    send_both(up, down, near, far)


def first_body_kernel(products, states, fetched, inv_mass, potential, slots, partial):
    rows, owned = states.shape
    summed = folded(dot(products[...], slots[...]))
    partial[:, :owned] = (
        inv_mass[...] * summed[:, :owned] + (potential[...] - CENTER) * states[...]
    ) * (1.0 / HALF_WIDTH)
    partial[:, owned:] = fetched[rows : rows + 1, :] * summed[:, owned:] * (1.0 / HALF_WIDTH)


def next_edges(
    gathered, message, fetched, got_near, got_far, down_before, shared_before, scale,
    late_slots, high, low, far, near,
):
    rows, count = near.shape
    got_up, got_down = got_both(got_near, got_far)
    ghost_inv = fetched[rows : rows + 1, :]
    shared_inv = message[rows : rows + 1, :]
    shared_pot = message[rows + 4 : rows + 5, :]
    late = jnp.concatenate([got_up * shared_inv, got_down * ghost_inv], axis=1)
    product = cell_products(gathered, late, late_slots[...], scale, high, low)
    summed = folded(dot_t(product, late_slots[...]))
    shared_now = down_before[...] + got_up
    up = ghost_inv * summed[:, count:] * (2.0 / HALF_WIDTH)
    down = (shared_inv * summed[:, :count] + (shared_pot - CENTER) * shared_now) * (
        2.0 / HALF_WIDTH
    ) - shared_before[:rows, :]
    send_both(up, down, near, far)
    return product, down, shared_now


def next_edge_kernel(*refs):
    products, down_out, shared_out = refs[-3:]
    products[...], down_out[...], shared_out[...] = next_edges(*refs[:-3])


def next_body(
    products, previous, part, fetched, got_near, got_far, inv_mass, potential, slots,
    chosen_t, partial,
):
    rows, owned = previous.shape
    got_up, _ = got_both(got_near, got_far)
    summed = folded(dot(products, slots[...]))
    current = part[:, :owned] + placed(got_up, chosen_t[...])
    here = (inv_mass[...] * summed[:, :owned] + (potential[...] - CENTER) * current) * (
        2.0 / HALF_WIDTH
    ) - previous[...]
    partial[:, :owned] = here
    partial[:, owned:] = fetched[rows : rows + 1, :] * summed[:, owned:] * (2.0 / HALF_WIDTH)
    return here, current


def next_body_kernel(products, *refs):
    _, refs[-1][...] = next_body(products[...], *refs[:-1])


def last_kernel(
    gathered, message, fetched, got_near, got_far, down_before, shared_before, scale,
    late_slots, high, low, previous, part, inv_mass, potential, slots, chosen_t,
    far, near, partial, again,
):
    products, _, _ = next_edges(
        gathered, message, fetched, got_near, got_far, down_before, shared_before, scale,
        late_slots, high, low, far, near,
    )
    here, _ = next_body(
        products, previous, part, fetched, got_near, got_far, inv_mass, potential, slots,
        chosen_t, partial,
    )
    rows, owned = here.shape
    for i in range(rows // 8):
        again[:, i * owned : (i + 1) * owned] = here[8 * i : 8 * (i + 1), :]
    again[:, rows // 8 * owned :] = jnp.zeros((8, again.shape[1] - rows // 8 * owned), f32)


def complete(part, late, chosen_t):
    count, owned = chosen_t.shape
    own = part[:, :owned] + placed(late[:, :count], chosen_t[...])
    return own, late[:, count : 2 * count]


def next_kernel(
    last, previous, part, gathered, message, fetched, got_near, got_far, inv_mass, potential, scale,
    slots, late_slots, high, low, chosen, chosen_t, far, near, partial, again,
):
    rows, owned = previous.shape
    got_up, got_down = got_both(got_near, got_far)
    ghost_inv = fetched[rows : rows + 1, :]
    shared_inv = message[rows : rows + 1, :]
    late = jnp.concatenate([got_up * shared_inv, got_down * ghost_inv], axis=1)
    summed = apply_cells(gathered, late, late_slots[...], scale, slots, high, low)
    current = part[:, :owned] + placed(got_up, chosen_t[...])
    up = ghost_inv * summed[:, owned:] * (2.0 / HALF_WIDTH)
    here = (inv_mass[...] * summed[:, :owned] + (potential[...] - CENTER) * current) * (
        2.0 / HALF_WIDTH
    ) - previous[...]
    partial[:, :owned] = here
    partial[:, owned:] = up
    again[...] = here if last else current
    send_both(up, picked(here, chosen[...]), near, far)


def relay_kernel(beside, block, own, near, block_out, own_out):
    del beside, near
    block_out[:8, :128] = block[:8, :128]
    own_out[:8, :128] = own[:8, :128]


def late_kernel(part, got_near, got_far, late):
    up, down = got_both(got_near, got_far)
    count = up.shape[1]
    late[:, :count] = up
    late[:, count : 2 * count] = part[:, part.shape[1] - count :] + down
    late[:, 2 * count :] = jnp.zeros((up.shape[0], late.shape[1] - 2 * count), f32)


def finish_kernel(part, late, chosen_t, filtered, left):
    owned = filtered.shape[1]
    current, ghost = complete(part, late, chosen_t)
    filtered[...] = current
    left[:, :owned] = current
    left[:, owned:] = ghost


def gram_kernel(total_nodes, left, sibling, late, chosen_t, *rest):
    blocks, (out, g_high, g_low) = rest[:-3], rest[-3:]
    chips = len(blocks)
    rows = left.shape[0]
    chip = lax.axis_index("chip")
    core = lax.axis_index("core")
    for s in range(chips):
        at = pl.ds(pl.multiple_of((chip ^ s) * rows, rows), rows)
        g_high[at, :], g_low[at, :] = parts(blocks[s][...], 2)
    owned = chosen_t.shape[1]
    rows_of = [sibling[:, i * owned : (i + 1) * owned] for i in range(rows // 8)]
    theirs = complete(jnp.concatenate(rows_of, axis=0), late, chosen_t)
    theirs = jnp.concatenate(theirs, axis=1)
    high, low = parts(jnp.concatenate([left[...], theirs], axis=0), 2)
    by_high = dot_t(jnp.concatenate([high, low], axis=0), g_high[...])
    whole = by_high[: 2 * rows] + by_high[2 * rows :] + dot_t(high, g_low[...])
    whole = whole * (1.0 / total_nodes)
    out[pl.ds(pl.multiple_of(core * rows, rows), rows), :] = whole[:rows]
    out[pl.ds(pl.multiple_of((1 - core) * rows, rows), rows), :] = whole[rows:]


def fold_kernel(rows, pieces, out):
    count = pieces.shape[0] // 2
    copies = out.shape[0]
    sums = []
    for core in range(2):
        total = pieces[core * count]
        for i in range(1, count):
            total = total + pieces[core * count + i]
        sums.append(total)
    chips = pieces.shape[2] // rows
    ordered = jnp.concatenate(
        [sums[core][:, i * rows : (i + 1) * rows] for i in range(chips) for core in range(2)],
        axis=1,
    )
    for i in range(copies):
        out[i] = ordered


def per_device(
    states_in, stiffness, cell_scale, potential, inv_mass_sqrt, cell_nodes, shared_nodes
):
    rows, owned = states_in.shape
    shared_count = shared_nodes.shape[0]
    n_cells, npc = cell_nodes.shape
    nodes = owned + shared_count
    pad = rounded_up(npc, 128)
    n_dom = lax.axis_size(DOM)
    n_band = lax.axis_size(BAND)
    chips = lax.axis_size("chip")
    backward = [(i, (i - 1) % n_dom) for i in range(n_dom)]
    near_pairs = [(i, i ^ 1) for i in range(n_dom)]
    far_pairs = [(i, (((i + 1) ^ 1) - 1) % n_dom) for i in range(n_dom)]

    in_vmem = pl.BlockSpec(memory_space=pltpu.VMEM)
    in_smem = pl.BlockSpec(memory_space=pltpu.SMEM)
    in_hbm = pl.BlockSpec(memory_space=pltpu.HBM)
    params = pltpu.CompilerParams(vmem_limit_bytes=LIMIT)

    def shape_of(*sizes, dtype=f32):
        return jax.ShapeDtypeStruct(sizes, dtype)

    block = shape_of(rows, owned)
    wide = shape_of(rows, nodes)
    edge = shape_of(rows, shared_count)
    tall = shape_of(rows + 8, shared_count)
    beside_rows = shape_of(8, rows // 8 * owned + EXTRA * 128)

    def call(kernel, out_shape, specs, scratch_shapes=(), aliases={}):
        return pl.pallas_call(
            kernel,
            out_shape=out_shape,
            in_specs=specs,
            out_specs=jax.tree.map(lambda _: in_vmem, out_shape),
            scratch_shapes=scratch_shapes,
            input_output_aliases=aliases,
            compiler_params=params,
        )

    message, states, inv_mass, shared, pot, cells, stiff = call(
        start_kernel,
        (
            tall, block, shape_of(1, owned), shape_of(1, shared_count, dtype=jnp.int32),
            shape_of(1, owned), shape_of(n_cells, npc, dtype=jnp.int32), shape_of(npc, npc),
        ),
        [in_hbm] * 6,
        [pltpu.SemaphoreType.DMA((6,))],
    )(
        *(
            pltpu.with_memory_space_constraint(x, pltpu.HBM)
            for x in (
                states_in, inv_mass_sqrt.reshape(1, owned),
                shared_nodes.reshape(1, shared_count), potential.reshape(1, owned),
                cell_nodes, stiffness,
            )
        )
    )
    fetched = lax.ppermute(message, DOM, backward)
    slot_count = n_cells * pad
    slots, late_slots, high, low, chosen_t, scale = call(
        prepare_kernel,
        (
            shape_of(slot_count, nodes, dtype=bf16),
            shape_of(2 * shared_count, slot_count, dtype=bf16),
            shape_of(pad, pad, dtype=bf16),
            shape_of(pad, pad, dtype=bf16),
            shape_of(shared_count, owned, dtype=bf16),
            shape_of(1, slot_count),
        ),
        [in_vmem] * 3 + [in_smem],
        [pltpu.VMEM((16, pad), jnp.int32), pltpu.VMEM((pad, pad), f32)],
    )(cells, stiff, shared, cell_scale)
    fixed = (scale, late_slots, high, low)
    by_slot = shape_of(rows, slot_count)

    def swapped(near, far):
        return lax.ppermute(near, DOM, near_pairs), lax.ppermute(far, DOM, far_pairs)

    gathered = call(first_gather_kernel, by_slot, [in_vmem] * 3)(states, inv_mass, slots)
    stacked = shape_of(2 * rows, slot_count, dtype=bf16)
    far, near, products, down = call(
        first_edge_kernel, (tall, edge, stacked, edge), [in_vmem] * 7
    )(gathered, message, fetched, *fixed)
    partial = call(first_body_kernel, wide, [in_vmem] * 6)(
        products, states, fetched, inv_mass, pot, slots
    )
    previous, shared_now = states, message
    for step in range(DEGREE - 1):
        gathered = call(gather_kernel, by_slot, [in_vmem] * 4)(
            partial, fetched, inv_mass, slots
        )
        got = swapped(near, far)
        edges = (gathered, message, fetched, *got, down, shared_now, *fixed)
        body = (inv_mass, pot, slots, chosen_t)
        if step == DEGREE - 2:
            far, near, partial, own = call(
                last_kernel, (tall, edge, wide, beside_rows), [in_vmem] * 17
            )(*edges, previous, partial, *body)
        else:
            far, near, products, down, shared_now = call(
                next_edge_kernel, (tall, edge, stacked, edge, edge), [in_vmem] * 11
            )(*edges)
            partial, previous = call(next_body_kernel, (wide, block), [in_vmem] * 10)(
                products, previous, partial, fetched, *got, *body
            )

    def from_chip(x, s):
        return lax.ppermute(x, "chip", [(i, i ^ s) for i in range(chips)])

    got_near, got_far = swapped(near, far)
    second = from_chip(partial, 2)
    beside = from_chip(partial, 1)
    relayed, own = call(relay_kernel, (wide, beside_rows), [in_vmem] * 4, aliases={1: 0, 2: 1})(
        beside, second, own, got_near
    )
    blocks = [partial, beside, relayed, from_chip(relayed, 1)]

    def from_sibling(x):
        return lax.ppermute(x, "core", [(0, 1), (1, 0)])

    late = call(late_kernel, shape_of(rows, LATE * shared_count), [in_vmem] * 3)(
        partial, got_near, got_far
    )
    filtered, left = call(finish_kernel, (block, wide), [in_vmem] * 3)(partial, late, chosen_t)
    gram = call(
        functools.partial(gram_kernel, owned * n_dom),
        shape_of(2 * rows, chips * rows),
        [in_vmem] * (4 + chips),
        [pltpu.VMEM((chips * rows, nodes), bf16)] * 2,
    )(left, from_sibling(own), from_sibling(late), chosen_t, *blocks)

    n_z = lax.axis_size("z")
    n_across = lax.axis_size(("x", "half"))
    each = rows // n_z
    pieces = lax.all_to_all(
        gram.reshape(2 * n_z, each, chips * rows), ("core", "z"), 0, 0, tiled=True
    )
    mine = call(functools.partial(fold_kernel, rows), shape_of(n_across, each, n_band * rows), [in_vmem])(pieces)
    spread = lax.all_to_all(mine, ("x", "half"), 0, 0, tiled=True)
    mine = jnp.sum(spread, axis=0)
    margin = lax.all_to_all(
        jnp.broadcast_to(mine[None], (n_z, *mine.shape)), "z", 0, 0, tiled=True
    )
    return filtered, margin.reshape(rows, n_band * rows)


def solution(mesh):
    fine = Mesh(mesh.devices.reshape(4, 2, 4, 2, 8), BAND + DOM)
    return jax.shard_map(
        per_device,
        mesh=fine,
        in_specs=(P(BAND, DOM), P(), P(DOM), P(DOM), P(DOM), P(DOM, None), P(DOM)),
        out_specs=(P(BAND, DOM), P(BAND, None)),
        check_vma=False,
    )
```

```python
import functools

import jax
import jax.numpy as jnp
from jax import lax
from jax.experimental import pallas as pl
from jax.experimental.pallas import tpu as pltpu
from jax.sharding import Mesh, PartitionSpec as P

DEGREE = 3
CENTER = 1.0
HALF_WIDTH = 4.0
LIMIT = 28 * 1024 * 1024
LATE = 8
EXTRA = 4
BAND = ("chip", "core")
DOM = ("x", "half", "z")

f32 = jnp.float32
bf16 = jnp.bfloat16


def rounded_up(count, to):
    return -(-count // to) * to


def parts(x, count):
    out = []
    for i in range(count):
        piece = x.astype(bf16)
        out.append(piece)
        if i + 1 < count:
            x = x - piece.astype(f32)
    return out


def dot(a, b):
    return jnp.dot(a, b, preferred_element_type=f32)


def dot_t(a, b):
    return lax.dot_general(a, b, (((1,), (1,)), ((), ())), preferred_element_type=f32)


def one_hot(row, count):
    at = lax.broadcasted_iota(jnp.int16, (count, row.shape[1]), 0)
    return jnp.where(at == row.astype(jnp.int16), jnp.array(1, bf16), jnp.array(0, bf16))


def one_hot_rows(column, count):
    at = lax.broadcasted_iota(jnp.int16, (column.shape[0], count), 1)
    return jnp.where(at == column.astype(jnp.int16), jnp.array(1, bf16), jnp.array(0, bf16))


def picked(x, chosen):
    rows = x.shape[0]
    got = dot(jnp.concatenate(parts(x, 3), axis=0), chosen)
    return got[:rows] + got[rows : 2 * rows] + got[2 * rows :]


def placed(x, chosen_t):
    return picked(x, chosen_t)


def start_kernel(
    states, inv_mass, shared, potential, cells, stiff,
    message, states_in, inv_in, shared_in, pot_in, cells_in, stiff_in, done,
):
    moves = [
        pltpu.make_async_copy(source, target, done.at[i])
        for i, (source, target) in enumerate(
            [
                (shared, shared_in), (inv_mass, inv_in), (states, states_in),
                (potential, pot_in), (cells, cells_in), (stiff, stiff_in),
            ]
        )
    ]
    for move in moves:
        move.start()
    for move in moves[:4]:
        move.wait()
    owned = states_in.shape[1]
    both = jnp.concatenate(
        [
            states_in[...],
            jnp.broadcast_to(inv_in[...], (4, owned)),
            jnp.broadcast_to(pot_in[...], (4, owned)),
        ],
        axis=0,
    )
    message[...] = picked(both, one_hot(shared_in[...], owned))
    for move in moves[4:]:
        move.wait()


def prepare_kernel(
    cells, stiff, shared, scale,
    slots, late_slots, late_columns, high, low, chosen_t, scale_row, cells_pad, stiff_pad,
):
    n_cells, npc = cells.shape
    pad = stiff_pad.shape[0]
    nodes = slots.shape[1]
    shared_count, owned = chosen_t.shape
    cells_pad[...] = jnp.full(cells_pad.shape, -1, jnp.int32)
    cells_pad[:n_cells, :npc] = cells[...]
    cells_pad[8:9, :shared_count] = shared[...]
    columns = jnp.transpose(cells_pad[...])
    shared_column = columns[:shared_count, 8:9]
    ghosts = lax.broadcasted_iota(jnp.int16, (shared_count, pad), 0) + jnp.int16(owned)
    shareds = jnp.broadcast_to(shared_column.astype(jnp.int16), (shared_count, pad))
    for c in range(n_cells):
        at = slice(c * pad, (c + 1) * pad)
        slots[at, :] = one_hot_rows(columns[:, c : c + 1], nodes)
        late_columns[at, :shared_count] = jnp.where(
            columns[:, c : c + 1].astype(jnp.int16) == shared[...].astype(jnp.int16),
            jnp.array(1, bf16),
            jnp.array(0, bf16),
        )
        late_columns[at, shared_count:] = slots[at, owned:]
        row = cells_pad[c : c + 1, :].astype(jnp.int16)
        for i, names in enumerate((shareds, ghosts)):
            late_slots[i * shared_count : (i + 1) * shared_count, at] = jnp.where(
                names == row, jnp.array(1, bf16), jnp.array(0, bf16)
            )
        scale_row[:, at] = jnp.full((1, pad), scale[c], f32)
    stiff_pad[...] = jnp.zeros(stiff_pad.shape, f32)
    stiff_pad[:npc, :npc] = stiff[...]
    high[...], low[...] = parts(stiff_pad[...], 2)
    chosen_t[...] = one_hot_rows(shared_column, owned)


def twice(x, apply):
    rows = x.shape[0]
    got = apply(jnp.concatenate(parts(x, 2), axis=0))
    return got[:rows] + got[rows:]


def first_gather_kernel(states, inv_mass, slots, gathered):
    owned = states.shape[1]
    values = states[...] * inv_mass[...]
    gathered[...] = twice(values, lambda x: dot_t(x, slots[:, :owned]))


def gather_kernel(part, fetched, inv_mass, slots, gathered):
    rows = part.shape[0]
    owned = inv_mass.shape[1]
    values = jnp.concatenate(
        [part[:, :owned] * inv_mass[...], part[:, owned:] * fetched[rows : rows + 1, :]],
        axis=1,
    )
    gathered[...] = twice(values, lambda x: dot_t(x, slots[...]))


def cell_products(gathered, late, late_slots, scale, high, low):
    rows = gathered.shape[0]
    pad = high.shape[0]
    n_cells = gathered.shape[1] // pad
    values = gathered[...] + twice(late, lambda x: dot(x, late_slots))
    v_high, v_low = parts(values, 2)
    stacked = jnp.concatenate(
        [v_high[:, c * pad : (c + 1) * pad] for c in range(n_cells)]
        + [v_low[:, c * pad : (c + 1) * pad] for c in range(n_cells)],
        axis=0,
    )
    half = n_cells * rows
    by_high = dot(stacked, high[...])
    product = by_high[:half] + by_high[half:] + dot(stacked[:half], low[...])
    product = jnp.concatenate(
        [product[c * rows : (c + 1) * rows] for c in range(n_cells)], axis=1
    ) * scale[...]
    return jnp.concatenate(parts(product, 2), axis=0)


def folded(got):
    rows = got.shape[0] // 2
    return got[:rows] + got[rows:]


def is_even():
    return lax.axis_index("z") % 2 == 0


def send_both(up, down, near, far):
    even = is_even()
    near[...] = jnp.where(even, up, down)
    far[...] = jnp.zeros(far.shape, f32)
    far[: down.shape[0], :] = jnp.where(even, down, up)


def got_both(near, far):
    rows = near.shape[0]
    even = is_even()
    up = jnp.where(even, far[:rows, :], near[...])
    down = jnp.where(even, near[...], far[:rows, :])
    return up, down


def first_edge_kernel(
    gathered, message, fetched, scale, late_slots, late_columns, high, low, far, near, products, down_out
):
    rows, count = down_out.shape
    ghost_inv = fetched[rows : rows + 1, :]
    shared_inv = message[rows : rows + 1, :]
    shared_pot = message[rows + 4 : rows + 5, :]
    late = fetched[:rows, :] * ghost_inv
    product = cell_products(gathered, late, late_slots[count:, :], scale, high, low)
    products[...] = product
    summed = folded(dot(product, late_columns[...]))
    up = ghost_inv * summed[:, count:] * (1.0 / HALF_WIDTH)
    down = (
        shared_inv * summed[:, :count] + (shared_pot - CENTER) * message[:rows, :]
    ) * (1.0 / HALF_WIDTH)
    down_out[...] = down
    send_both(up, down, near, far)


def first_body_kernel(products, states, fetched, inv_mass, potential, slots, partial):
    rows, owned = states.shape
    summed = folded(dot(products[...], slots[...]))
    partial[:, :owned] = (
        inv_mass[...] * summed[:, :owned] + (potential[...] - CENTER) * states[...]
    ) * (1.0 / HALF_WIDTH)
    partial[:, owned:] = fetched[rows : rows + 1, :] * summed[:, owned:] * (1.0 / HALF_WIDTH)


def next_edges(
    gathered, message, fetched, got_near, got_far, down_before, shared_before, scale,
    late_slots, late_columns, high, low, far, near,
):
    rows, count = near.shape
    got_up, got_down = got_both(got_near, got_far)
    ghost_inv = fetched[rows : rows + 1, :]
    shared_inv = message[rows : rows + 1, :]
    shared_pot = message[rows + 4 : rows + 5, :]
    late = jnp.concatenate([got_up * shared_inv, got_down * ghost_inv], axis=1)
    product = cell_products(gathered, late, late_slots[...], scale, high, low)
    summed = folded(dot(product, late_columns[...]))
    shared_now = down_before[...] + got_up
    up = ghost_inv * summed[:, count:] * (2.0 / HALF_WIDTH)
    down = (shared_inv * summed[:, :count] + (shared_pot - CENTER) * shared_now) * (
        2.0 / HALF_WIDTH
    ) - shared_before[:rows, :]
    send_both(up, down, near, far)
    return product, down, shared_now


def next_edge_kernel(*refs):
    products, down_out, shared_out = refs[-3:]
    products[...], down_out[...], shared_out[...] = next_edges(*refs[:-3])


def next_body(
    products, previous, part, fetched, got_near, got_far, inv_mass, potential, slots,
    chosen_t, partial,
):
    rows, owned = previous.shape
    got_up, _ = got_both(got_near, got_far)
    summed = folded(dot(products, slots[...]))
    current = part[:, :owned] + placed(got_up, chosen_t[...])
    here = (inv_mass[...] * summed[:, :owned] + (potential[...] - CENTER) * current) * (
        2.0 / HALF_WIDTH
    ) - previous[...]
    partial[:, :owned] = here
    partial[:, owned:] = fetched[rows : rows + 1, :] * summed[:, owned:] * (2.0 / HALF_WIDTH)
    return here, current


def next_body_kernel(products, *refs):
    _, refs[-1][...] = next_body(products[...], *refs[:-1])


def last_kernel(
    gathered, message, fetched, got_near, got_far, down_before, shared_before, scale,
    late_slots, late_columns, high, low, previous, part, inv_mass, potential, slots, chosen_t,
    far, near, partial, again,
):
    products, _, _ = next_edges(
        gathered, message, fetched, got_near, got_far, down_before, shared_before, scale,
        late_slots, late_columns, high, low, far, near,
    )
    here, _ = next_body(
        products, previous, part, fetched, got_near, got_far, inv_mass, potential, slots,
        chosen_t, partial,
    )
    rows, owned = here.shape
    for i in range(rows // 8):
        again[:, i * owned : (i + 1) * owned] = here[8 * i : 8 * (i + 1), :]
    again[:, rows // 8 * owned :] = jnp.zeros((8, again.shape[1] - rows // 8 * owned), f32)


def complete(part, late, chosen_t):
    count, owned = chosen_t.shape
    own = part[:, :owned] + placed(late[:, :count], chosen_t[...])
    return own, late[:, count : 2 * count]


def relay_kernel(beside, block, own, near, block_out, own_out):
    del beside, near
    block_out[:8, :128] = block[:8, :128]
    own_out[:8, :128] = own[:8, :128]


def late_kernel(part, got_near, got_far, late):
    up, down = got_both(got_near, got_far)
    count = up.shape[1]
    late[:, :count] = up
    late[:, count : 2 * count] = part[:, part.shape[1] - count :] + down
    late[:, 2 * count :] = jnp.zeros((up.shape[0], late.shape[1] - 2 * count), f32)


def finish_kernel(part, late, chosen_t, filtered, left):
    owned = filtered.shape[1]
    current, ghost = complete(part, late, chosen_t)
    filtered[...] = current
    left[:, :owned] = current
    left[:, owned:] = ghost


def gram_kernel(total_nodes, left, sibling, late, chosen_t, *rest):
    blocks, (out, g_high, g_low) = rest[:-3], rest[-3:]
    chips = len(blocks)
    rows = left.shape[0]
    chip = lax.axis_index("chip")
    core = lax.axis_index("core")
    for s in range(chips):
        at = pl.ds(pl.multiple_of((chip ^ s) * rows, rows), rows)
        g_high[at, :], g_low[at, :] = parts(blocks[s][...], 2)
    owned = chosen_t.shape[1]
    rows_of = [sibling[:, i * owned : (i + 1) * owned] for i in range(rows // 8)]
    theirs = complete(jnp.concatenate(rows_of, axis=0), late, chosen_t)
    theirs = jnp.concatenate(theirs, axis=1)
    high, low = parts(jnp.concatenate([left[...], theirs], axis=0), 2)
    by_high = dot_t(jnp.concatenate([high, low], axis=0), g_high[...])
    whole = by_high[: 2 * rows] + by_high[2 * rows :] + dot_t(high, g_low[...])
    whole = whole * (1.0 / total_nodes)
    out[pl.ds(pl.multiple_of(core * rows, rows), rows), :] = whole[:rows]
    out[pl.ds(pl.multiple_of((1 - core) * rows, rows), rows), :] = whole[rows:]


def fold_kernel(rows, pieces, out):
    count = pieces.shape[0] // 2
    copies = out.shape[0]
    sums = []
    for core in range(2):
        total = pieces[core * count]
        for i in range(1, count):
            total = total + pieces[core * count + i]
        sums.append(total)
    chips = pieces.shape[2] // rows
    ordered = jnp.concatenate(
        [sums[core][:, i * rows : (i + 1) * rows] for i in range(chips) for core in range(2)],
        axis=1,
    )
    for i in range(copies):
        out[i] = ordered


def per_device(
    states_in, stiffness, cell_scale, potential, inv_mass_sqrt, cell_nodes, shared_nodes
):
    rows, owned = states_in.shape
    shared_count = shared_nodes.shape[0]
    n_cells, npc = cell_nodes.shape
    nodes = owned + shared_count
    pad = rounded_up(npc, 128)
    n_dom = lax.axis_size(DOM)
    n_band = lax.axis_size(BAND)
    chips = lax.axis_size("chip")
    backward = [(i, (i - 1) % n_dom) for i in range(n_dom)]
    near_pairs = [(i, i ^ 1) for i in range(n_dom)]
    far_pairs = [(i, (((i + 1) ^ 1) - 1) % n_dom) for i in range(n_dom)]

    in_vmem = pl.BlockSpec(memory_space=pltpu.VMEM)
    in_smem = pl.BlockSpec(memory_space=pltpu.SMEM)
    in_hbm = pl.BlockSpec(memory_space=pltpu.HBM)
    params = pltpu.CompilerParams(vmem_limit_bytes=LIMIT)

    def shape_of(*sizes, dtype=f32):
        return jax.ShapeDtypeStruct(sizes, dtype)

    block = shape_of(rows, owned)
    wide = shape_of(rows, nodes)
    edge = shape_of(rows, shared_count)
    tall = shape_of(rows + 8, shared_count)
    beside_rows = shape_of(8, rows // 8 * owned + EXTRA * 128)

    def call(kernel, out_shape, specs, scratch_shapes=(), aliases={}):
        return pl.pallas_call(
            kernel,
            out_shape=out_shape,
            in_specs=specs,
            out_specs=jax.tree.map(lambda _: in_vmem, out_shape),
            scratch_shapes=scratch_shapes,
            input_output_aliases=aliases,
            compiler_params=params,
        )

    message, states, inv_mass, shared, pot, cells, stiff = call(
        start_kernel,
        (
            tall, block, shape_of(1, owned), shape_of(1, shared_count, dtype=jnp.int32),
            shape_of(1, owned), shape_of(n_cells, npc, dtype=jnp.int32), shape_of(npc, npc),
        ),
        [in_hbm] * 6,
        [pltpu.SemaphoreType.DMA((6,))],
    )(
        *(
            pltpu.with_memory_space_constraint(x, pltpu.HBM)
            for x in (
                states_in, inv_mass_sqrt.reshape(1, owned),
                shared_nodes.reshape(1, shared_count), potential.reshape(1, owned),
                cell_nodes, stiffness,
            )
        )
    )
    fetched = lax.ppermute(message, DOM, backward)
    slot_count = n_cells * pad
    slots, late_slots, late_columns, high, low, chosen_t, scale = call(
        prepare_kernel,
        (
            shape_of(slot_count, nodes, dtype=bf16),
            shape_of(2 * shared_count, slot_count, dtype=bf16),
            shape_of(slot_count, 2 * shared_count, dtype=bf16),
            shape_of(pad, pad, dtype=bf16),
            shape_of(pad, pad, dtype=bf16),
            shape_of(shared_count, owned, dtype=bf16),
            shape_of(1, slot_count),
        ),
        [in_vmem] * 3 + [in_smem],
        [pltpu.VMEM((16, pad), jnp.int32), pltpu.VMEM((pad, pad), f32)],
    )(cells, stiff, shared, cell_scale)
    fixed = (scale, late_slots, late_columns, high, low)
    by_slot = shape_of(rows, slot_count)

    def swapped(near, far):
        return lax.ppermute(near, DOM, near_pairs), lax.ppermute(far, DOM, far_pairs)

    gathered = call(first_gather_kernel, by_slot, [in_vmem] * 3)(states, inv_mass, slots)
    stacked = shape_of(2 * rows, slot_count, dtype=bf16)
    far, near, products, down = call(
        first_edge_kernel, (tall, edge, stacked, edge), [in_vmem] * 8
    )(gathered, message, fetched, *fixed)
    partial = call(first_body_kernel, wide, [in_vmem] * 6)(
        products, states, fetched, inv_mass, pot, slots
    )
    previous, shared_now = states, message
    for step in range(DEGREE - 1):
        gathered = call(gather_kernel, by_slot, [in_vmem] * 4)(
            partial, fetched, inv_mass, slots
        )
        got = swapped(near, far)
        edges = (gathered, message, fetched, *got, down, shared_now, *fixed)
        body = (inv_mass, pot, slots, chosen_t)
        if step == DEGREE - 2:
            far, near, partial, own = call(
                last_kernel, (tall, edge, wide, beside_rows), [in_vmem] * 18
            )(*edges, previous, partial, *body)
        else:
            far, near, products, down, shared_now = call(
                next_edge_kernel, (tall, edge, stacked, edge, edge), [in_vmem] * 12
            )(*edges)
            partial, previous = call(next_body_kernel, (wide, block), [in_vmem] * 10)(
                products, previous, partial, fetched, *got, *body
            )

    def from_chip(x, s):
        return lax.ppermute(x, "chip", [(i, i ^ s) for i in range(chips)])

    got_near, got_far = swapped(near, far)
    second = from_chip(partial, 2)
    beside = from_chip(partial, 1)
    relayed, own = call(relay_kernel, (wide, beside_rows), [in_vmem] * 4, aliases={1: 0, 2: 1})(
        beside, second, own, got_near
    )
    blocks = [partial, beside, relayed, from_chip(relayed, 1)]

    def from_sibling(x):
        return lax.ppermute(x, "core", [(0, 1), (1, 0)])

    late = call(late_kernel, shape_of(rows, LATE * shared_count), [in_vmem] * 3)(
        partial, got_near, got_far
    )
    filtered, left = call(finish_kernel, (block, wide), [in_vmem] * 3)(partial, late, chosen_t)
    gram = call(
        functools.partial(gram_kernel, owned * n_dom),
        shape_of(2 * rows, chips * rows),
        [in_vmem] * (4 + chips),
        [pltpu.VMEM((chips * rows, nodes), bf16)] * 2,
    )(left, from_sibling(own), from_sibling(late), chosen_t, *blocks)

    n_z = lax.axis_size("z")
    n_across = lax.axis_size(("x", "half"))
    each = rows // n_z
    pieces = lax.all_to_all(
        gram.reshape(2 * n_z, each, chips * rows), ("core", "z"), 0, 0, tiled=True
    )
    mine = call(functools.partial(fold_kernel, rows), shape_of(n_across, each, n_band * rows), [in_vmem])(pieces)
    spread = lax.all_to_all(mine, ("x", "half"), 0, 0, tiled=True)
    mine = jnp.sum(spread, axis=0)
    margin = lax.all_to_all(
        jnp.broadcast_to(mine[None], (n_z, *mine.shape)), "z", 0, 0, tiled=True
    )
    return filtered, margin.reshape(rows, n_band * rows)


def solution(mesh):
    fine = Mesh(mesh.devices.reshape(4, 2, 4, 2, 8), BAND + DOM)
    return jax.shard_map(
        per_device,
        mesh=fine,
        in_specs=(P(BAND, DOM), P(), P(DOM), P(DOM), P(DOM), P(DOM, None), P(DOM)),
        out_specs=(P(BAND, DOM), P(BAND, None)),
        check_vma=False,
    )
```

```python
import functools

import jax
import jax.numpy as jnp
from jax import lax
from jax.experimental import pallas as pl
from jax.experimental.pallas import tpu as pltpu
from jax.sharding import Mesh, PartitionSpec as P

DEGREE = 3
CENTER = 1.0
HALF_WIDTH = 4.0
LIMIT = 28 * 1024 * 1024
LATE = 8
EXTRA = 4
BAND = ("chip", "core")
DOM = ("x", "half", "z")

f32 = jnp.float32
bf16 = jnp.bfloat16


def rounded_up(count, to):
    return -(-count // to) * to


def parts(x, count):
    out = []
    for i in range(count):
        piece = x.astype(bf16)
        out.append(piece)
        if i + 1 < count:
            x = x - piece.astype(f32)
    return out


def dot(a, b):
    return jnp.dot(a, b, preferred_element_type=f32)


def dot_t(a, b):
    return lax.dot_general(a, b, (((1,), (1,)), ((), ())), preferred_element_type=f32)


def one_hot(row, count):
    at = lax.broadcasted_iota(jnp.int16, (count, row.shape[1]), 0)
    return jnp.where(at == row.astype(jnp.int16), jnp.array(1, bf16), jnp.array(0, bf16))


def one_hot_rows(column, count):
    at = lax.broadcasted_iota(jnp.int16, (column.shape[0], count), 1)
    return jnp.where(at == column.astype(jnp.int16), jnp.array(1, bf16), jnp.array(0, bf16))


def picked(x, chosen):
    rows = x.shape[0]
    got = dot(jnp.concatenate(parts(x, 3), axis=0), chosen)
    return got[:rows] + got[rows : 2 * rows] + got[2 * rows :]


def placed(x, chosen_t):
    return picked(x, chosen_t)


def start_kernel(
    states, inv_mass, shared, potential, cells, stiff,
    message, states_in, inv_in, shared_in, pot_in, cells_in, stiff_in, done,
):
    moves = [
        pltpu.make_async_copy(source, target, done.at[i])
        for i, (source, target) in enumerate(
            [
                (shared, shared_in), (inv_mass, inv_in), (states, states_in),
                (potential, pot_in), (cells, cells_in), (stiff, stiff_in),
            ]
        )
    ]
    for move in moves:
        move.start()
    for move in moves[:4]:
        move.wait()
    owned = states_in.shape[1]
    both = jnp.concatenate(
        [
            states_in[...],
            jnp.broadcast_to(inv_in[...], (4, owned)),
            jnp.broadcast_to(pot_in[...], (4, owned)),
        ],
        axis=0,
    )
    message[...] = picked(both, one_hot(shared_in[...], owned))
    for move in moves[4:]:
        move.wait()


def prepare_kernel(
    cells, stiff, shared, scale,
    slots, late_slots, late_columns, high, low, chosen_t, scale_row, cells_pad, stiff_pad,
):
    n_cells, npc = cells.shape
    pad = stiff_pad.shape[0]
    nodes = slots.shape[1]
    shared_count, owned = chosen_t.shape
    cells_pad[...] = jnp.full(cells_pad.shape, -1, jnp.int32)
    cells_pad[:n_cells, :npc] = cells[...]
    cells_pad[8:9, :shared_count] = shared[...]
    columns = jnp.transpose(cells_pad[...])
    shared_column = columns[:shared_count, 8:9]
    ghosts = lax.broadcasted_iota(jnp.int16, (shared_count, pad), 0) + jnp.int16(owned)
    shareds = jnp.broadcast_to(shared_column.astype(jnp.int16), (shared_count, pad))
    for c in range(n_cells):
        at = slice(c * pad, (c + 1) * pad)
        slots[at, :] = one_hot_rows(columns[:, c : c + 1], nodes)
        late_columns[at, :shared_count] = jnp.where(
            columns[:, c : c + 1].astype(jnp.int16) == shared[...].astype(jnp.int16),
            jnp.array(1, bf16),
            jnp.array(0, bf16),
        )
        late_columns[at, shared_count:] = slots[at, owned:]
        row = cells_pad[c : c + 1, :].astype(jnp.int16)
        for i, names in enumerate((shareds, ghosts)):
            late_slots[i * shared_count : (i + 1) * shared_count, at] = jnp.where(
                names == row, jnp.array(1, bf16), jnp.array(0, bf16)
            )
        scale_row[:, at] = jnp.full((1, pad), scale[c], f32)
    stiff_pad[...] = jnp.zeros(stiff_pad.shape, f32)
    stiff_pad[:npc, :npc] = stiff[...]
    high[...], low[...] = parts(stiff_pad[...], 2)
    chosen_t[...] = one_hot_rows(shared_column, owned)


def twice(x, apply):
    rows = x.shape[0]
    got = apply(jnp.concatenate(parts(x, 2), axis=0))
    return got[:rows] + got[rows:]


def first_gather_kernel(states, inv_mass, slots, gathered):
    owned = states.shape[1]
    values = states[...] * inv_mass[...]
    gathered[...] = twice(values, lambda x: dot_t(x, slots[:, :owned]))


def gather_kernel(part, fetched, inv_mass, slots, gathered):
    rows = part.shape[0]
    owned = inv_mass.shape[1]
    values = jnp.concatenate(
        [part[:, :owned] * inv_mass[...], part[:, owned:] * fetched[rows : rows + 1, :]],
        axis=1,
    )
    gathered[...] = twice(values, lambda x: dot_t(x, slots[...]))


def cell_products(gathered, late, late_slots, scale, high, low):
    rows = gathered.shape[0]
    pad = high.shape[0]
    n_cells = gathered.shape[1] // pad
    values = gathered[...] + twice(late, lambda x: dot(x, late_slots))
    v_high, v_low = parts(values, 2)
    stacked = jnp.concatenate(
        [v_high[:, c * pad : (c + 1) * pad] for c in range(n_cells)]
        + [v_low[:, c * pad : (c + 1) * pad] for c in range(n_cells)],
        axis=0,
    )
    half = n_cells * rows
    by_high = dot(stacked, high[...])
    product = by_high[:half] + by_high[half:] + dot(stacked[:half], low[...])
    product = jnp.concatenate(
        [product[c * rows : (c + 1) * rows] for c in range(n_cells)], axis=1
    ) * scale[...]
    return jnp.concatenate(parts(product, 2), axis=0)


def folded(got):
    rows = got.shape[0] // 2
    return got[:rows] + got[rows:]


def is_even():
    return lax.axis_index("z") % 2 == 0


def send_both(up, down, near, far):
    even = is_even()
    near[...] = jnp.where(even, up, down)
    far[...] = jnp.zeros(far.shape, f32)
    far[: down.shape[0], :] = jnp.where(even, down, up)


def got_both(near, far):
    rows = near.shape[0]
    even = is_even()
    up = jnp.where(even, far[:rows, :], near[...])
    down = jnp.where(even, near[...], far[:rows, :])
    return up, down


def first_edge_kernel(
    gathered, message, fetched, scale, late_slots, late_columns, high, low, far, near, products, down_out
):
    rows, count = down_out.shape
    ghost_inv = fetched[rows : rows + 1, :]
    shared_inv = message[rows : rows + 1, :]
    shared_pot = message[rows + 4 : rows + 5, :]
    late = fetched[:rows, :] * ghost_inv
    product = cell_products(gathered, late, late_slots[count:, :], scale, high, low)
    products[...] = product
    summed = folded(dot(product, late_columns[...]))
    up = ghost_inv * summed[:, count:] * (1.0 / HALF_WIDTH)
    down = (
        shared_inv * summed[:, :count] + (shared_pot - CENTER) * message[:rows, :]
    ) * (1.0 / HALF_WIDTH)
    down_out[...] = down
    send_both(up, down, near, far)


def first_body_kernel(products, states, fetched, inv_mass, potential, slots, partial):
    rows, owned = states.shape
    summed = folded(dot(products[...], slots[...]))
    partial[:, :owned] = (
        inv_mass[...] * summed[:, :owned] + (potential[...] - CENTER) * states[...]
    ) * (1.0 / HALF_WIDTH)
    partial[:, owned:] = fetched[rows : rows + 1, :] * summed[:, owned:] * (1.0 / HALF_WIDTH)


def next_edges(
    gathered, message, fetched, got_near, got_far, down_before, shared_before, scale,
    late_slots, late_columns, high, low, far, near,
):
    rows, count = near.shape
    got_up, got_down = got_both(got_near, got_far)
    ghost_inv = fetched[rows : rows + 1, :]
    shared_inv = message[rows : rows + 1, :]
    shared_pot = message[rows + 4 : rows + 5, :]
    late = jnp.concatenate([got_up * shared_inv, got_down * ghost_inv], axis=1)
    product = cell_products(gathered, late, late_slots[...], scale, high, low)
    summed = folded(dot(product, late_columns[...]))
    shared_now = down_before[...] + got_up
    up = ghost_inv * summed[:, count:] * (2.0 / HALF_WIDTH)
    down = (shared_inv * summed[:, :count] + (shared_pot - CENTER) * shared_now) * (
        2.0 / HALF_WIDTH
    ) - shared_before[:rows, :]
    send_both(up, down, near, far)
    return product, down, shared_now


def next_edge_kernel(*refs):
    products, down_out, shared_out = refs[-3:]
    products[...], down_out[...], shared_out[...] = next_edges(*refs[:-3])


def next_body(
    products, previous, part, fetched, got_near, got_far, inv_mass, potential, slots,
    chosen_t, partial,
):
    rows, owned = previous.shape
    got_up, _ = got_both(got_near, got_far)
    summed = folded(dot(products, slots[...]))
    current = part[:, :owned] + placed(got_up, chosen_t[...])
    here = (inv_mass[...] * summed[:, :owned] + (potential[...] - CENTER) * current) * (
        2.0 / HALF_WIDTH
    ) - previous[...]
    partial[:, :owned] = here
    partial[:, owned:] = fetched[rows : rows + 1, :] * summed[:, owned:] * (2.0 / HALF_WIDTH)
    return here, current


def next_body_kernel(products, *refs):
    _, refs[-1][...] = next_body(products[...], *refs[:-1])


def last_kernel(
    gathered, message, fetched, got_near, got_far, down_before, shared_before, scale,
    late_slots, late_columns, high, low, previous, part, inv_mass, potential, slots, chosen_t,
    far, near, partial, again,
):
    products, _, _ = next_edges(
        gathered, message, fetched, got_near, got_far, down_before, shared_before, scale,
        late_slots, late_columns, high, low, far, near,
    )
    here, _ = next_body(
        products, previous, part, fetched, got_near, got_far, inv_mass, potential, slots,
        chosen_t, partial,
    )
    rows, owned = here.shape
    for i in range(rows // 8):
        again[:, i * owned : (i + 1) * owned] = here[8 * i : 8 * (i + 1), :]
    again[:, rows // 8 * owned :] = jnp.zeros((8, again.shape[1] - rows // 8 * owned), f32)


def complete(part, late, chosen_t):
    count, owned = chosen_t.shape
    own = part[:, :owned] + placed(late[:, :count], chosen_t[...])
    return own, late[:, count : 2 * count]


def relay_kernel(beside, block, own, block_out, own_out):
    del beside
    block_out[:8, :128] = block[:8, :128]
    own_out[:8, :128] = own[:8, :128]


def late_kernel(part, got_near, got_far, late):
    up, down = got_both(got_near, got_far)
    count = up.shape[1]
    late[:, :count] = up
    late[:, count : 2 * count] = part[:, part.shape[1] - count :] + down
    late[:, 2 * count :] = jnp.zeros((up.shape[0], late.shape[1] - 2 * count), f32)


def finish_kernel(part, late, chosen_t, filtered, left):
    owned = filtered.shape[1]
    current, ghost = complete(part, late, chosen_t)
    filtered[...] = current
    left[:, :owned] = current
    left[:, owned:] = ghost


def gram_kernel(total_nodes, left, sibling, late, chosen_t, *rest):
    blocks, (out, g_high, g_low) = rest[:-3], rest[-3:]
    chips = len(blocks)
    rows = left.shape[0]
    chip = lax.axis_index("chip")
    core = lax.axis_index("core")
    for s in range(chips):
        at = pl.ds(pl.multiple_of((chip ^ s) * rows, rows), rows)
        g_high[at, :], g_low[at, :] = parts(blocks[s][...], 2)
    owned = chosen_t.shape[1]
    rows_of = [sibling[:, i * owned : (i + 1) * owned] for i in range(rows // 8)]
    theirs = complete(jnp.concatenate(rows_of, axis=0), late, chosen_t)
    theirs = jnp.concatenate(theirs, axis=1)
    high, low = parts(jnp.concatenate([left[...], theirs], axis=0), 2)
    by_high = dot_t(jnp.concatenate([high, low], axis=0), g_high[...])
    whole = by_high[: 2 * rows] + by_high[2 * rows :] + dot_t(high, g_low[...])
    whole = whole * (1.0 / total_nodes)
    out[pl.ds(pl.multiple_of(core * rows, rows), rows), :] = whole[:rows]
    out[pl.ds(pl.multiple_of((1 - core) * rows, rows), rows), :] = whole[rows:]


def fold_kernel(rows, pieces, out):
    count = pieces.shape[0] // 2
    copies = out.shape[0]
    sums = []
    for core in range(2):
        total = pieces[core * count]
        for i in range(1, count):
            total = total + pieces[core * count + i]
        sums.append(total)
    chips = pieces.shape[2] // rows
    ordered = jnp.concatenate(
        [sums[core][:, i * rows : (i + 1) * rows] for i in range(chips) for core in range(2)],
        axis=1,
    )
    for i in range(copies):
        out[i] = ordered


def per_device(
    states_in, stiffness, cell_scale, potential, inv_mass_sqrt, cell_nodes, shared_nodes
):
    rows, owned = states_in.shape
    shared_count = shared_nodes.shape[0]
    n_cells, npc = cell_nodes.shape
    nodes = owned + shared_count
    pad = rounded_up(npc, 128)
    n_dom = lax.axis_size(DOM)
    n_band = lax.axis_size(BAND)
    chips = lax.axis_size("chip")
    backward = [(i, (i - 1) % n_dom) for i in range(n_dom)]
    near_pairs = [(i, i ^ 1) for i in range(n_dom)]
    far_pairs = [(i, (((i + 1) ^ 1) - 1) % n_dom) for i in range(n_dom)]

    in_vmem = pl.BlockSpec(memory_space=pltpu.VMEM)
    in_smem = pl.BlockSpec(memory_space=pltpu.SMEM)
    in_hbm = pl.BlockSpec(memory_space=pltpu.HBM)
    params = pltpu.CompilerParams(vmem_limit_bytes=LIMIT)

    def shape_of(*sizes, dtype=f32):
        return jax.ShapeDtypeStruct(sizes, dtype)

    block = shape_of(rows, owned)
    wide = shape_of(rows, nodes)
    edge = shape_of(rows, shared_count)
    tall = shape_of(rows + 8, shared_count)
    beside_rows = shape_of(8, rows // 8 * owned + EXTRA * 128)

    def call(kernel, out_shape, specs, scratch_shapes=(), aliases={}):
        return pl.pallas_call(
            kernel,
            out_shape=out_shape,
            in_specs=specs,
            out_specs=jax.tree.map(lambda _: in_vmem, out_shape),
            scratch_shapes=scratch_shapes,
            input_output_aliases=aliases,
            compiler_params=params,
        )

    message, states, inv_mass, shared, pot, cells, stiff = call(
        start_kernel,
        (
            tall, block, shape_of(1, owned), shape_of(1, shared_count, dtype=jnp.int32),
            shape_of(1, owned), shape_of(n_cells, npc, dtype=jnp.int32), shape_of(npc, npc),
        ),
        [in_hbm] * 6,
        [pltpu.SemaphoreType.DMA((6,))],
    )(
        *(
            pltpu.with_memory_space_constraint(x, pltpu.HBM)
            for x in (
                states_in, inv_mass_sqrt.reshape(1, owned),
                shared_nodes.reshape(1, shared_count), potential.reshape(1, owned),
                cell_nodes, stiffness,
            )
        )
    )
    fetched = lax.ppermute(message, DOM, backward)
    slot_count = n_cells * pad
    slots, late_slots, late_columns, high, low, chosen_t, scale = call(
        prepare_kernel,
        (
            shape_of(slot_count, nodes, dtype=bf16),
            shape_of(2 * shared_count, slot_count, dtype=bf16),
            shape_of(slot_count, 2 * shared_count, dtype=bf16),
            shape_of(pad, pad, dtype=bf16),
            shape_of(pad, pad, dtype=bf16),
            shape_of(shared_count, owned, dtype=bf16),
            shape_of(1, slot_count),
        ),
        [in_vmem] * 3 + [in_smem],
        [pltpu.VMEM((16, pad), jnp.int32), pltpu.VMEM((pad, pad), f32)],
    )(cells, stiff, shared, cell_scale)
    fixed = (scale, late_slots, late_columns, high, low)
    by_slot = shape_of(rows, slot_count)

    def swapped(near, far):
        return lax.ppermute(near, DOM, near_pairs), lax.ppermute(far, DOM, far_pairs)

    gathered = call(first_gather_kernel, by_slot, [in_vmem] * 3)(states, inv_mass, slots)
    stacked = shape_of(2 * rows, slot_count, dtype=bf16)
    far, near, products, down = call(
        first_edge_kernel, (tall, edge, stacked, edge), [in_vmem] * 8
    )(gathered, message, fetched, *fixed)
    partial = call(first_body_kernel, wide, [in_vmem] * 6)(
        products, states, fetched, inv_mass, pot, slots
    )
    previous, shared_now = states, message
    for step in range(DEGREE - 1):
        gathered = call(gather_kernel, by_slot, [in_vmem] * 4)(
            partial, fetched, inv_mass, slots
        )
        got = swapped(near, far)
        edges = (gathered, message, fetched, *got, down, shared_now, *fixed)
        body = (inv_mass, pot, slots, chosen_t)
        if step == DEGREE - 2:
            far, near, partial, own = call(
                last_kernel, (tall, edge, wide, beside_rows), [in_vmem] * 18
            )(*edges, previous, partial, *body)
        else:
            far, near, products, down, shared_now = call(
                next_edge_kernel, (tall, edge, stacked, edge, edge), [in_vmem] * 12
            )(*edges)
            partial, previous = call(next_body_kernel, (wide, block), [in_vmem] * 10)(
                products, previous, partial, fetched, *got, *body
            )

    def from_chip(x, s):
        return lax.ppermute(x, "chip", [(i, i ^ s) for i in range(chips)])

    got_near, got_far = swapped(near, far)
    second = from_chip(partial, 2)
    beside = from_chip(partial, 1)
    relayed, own = call(relay_kernel, (wide, beside_rows), [in_vmem] * 3, aliases={1: 0, 2: 1})(
        beside, second, own
    )
    blocks = [partial, beside, relayed, from_chip(relayed, 1)]

    def from_sibling(x):
        return lax.ppermute(x, "core", [(0, 1), (1, 0)])

    late = call(late_kernel, shape_of(rows, LATE * shared_count), [in_vmem] * 3)(
        partial, got_near, got_far
    )
    filtered, left = call(finish_kernel, (block, wide), [in_vmem] * 3)(partial, late, chosen_t)
    gram = call(
        functools.partial(gram_kernel, owned * n_dom),
        shape_of(2 * rows, chips * rows),
        [in_vmem] * (4 + chips),
        [pltpu.VMEM((chips * rows, nodes), bf16)] * 2,
    )(left, from_sibling(own), from_sibling(late), chosen_t, *blocks)

    n_z = lax.axis_size("z")
    n_across = lax.axis_size(("x", "half"))
    each = rows // n_z
    pieces = lax.all_to_all(
        gram.reshape(2 * n_z, each, chips * rows), ("core", "z"), 0, 0, tiled=True
    )
    mine = call(functools.partial(fold_kernel, rows), shape_of(n_across, each, n_band * rows), [in_vmem])(pieces)
    spread = lax.all_to_all(mine, ("x", "half"), 0, 0, tiled=True)
    mine = jnp.sum(spread, axis=0)
    margin = lax.all_to_all(
        jnp.broadcast_to(mine[None], (n_z, *mine.shape)), "z", 0, 0, tiled=True
    )
    return filtered, margin.reshape(rows, n_band * rows)


def solution(mesh):
    fine = Mesh(mesh.devices.reshape(4, 2, 4, 2, 8), BAND + DOM)
    return jax.shard_map(
        per_device,
        mesh=fine,
        in_specs=(P(BAND, DOM), P(), P(DOM), P(DOM), P(DOM), P(DOM, None), P(DOM)),
        out_specs=(P(BAND, DOM), P(BAND, None)),
        check_vma=False,
    )
```
